128 devices in a mesh: section: 2 (over core), ctx: 16 (over z, y), tp: 4 (over x).
Axes of the slice: x: 4, y: 4, z: 4, core: 2. Of those that a mesh axis runs over, the one named last changes fastest.
Arguments:
- block_input: bfloat16 [2, 8192, 512], P(None, ('ctx', 'tp')), may hold values from -6 to 6
- output_grad: bfloat16 [2, 8192, 512], P(None, ('ctx', 'tp')), may hold values from -6 to 6
- sequence_lengths: int32 [2, 4], replicated, may hold values from 1 to 7680, as said below
- norm_gain: float32 [2, 2, 512], P('section'), may hold values from 0.1 to 1.9
- norm_bias: float32 [2, 2, 512], P('section'), may hold values from -1.8 to 1.8
- attention_weight: bfloat16 [2, 3, 512, 512], P('section', None, None, 'tp'), may hold values from -0.25 to 0.25
- attention_bias: float32 [2, 3, 512], P('section', None, 'tp'), may hold values from -0.6 to 0.6
- output_weight: bfloat16 [2, 512, 512], P('section', 'tp'), may hold values from -3 to 3
- up_weight: bfloat16 [2, 512, 2048], P('section', None, 'tp'), may hold values from -0.25 to 0.25
- up_bias: float32 [2, 2048], P('section', 'tp'), may hold values from -1.8 to 1.8
- down_weight: bfloat16 [2, 2048, 512], P('section', 'tp'), may hold values from -0.125 to 0.125
- branch_bias: float32 [2, 512], P('section'), may hold values from -1.8 to 1.8
Outputs:
- section_output: bfloat16 [2, 2, 8192, 512], P('section', None, ('ctx', 'tp'))
- section_input_grad: bfloat16 [2, 2, 8192, 512], P('section', None, ('ctx', 'tp'))
- norm_gain_grad: float32 [2, 2, 512], P('section')
- norm_bias_grad: float32 [2, 2, 512], P('section')
- attention_weight_grad: float32 [2, 3, 512, 512], P('section', None, None, 'tp')
- attention_bias_grad: float32 [2, 3, 512], P('section', None, 'tp')
- output_weight_grad: float32 [2, 512, 512], P('section', 'tp')
- up_weight_grad: float32 [2, 512, 2048], P('section', None, 'tp')
- up_bias_grad: float32 [2, 2048], P('section', 'tp')
- down_weight_grad: float32 [2, 2048, 512], P('section', 'tp')
- branch_bias_grad: float32 [2, 512], P('section')
The draws below stay inside these ranges and needn't reach their ends.
Inputs may be any that keep to these rules, and one draw needn't show every extreme that they name: `sequence_lengths`: row m holds the lengths of the 4 sequences packed in order into micro-batch m; they sum to 8192. The second sequence is the longest, exactly 7680 tokens; it begins within the first 512 tokens and ends within the last 512.
All inputs are finite; a program needn't handle non-finite values.
Results may differ from the reference program's by a relative error of at most 0.028.
Values may be sent and summed in bfloat16 or wider, within the bound.
A program may use at most 128 MiB of HBM per device.

```python
import jax
import jax.numpy as jnp
from jax import lax

D = 512
HEADS = 8
HEAD_DIM = 64
FF = 2048
ROT = 16
GROUP = 512
MICRO = 2
TOKENS = 8192


def draw_sequence_lengths(key, part):
    key = jax.random.fold_in(key, 11)
    pieces = jax.random.split(key, 2)
    leading = jax.random.randint(pieces[0], (MICRO,), 1, GROUP - 1)
    trailing = GROUP - leading
    divide = jax.random.randint(pieces[1], (MICRO,), 0, 1 << 20) % (trailing - 1) + 1
    longest = jnp.full((MICRO,), TOKENS - GROUP, jnp.int32)
    return jnp.stack([leading, longest, divide, trailing - divide], axis=1).astype(jnp.int32)


def block_levels(stream_key, extent, cuts, smallest, high):
    factor_of, own = 1.0, jax.random.fold_in(stream_key, 6)
    for dim, parts in cuts:
        heights = jnp.exp(jax.random.uniform(jax.random.fold_in(own, dim), (parts,), jnp.float32, smallest / len(cuts), high / len(cuts)))
        factor_of = factor_of * jnp.repeat(heights, extent[dim] // parts).reshape([-1 if axis == dim else 1 for axis in range(len(extent))])
    return factor_of


def noise(own_key, shape, scale, reach, shards=(), held_as=jnp.bfloat16):
    drawn = jax.random.normal(own_key, shape, jnp.float32) * scale
    if len(shards) > 0:
        drawn = block_levels(own_key, shape, shards, -0.22, 0.18) * drawn
    return jnp.clip(drawn, min=-reach, max=reach).astype(held_as)


def setup_inputs(seed: int = 0) -> dict:
    key_list = jax.random.split(jax.random.key(seed), 13)
    return {
        "block_input": noise(key_list[0], (MICRO, TOKENS, D), 1.0, 6.0, ((1, 64),)),
        "output_grad": noise(key_list[1], (MICRO, TOKENS, D), 1.0, 6.0, ((1, 64),)),
        "sequence_lengths": draw_sequence_lengths(jax.random.fold_in(key_list[12], 71), 0),
        "norm_gain": jnp.clip(1.0 + 0.18 * jax.random.normal(key_list[3], (2, 2, D), jnp.float32), 0.1, 1.9),
        "norm_bias": noise(key_list[4], (2, 2, D), 0.3, 1.8, ((0, 2),), jnp.float32),
        "attention_weight": noise(key_list[5], (2, 3, D, D), D ** -0.5, 0.25, ((0, 2), (3, 4))),
        "attention_bias": noise(key_list[6], (2, 3, D), 0.1, 0.6, ((0, 2), (2, 4)), jnp.float32),
        "output_weight": noise(key_list[7], (2, D, D), (max(D // 128, 1)) ** -0.5, 3.0, ((0, 2), (1, 4))),
        "up_weight": noise(key_list[8], (2, D, FF), D ** -0.5, 0.25, ((0, 2), (2, 4))),
        "up_bias": noise(key_list[9], (2, FF), 0.3, 1.8, ((0, 2), (1, 4)), jnp.float32),
        "down_weight": noise(key_list[10], (2, FF, D), FF ** -0.5, 0.125, ((0, 2), (1, 4))),
        "branch_bias": noise(key_list[11], (2, D), 0.3, 1.8, ((0, 2),), jnp.float32),
    }


@jax.custom_vjp
def low(v):
    return lax.optimization_barrier(v.astype(jnp.bfloat16)).astype(jnp.float32)

@jax.custom_vjp
def low_back(v):
    return v

def low_keep(v):
    return (low(v), None)

def low_pass(kept, grad):
    return (grad,)

def back_keep(v):
    return (v, None)

def back_low(kept, grad):
    return (low(grad),)
low.defvjp(low_keep, low_pass)
low_back.defvjp(back_keep, back_low)

def product(left, right):
    return jnp.dot(left, right, precision=lax.Precision.HIGHEST, preferred_element_type=jnp.float32)

def norm_pair(rows, gains, biases):
    centre = rows - lax.optimization_barrier(jnp.mean(rows, axis=-1, keepdims=True))
    spread = lax.optimization_barrier(jnp.mean(centre * centre, axis=-1, keepdims=True))
    normed = centre * lax.rsqrt(spread + 1e-05)
    return (normed * gains[0] + biases[0], normed * gains[1] + biases[1])

def sequence_starts(lengths, positions):
    ends = jnp.cumsum(lengths).astype(jnp.int32)
    before = jnp.where(ends[None, :] <= positions[:, None], lengths[None, :], 0)
    return lax.optimization_barrier(jnp.sum(before, axis=1)).astype(jnp.int32)

def rotary_tables(offsets):
    rates = 1.0 / 10000.0 ** (jnp.arange(0, ROT, 2).astype(jnp.float32) / ROT)
    angles = offsets.astype(jnp.float32)[:, None] * rates[None, :]
    return (jnp.cos(angles), jnp.sin(angles))

def rotate(values, cosine, sine):
    width = cosine.shape[-1]
    first = values[..., :width]
    second = values[..., width:2 * width]
    rest = values[..., 2 * width:]
    cos_rows = cosine[:, None, :]
    sin_rows = sine[:, None, :]
    return jnp.concatenate([first * cos_rows - second * sin_rows, second * cos_rows + first * sin_rows, rest], axis=-1)

def attend_block(queries, keys, values, query_place, query_start):
    scores = jnp.einsum('qhd,khd->hqk', queries, keys, precision=lax.Precision.HIGHEST) * HEAD_DIM ** (-0.5)
    scores = low_back(scores)
    key_place = jnp.arange(keys.shape[0], dtype=jnp.int32)
    allowed = (key_place[None, :] <= query_place[:, None]) & (key_place[None, :] >= query_start[:, None])
    weights = jax.nn.softmax(jnp.where(allowed[None], scores, -jnp.inf), axis=-1)
    return jnp.einsum('hqk,khd->qhd', low(weights), values, precision=lax.Precision.HIGHEST)

def layer(rows, lengths, section_params):
    gains, biases, attention_weight, attention_bias, output_weight, up_weight, up_bias, down_weight, branch_bias = section_params
    attention_in, feed_in = norm_pair(rows, gains, biases)
    attention_in = low(attention_in)
    feed_in = low(feed_in)
    query_pre = low_back(product(attention_in, attention_weight[0]) + attention_bias[0])
    key_pre = low_back(product(attention_in, attention_weight[1]) + attention_bias[1])
    values = low_back(low(product(attention_in, attention_weight[2]) + attention_bias[2]))
    positions = jnp.arange(TOKENS, dtype=jnp.int32)
    starts = sequence_starts(lengths, positions)
    cosine, sine = rotary_tables(positions - starts)
    shaped = (TOKENS, HEADS, HEAD_DIM)
    queries = low(rotate(query_pre.reshape(shaped), cosine, sine))
    keys = low(rotate(key_pre.reshape(shaped), cosine, sine))
    values = values.reshape(shaped)
    blocks = TOKENS // GROUP

    def one_block(pieces):
        return attend_block(pieces[0], keys, values, pieces[1], pieces[2])
    attention = lax.map(jax.checkpoint(one_block), (queries.reshape(blocks, GROUP, HEADS, HEAD_DIM), positions.reshape(blocks, GROUP), starts.reshape(blocks, GROUP)))
    attention = low_back(low(attention.reshape(TOKENS, D)))
    up_pre = low_back(product(feed_in, up_weight) + up_bias)
    hidden = low(jax.nn.gelu(up_pre, approximate=False))
    return rows + product(attention, output_weight) + product(hidden, down_weight) + branch_bias

def reference(block_input, output_grad, sequence_lengths, norm_gain, norm_bias, attention_weight, attention_bias, output_weight, up_weight, up_bias, down_weight, branch_bias):
    params = tuple((item.astype(jnp.float32) for item in (norm_gain, norm_bias, attention_weight, attention_bias, output_weight, up_weight, up_bias, down_weight, branch_bias)))
    inputs = block_input.astype(jnp.float32)
    nudge = jnp.zeros_like(inputs)

    def forward(inputs, nudge, params):
        firsts = []
        lasts = []
        for micro_index in range(MICRO):
            lengths = sequence_lengths[micro_index]
            early = low(layer(inputs[micro_index], lengths, tuple((item[0] for item in params))))
            early = low_back(early + nudge[micro_index])
            firsts.append(early)
            lasts.append(layer(early, lengths, tuple((item[1] for item in params))))
        return (jnp.stack(firsts), jnp.stack(lasts))
    (firsts, lasts), pullback = jax.vjp(forward, inputs, nudge, params)
    input_grad, middle_grad, param_grads = pullback((jnp.zeros_like(firsts), output_grad.astype(jnp.float32)))
    section_output = jnp.stack([firsts, lasts]).astype(jnp.bfloat16)
    section_input_grad = jnp.stack([input_grad, middle_grad]).astype(jnp.bfloat16)
    return (section_output, section_input_grad, param_grads[0], param_grads[1], param_grads[2], param_grads[3], param_grads[4], param_grads[5], param_grads[6], param_grads[7], param_grads[8])
```

```python
from functools import partial

import jax
import jax.numpy as jnp
from jax import lax
from jax.experimental import pallas as pl
from jax.experimental.pallas import tpu as pltpu
from jax.sharding import PartitionSpec as P

HEAD_DIM = 64
ROT = 16
MESH = pl.DeviceIdType.MESH
F32 = jnp.float32
BF16 = jnp.bfloat16
VMEM_LIMIT = 56 * 1024 * 1024
NCTX = 16
NTP = 4
BLK = 512
OWN = 128
MASKED = -1e30
LOWEST = -1e29


def dot_nn(a, b):
    return lax.dot_general(a, b, (((1,), (0,)), ((), ())), preferred_element_type=F32)


def dot_nt(a, b):
    return lax.dot_general(a, b, (((1,), (1,)), ((), ())), preferred_element_type=F32)


def dot_tn(a, b):
    return lax.dot_general(a, b, (((0,), (0,)), ((), ())), preferred_element_type=F32)


def phi(v):
    return 0.5 * (1.0 + lax.erf(v * (0.5**0.5)))


def gelu(v):
    return v * phi(v)


def gelu_slope(v):
    return phi(v) + v * jnp.exp(-0.5 * v * v) * 0.3989422804014327


def normed(rows):
    centre = rows - jnp.mean(rows, axis=-1, keepdims=True)
    spread = jnp.mean(centre * centre, axis=-1, keepdims=True)
    inverse = lax.rsqrt(spread + 1e-05)
    return centre * inverse, inverse


def greet(peers):
    barrier = pltpu.get_barrier_semaphore()
    for peer in peers:
        pl.semaphore_signal(barrier, inc=1, device_id=peer, device_id_type=MESH)
    pl.semaphore_wait(barrier, len(peers))


def ctx_peers(c):
    return [{"ctx": lax.rem(c + r, NCTX)} for r in range(1, NCTX)]


def tp_peers(t):
    return [{"tp": lax.rem(t + r, NTP)} for r in range(1, NTP)]


def remote(src, dst, send, recv, peer):
    return pltpu.make_async_remote_copy(
        src_ref=src, dst_ref=dst, send_sem=send, recv_sem=recv, device_id=peer, device_id_type=MESH
    )


def lanes(shape):
    return lax.broadcasted_iota(jnp.int32, shape, 1)


def turn(tile, table, sign):
    back = pltpu.roll(tile, tile.shape[1] - 8, 1)
    ahead = pltpu.roll(tile, 8, 1)
    return tile * table[0] + (back * table[1] + ahead * table[2]) * sign


def turn_left(tile, table, sign):
    back = pltpu.roll(tile, tile.shape[1] - 8, 1)
    ahead = pltpu.roll(tile, 8, 1)
    left = lanes(tile.shape) < HEAD_DIM
    return jnp.where(left, tile * table[0] + (back * table[1] + ahead * table[2]) * sign, tile)


def my_head(tile, group, place):
    swapped = pltpu.roll(tile, HEAD_DIM, 1)
    chosen = jnp.where(group == place, tile, swapped)
    half = lanes(tile.shape) // HEAD_DIM
    return jnp.where(half == place, chosen, 0.0)


def top_block(d):
    return jnp.maximum(d, NCTX - 1 - d)


def key_mask(key_block, first, shape, place_ref, slot, columns):
    key = key_block * BLK + first + lax.broadcasted_iota(jnp.int32, shape, 0)
    return (key <= place_ref[slot, 0:1, columns]) & (key >= place_ref[slot, 1:2, columns])


def needs_mask(key_block, query_block):
    return (key_block == 0) | (key_block == query_block) | (query_block == NCTX - 1)


def forward_kernel(
    x_ref,
    watt,
    batt,
    wo,
    wup,
    bup,
    wdn,
    bbr,
    gains,
    biases,
    rot,
    place,
    out_ref,
    xg,
    qpad,
    kvall,
    ot,
    lse,
    att,
    hid,
    kvs,
    qs,
    qin,
    kvt,
    acc,
    top,
    oout,
    oin,
    ffo,
    br,
    rsin,
    xsend,
    xrecv,
    kvsend,
    kvrecv,
    psend,
    precv,
    rsend,
    rrecv,
):
    c = lax.axis_index("ctx")
    t = lax.axis_index("tp")
    group = c // (NCTX // 2)
    partner = NCTX - 1 - c
    greet(tp_peers(t) + ctx_peers(c))

    gathers = [
        remote(x_ref, xg.at[t], xsend.at[r], xrecv.at[r], peer)
        for r, peer in enumerate(tp_peers(t))
    ]
    for copy in gathers:
        copy.start()
    xg[t] = x_ref[...]

    def project(part):
        xhat, _ = normed(xg[part].astype(F32))
        attention_in = (xhat * gains[0:1] + biases[0:1]).astype(BF16)
        pre = dot_nn(attention_in, watt[...]) + batt[...]
        rows = pl.ds(pl.multiple_of(part * OWN, OWN), OWN)
        table = [rot[0, j, rows, :] for j in range(3)]
        qs[rows, :] = (turn(pre[:, 0:128], table, 1.0) * 0.125).astype(BF16)
        kvs[0, rows, :] = turn_left(pre[:, 128:256], table, 1.0).astype(BF16)
        kvs[1, rows, :] = turn_left(pre[:, 256:384], table, 1.0).astype(BF16)

    project(t)
    for r, copy in enumerate(gathers):
        copy.wait_recv()
        project(lax.rem(t + NTP - 1 - r, NTP))

    query_copy = remote(qs, qin, psend.at[0], precv.at[0], {"ctx": partner})
    query_copy.start()

    def key_copy(r):
        d = lax.rem(c + r, NCTX)
        return c <= top_block(d), remote(
            kvs.at[d // (NCTX // 2)], kvall.at[c], kvsend.at[d], kvrecv.at[c], {"ctx": d}
        )

    @pl.loop(1, NCTX)
    def _(r):
        wanted, copy = key_copy(r)

        @pl.when(wanted)
        def _():
            copy.start()

    kvall[c] = kvs[group]

    @pl.loop(0, NTP)
    def _(part):
        xhat, _ = normed(xg[part].astype(F32))
        feed_in = (xhat * gains[1:2] + biases[1:2]).astype(BF16)
        hidden = gelu(dot_nn(feed_in, wup[...]) + bup[...]).astype(BF16)
        hid[part] = hidden
        ffo[part] = dot_nn(hidden, wdn[...])

    qpad[0] = my_head(qs[...].astype(F32), group, 0).astype(BF16)
    query_copy.wait_recv()
    qpad[1] = my_head(qin[...].astype(F32), group, 0).astype(BF16)
    acc[...] = jnp.zeros_like(acc)
    top[...] = jnp.full_like(top, LOWEST)

    def visit(key_block, slot, masked):
        scores = dot_nt(kvall[key_block], qpad[slot])
        if masked:
            allowed = key_mask(key_block, 0, scores.shape, place, slot, slice(None))
            scores = jnp.where(allowed, scores, MASKED)
        old = top[slot]
        new = jnp.maximum(old, jnp.max(scores, axis=0, keepdims=True))
        weights = jnp.exp(scores - new).astype(BF16)
        top[slot] = new
        acc[slot] = acc[slot] * jnp.exp(old - new) + dot_nn(kvt[...], weights)

    @pl.loop(0, NCTX)
    def _(r):
        key_block = lax.rem(c + NCTX - r, NCTX)

        @pl.when(key_block <= top_block(c))
        def _():
            @pl.when(r > 0)
            def _():
                remote(
                    kvs.at[0],
                    kvall.at[key_block],
                    kvsend.at[0],
                    kvrecv.at[key_block],
                    {"ctx": partner},
                ).wait_recv()

            turned = kvall[key_block].astype(F32).T
            row = lax.broadcasted_iota(jnp.int32, turned.shape, 0)
            kvt[...] = jnp.where(row < HEAD_DIM, 1.0, turned).astype(BF16)

            @pl.loop(0, 2)
            def _(slot):
                query_block = jnp.where(slot == 0, c, partner)
                reached = key_block <= query_block
                edge = needs_mask(key_block, query_block)

                @pl.when(reached & edge)
                def _():
                    visit(key_block, slot, True)

                @pl.when(reached & jnp.logical_not(edge))
                def _():
                    visit(key_block, slot, False)

    def finish(slot):
        total = acc[slot, 0:HEAD_DIM, :]
        mean = acc[slot, HEAD_DIM:, :] / total
        ot[slot] = mean
        lse[slot] = top[slot] + jnp.log(total[0:1])
        blank = jnp.zeros_like(mean)
        first = jnp.where(group == 0, mean, blank)
        second = jnp.where(group == 0, blank, mean)
        return jnp.concatenate([first, second], axis=0).T.astype(BF16)

    oout[...] = finish(1)
    out_copy = remote(oout, oin, psend.at[1], precv.at[1], {"ctx": partner})
    out_copy.start()
    own_out = finish(0)
    out_copy.wait_recv()
    att[...] = own_out + oin[...]

    def branch(part):
        rows = pl.ds(pl.multiple_of(part * OWN, OWN), OWN)
        return dot_nn(att[rows, :], wo[...]) + ffo[part]

    scatters = []
    for r in range(1, NTP):
        d = lax.rem(t + r, NTP)
        br[r - 1] = branch(d).astype(BF16)
        copy = remote(br.at[r - 1], rsin.at[r - 1], rsend.at[r - 1], rrecv.at[r - 1], {"tp": d})
        copy.start()
        scatters.append(copy)
    result = x_ref[...].astype(F32) + bbr[...] + branch(t)
    for r, copy in enumerate(scatters):
        copy.wait_recv()
        result = result + rsin[r].astype(F32)
    out_ref[...] = result.astype(BF16)

    for copy in gathers + scatters + [query_copy, out_copy]:
        copy.wait_send()

    @pl.loop(1, NCTX)
    def _(r):
        wanted, copy = key_copy(r)

        @pl.when(wanted)
        def _():
            copy.wait_send()


def whole(count):
    return [pl.BlockSpec(memory_space=pltpu.VMEM)] * count


def dma(*shape):
    return pltpu.SemaphoreType.DMA(shape)


def layer_forward(layer, x, weights, rot, place):
    d = x.shape[1]
    shapes = [
        ((OWN, d), BF16),
        ((NTP, OWN, d), BF16),
        ((2, BLK, 128), BF16),
        ((NCTX, BLK, 128), BF16),
        ((2, HEAD_DIM, BLK), F32),
        ((2, 1, BLK), F32),
        ((BLK, 128), BF16),
        ((NTP, OWN, d), BF16),
    ]
    operands = (x, *weights, rot, place)
    return pl.pallas_call(
        forward_kernel,
        out_shape=[jax.ShapeDtypeStruct(s, k) for s, k in shapes],
        in_specs=whole(len(operands)),
        out_specs=whole(len(shapes)),
        scratch_shapes=[
            pltpu.VMEM((2, BLK, 128), BF16),
            pltpu.VMEM((BLK, 128), BF16),
            pltpu.VMEM((BLK, 128), BF16),
            pltpu.VMEM((128, BLK), BF16),
            pltpu.VMEM((2, 128, BLK), F32),
            pltpu.VMEM((2, 1, BLK), F32),
            pltpu.VMEM((BLK, 128), BF16),
            pltpu.VMEM((BLK, 128), BF16),
            pltpu.VMEM((NTP, OWN, d), F32),
            pltpu.VMEM((NTP - 1, OWN, d), BF16),
            pltpu.VMEM((NTP - 1, OWN, d), BF16),
            dma(3),
            dma(3),
            dma(NCTX),
            dma(NCTX),
            dma(2),
            dma(2),
            dma(3),
            dma(3),
        ],
        compiler_params=pltpu.CompilerParams(
            collective_id=1 + layer, has_side_effects=True, vmem_limit_bytes=VMEM_LIMIT
        ),
        name=f"layer_forward_{layer}",
    )(*operands)


def backward_kernel(
    g_ref,
    xg,
    qpad,
    kvall,
    ot,
    lse,
    att,
    hid,
    watt,
    wo,
    wup,
    bup,
    wdn,
    gains,
    biases,
    rot,
    place,
    out_ref,
    gw,
    gv,
    gg,
    dos,
    doin,
    dopad,
    delta,
    dqt,
    dkva,
    dkvo,
    dkvi,
    dqs,
    dqi,
    ain,
    fin,
    ugs,
    dxh,
    dproj,
    dxs,
    rsin,
    kvt,
    xsend,
    xrecv,
    kvsend,
    kvrecv,
    psend,
    precv,
    rsend,
    rrecv,
):
    c = lax.axis_index("ctx")
    t = lax.axis_index("tp")
    group = c // (NCTX // 2)
    partner = NCTX - 1 - c
    d_model = g_ref.shape[1]
    greet(tp_peers(t) + ctx_peers(c))

    gathers = [
        remote(g_ref, gg.at[t], xsend.at[r], xrecv.at[r], peer)
        for r, peer in enumerate(tp_peers(t))
    ]
    for copy in gathers:
        copy.start()
    gg[t] = g_ref[...]

    def attention_grad(part):
        rows = pl.ds(pl.multiple_of(part * OWN, OWN), OWN)
        dos[rows, :] = dot_nt(gg[part], wo[...]).astype(BF16)

    gv[...] = jnp.zeros_like(gv)
    gv[4:5, :] = jnp.sum(g_ref[...].astype(F32), axis=0, keepdims=True)
    attention_grad(t)
    for r, copy in enumerate(gathers):
        copy.wait_recv()
        attention_grad(lax.rem(t + NTP - 1 - r, NTP))
    grad_copy = remote(dos, doin, psend.at[0], precv.at[0], {"ctx": partner})
    grad_copy.start()

    @pl.loop(0, NTP)
    def _(part):
        xhat, _ = normed(xg[part].astype(F32))
        ain[part] = (xhat * gains[0:1] + biases[0:1]).astype(BF16)
        feed_in = (xhat * gains[1:2] + biases[1:2]).astype(BF16)
        fin[part] = feed_in
        up_pre = dot_nn(feed_in, wup[...]) + bup[...]
        up_grad = (dot_nt(gg[part], wdn[...]) * gelu_slope(up_pre)).astype(BF16)
        ugs[part] = up_grad
        gv[5:6, :] += jnp.sum(up_grad.astype(F32), axis=0, keepdims=True)
        feed_grad = dot_nt(up_grad, wup[...])
        gv[1:2, :] += jnp.sum(xhat * feed_grad, axis=0, keepdims=True)
        gv[3:4, :] += jnp.sum(feed_grad, axis=0, keepdims=True)
        dxh[part] = feed_grad * gains[1:2]

    full_grad = gg[...].reshape(BLK, d_model)
    gw[0:128, :] = dot_tn(att[...], full_grad).astype(BF16)
    gw[128:640, :] = dot_tn(fin[...].reshape(BLK, d_model), ugs[...].reshape(BLK, -1)).astype(BF16)
    gw[640:1152, :] = dot_tn(hid[...].reshape(BLK, -1), full_grad).astype(BF16)

    def prepare(slot, tile):
        padded = my_head(tile, group, 1)
        dopad[slot] = padded.astype(BF16)
        delta[slot] = jnp.sum(padded.T[HEAD_DIM:, :] * ot[slot], axis=0, keepdims=True)

    prepare(0, dos[...].astype(F32))
    grad_copy.wait_recv()
    prepare(1, doin[...].astype(F32))
    dqt[...] = jnp.zeros_like(dqt)

    def visit(key_block, slot, masked):
        keys = kvall[key_block]
        scores = dot_nt(keys, qpad[slot])
        weights = jnp.exp(scores - lse[slot])
        if masked:
            allowed = key_mask(key_block, 0, scores.shape, place, slot, slice(None))
            weights = jnp.where(allowed, weights, 0.0)
        weight_grad = dot_nt(keys, dopad[slot])
        score_grad = (weights * (weight_grad - delta[slot])).astype(BF16)
        dkva[...] += dot_nn(weights.astype(BF16), dopad[slot]) + dot_nn(score_grad, qpad[slot])
        dqt[slot] += dot_nn(kvt[...], score_grad)

    def key_copy(key_block):
        return remote(
            dkvo.at[key_block],
            dkvi.at[c],
            kvsend.at[key_block],
            kvrecv.at[c],
            {"ctx": key_block},
        )

    @pl.loop(1, NCTX + 1)
    def _(r):
        key_block = lax.rem(c + r, NCTX)

        @pl.when(key_block <= top_block(c))
        def _():
            kvt[...] = kvall[key_block].astype(F32).T.astype(BF16)
            dkva[...] = jnp.zeros_like(dkva)

            @pl.loop(0, 2)
            def _(slot):
                query_block = jnp.where(slot == 0, c, partner)
                reached = key_block <= query_block
                edge = needs_mask(key_block, query_block)

                @pl.when(reached & edge)
                def _():
                    visit(key_block, slot, True)

                @pl.when(reached & jnp.logical_not(edge))
                def _():
                    visit(key_block, slot, False)

            dkvo[key_block] = dkva[...].astype(BF16)

            @pl.when(r < NCTX)
            def _():
                key_copy(key_block).start()

    def query_grad(slot):
        mean = dqt[slot, 0:HEAD_DIM, :] * 0.125
        blank = jnp.zeros_like(mean)
        first = jnp.where(group == 0, mean, blank)
        second = jnp.where(group == 0, blank, mean)
        tile = jnp.concatenate([first, second], axis=0).T
        return turn(tile, [rot[slot, j] for j in range(3)], -1.0).astype(BF16)

    dqs[...] = query_grad(1)
    query_copy = remote(dqs, dqi, psend.at[1], precv.at[1], {"ctx": partner})
    query_copy.start()
    own_query = query_grad(0)
    table = [rot[0, j] for j in range(3)]

    def key_grad(half):
        dkva[...] = jnp.zeros_like(dkva)

        @pl.loop(0, NCTX // 2)
        def _(step):
            source = half * (NCTX // 2) + step

            @pl.when(source == c)
            def _():
                dkva[...] += dkvo[c].astype(F32)

            @pl.when((c <= top_block(source)) & (source != c))
            def _():
                remote(
                    dkvo.at[0], dkvi.at[source], kvsend.at[0], kvrecv.at[source], {"ctx": partner}
                ).wait_recv()
                dkva[...] += dkvi[source].astype(F32)

        return turn_left(dkva[...], table, -1.0).astype(BF16)

    dproj[:, 128:256] = key_grad(0)
    dproj[:, 256:384] = key_grad(1)
    query_copy.wait_recv()
    dproj[:, 0:128] = own_query + dqi[...]
    gv[6:7, 0:384] = jnp.sum(dproj[...].astype(F32), axis=0, keepdims=True)

    def input_part(part):
        rows = pl.ds(pl.multiple_of(part * OWN, OWN), OWN)
        xhat, _ = normed(xg[part].astype(F32))
        grad = dot_nt(dproj[rows, :], watt[...])
        gv[0:1, :] += jnp.sum(xhat * grad, axis=0, keepdims=True)
        gv[2:3, :] += jnp.sum(grad, axis=0, keepdims=True)
        return dxh[part] + grad * gains[0:1]

    scatters = []
    for r in range(1, NTP):
        d = lax.rem(t + r, NTP)
        dxs[r - 1] = input_part(d).astype(BF16)
        copy = remote(dxs.at[r - 1], rsin.at[r - 1], rsend.at[r - 1], rrecv.at[r - 1], {"tp": d})
        copy.start()
        scatters.append(copy)
    total = input_part(t)
    gw[1152:1536, :] = dot_tn(dproj[...], ain[...].reshape(BLK, d_model)).astype(BF16)
    for r, copy in enumerate(scatters):
        copy.wait_recv()
        total = total + rsin[r].astype(F32)
    xhat, inverse = normed(xg[t].astype(F32))
    along = jnp.mean(total * xhat, axis=-1, keepdims=True)
    rows_grad = (total - jnp.mean(total, axis=-1, keepdims=True) - xhat * along) * inverse
    out_ref[...] = (g_ref[...].astype(F32) + rows_grad).astype(BF16)

    for copy in gathers + scatters + [grad_copy, query_copy]:
        copy.wait_send()

    @pl.loop(1, NCTX)
    def _(r):
        key_block = lax.rem(c + r, NCTX)

        @pl.when(key_block <= top_block(c))
        def _():
            key_copy(key_block).wait_send()


def layer_backward(layer, g, saved, weights, rot, place):
    d = g.shape[1]
    shapes = [((OWN, d), BF16), ((1536, d), BF16), ((8, d), F32)]
    watt, batt, wo, wup, bup, wdn, bbr, gains, biases = weights
    operands = (g, *saved, watt, wo, wup, bup, wdn, gains, biases, rot, place)
    return pl.pallas_call(
        backward_kernel,
        out_shape=[jax.ShapeDtypeStruct(s, k) for s, k in shapes],
        in_specs=whole(len(operands)),
        out_specs=whole(len(shapes)),
        scratch_shapes=[
            pltpu.VMEM((NTP, OWN, d), BF16),
            pltpu.VMEM((BLK, 128), BF16),
            pltpu.VMEM((BLK, 128), BF16),
            pltpu.VMEM((2, BLK, 128), BF16),
            pltpu.VMEM((2, 1, BLK), F32),
            pltpu.VMEM((2, 128, BLK), F32),
            pltpu.VMEM((BLK, 128), F32),
            pltpu.VMEM((NCTX, BLK, 128), BF16),
            pltpu.VMEM((NCTX, BLK, 128), BF16),
            pltpu.VMEM((BLK, 128), BF16),
            pltpu.VMEM((BLK, 128), BF16),
            pltpu.VMEM((NTP, OWN, d), BF16),
            pltpu.VMEM((NTP, OWN, d), BF16),
            pltpu.VMEM((NTP, OWN, d), BF16),
            pltpu.VMEM((NTP, OWN, d), F32),
            pltpu.VMEM((BLK, 384), BF16),
            pltpu.VMEM((NTP - 1, OWN, d), BF16),
            pltpu.VMEM((NTP - 1, OWN, d), BF16),
            pltpu.VMEM((128, BLK), BF16),
            dma(3),
            dma(3),
            dma(NCTX),
            dma(NCTX),
            dma(2),
            dma(2),
            dma(3),
            dma(3),
        ],
        compiler_params=pltpu.CompilerParams(
            collective_id=3 + layer, has_side_effects=True, vmem_limit_bytes=VMEM_LIMIT
        ),
        name=f"layer_backward_{layer}",
    )(*operands)


def swap_kernel(count, *refs):
    sources = refs[:count]
    results = refs[count : 2 * count]
    send, recv = refs[2 * count :]
    other = {"section": 1 - lax.axis_index("section")}
    greet([other])
    copies = [
        remote(source, result, send.at[i], recv.at[i], other)
        for i, (source, result) in enumerate(zip(sources, results))
    ]
    for copy in copies:
        copy.start()
    for copy in copies:
        copy.wait()


def swap(arrays):
    count = len(arrays)
    return pl.pallas_call(
        partial(swap_kernel, count),
        out_shape=[jax.ShapeDtypeStruct(a.shape, a.dtype) for a in arrays],
        in_specs=[pl.BlockSpec(memory_space=pl.ANY)] * count,
        out_specs=[pl.BlockSpec(memory_space=pl.ANY)] * count,
        scratch_shapes=[dma(count), dma(count)],
        compiler_params=pltpu.CompilerParams(collective_id=0, has_side_effects=True),
        name="swap_weights",
    )(*arrays)


def reduce_kernel(
    gw0,
    gw1,
    gv0,
    gv1,
    rows0,
    rows1,
    wide,
    small,
    rows_out,
    other_w,
    sums,
    chunk_in,
    mine,
    gathered,
    other_v,
    vec,
    vec_in,
    vec_tp,
    vec_tp_in,
    csend,
    crecv,
    ssend,
    srecv,
    asend,
    arecv,
    vsend,
    vrecv,
    tsend,
    trecv,
):
    s = lax.axis_index("section")
    c = lax.axis_index("ctx")
    t = lax.axis_index("tp")
    other = {"section": 1 - s}
    greet([other] + tp_peers(t) + ctx_peers(c))
    chunk = sums.shape[1]

    def cross(sources, results):
        return [
            remote(source, result, csend.at[i], crecv.at[i], other)
            for i, (source, result) in enumerate(zip(sources, results))
        ]

    results = (other_w, other_v, rows_out.at[s])

    @pl.when(s == 0)
    def _():
        for copy in cross((gw1, gv1, rows1), results):
            copy.start()
        rows_out[0] = rows0[...]

    @pl.when(s == 1)
    def _():
        for copy in cross((gw0, gv0, rows0), results):
            copy.start()
        rows_out[1] = rows1[...]

    crosses = cross((gw0, gv0, rows0), results)
    crosses[1].wait_recv()
    vec[...] = jnp.where(s == 0, gv0[...], gv1[...]) + other_v[...]

    def vec_copy(r):
        d = lax.rem(c + r, NCTX)
        return remote(vec, vec_in.at[r], vsend.at[r], vrecv.at[r], {"ctx": d})

    @pl.loop(1, NCTX)
    def _(r):
        vec_copy(r).start()

    crosses[0].wait_recv()

    @pl.loop(0, NCTX)
    def _(j):
        rows = pl.ds(pl.multiple_of(j * chunk, chunk), chunk)
        mine_part = jnp.where(s == 0, gw0[rows, :].astype(F32), gw1[rows, :].astype(F32))
        sums[j] = (mine_part + other_w[rows, :].astype(F32)).astype(BF16)

    def scatter(r):
        d = lax.rem(c + r, NCTX)
        return remote(sums.at[d], chunk_in.at[r], ssend.at[r], srecv.at[r], {"ctx": d})

    @pl.loop(1, NCTX)
    def _(r):
        scatter(r).start()

    total_vec = vec[...]
    for r in range(1, NCTX):
        vec_copy(r).wait_recv()
        total_vec = total_vec + vec_in[r]
    vec_tp[...] = total_vec
    tp_copies = [
        remote(vec_tp, vec_tp_in.at[r], tsend.at[r], trecv.at[r], peer)
        for r, peer in enumerate(tp_peers(t))
    ]
    for copy in tp_copies:
        copy.start()

    total = sums[c].astype(F32)
    for r in range(1, NCTX):
        scatter(r).wait_recv()
        total = total + chunk_in[r].astype(F32)
    mine[...] = total.astype(BF16)

    def gather(r):
        d = lax.rem(c + r, NCTX)
        return remote(mine, gathered.at[c], asend.at[r], arecv.at[r], {"ctx": d})

    @pl.loop(1, NCTX)
    def _(r):
        gather(r).start()

    rows = pl.ds(pl.multiple_of(c * chunk, chunk), chunk)
    wide[rows, :] = total
    shared = total_vec
    for r, copy in enumerate(tp_copies):
        copy.wait_recv()
        shared = shared + vec_tp_in[r]
    row = lax.broadcasted_iota(jnp.int32, shared.shape, 0)
    small[...] = jnp.where(row < 5, shared, total_vec)

    @pl.loop(1, NCTX)
    def _(r):
        source = lax.rem(c + NCTX - r, NCTX)
        remote(mine, gathered.at[source], asend.at[r], arecv.at[r], other).wait_recv()
        rows = pl.ds(pl.multiple_of(source * chunk, chunk), chunk)
        wide[rows, :] = gathered[source].astype(F32)

    crosses[2].wait_recv()
    for copy in tp_copies + crosses:
        copy.wait_send()

    @pl.loop(1, NCTX)
    def _(r):
        vec_copy(r).wait_send()
        scatter(r).wait_send()
        gather(r).wait_send()


def reduce_gradients(gw, gv, rows):
    total, d = gw[0].shape
    chunk = total // NCTX
    operands = (*gw, *gv, *rows)
    shapes = [((total, d), F32), ((8, d), F32), ((2, *rows[0].shape), BF16)]
    return pl.pallas_call(
        reduce_kernel,
        out_shape=[jax.ShapeDtypeStruct(s, k) for s, k in shapes],
        in_specs=whole(len(operands)),
        out_specs=whole(len(shapes)),
        scratch_shapes=[
            pltpu.VMEM((total, d), BF16),
            pltpu.VMEM((NCTX, chunk, d), BF16),
            pltpu.VMEM((NCTX, chunk, d), BF16),
            pltpu.VMEM((chunk, d), BF16),
            pltpu.VMEM((NCTX, chunk, d), BF16),
            pltpu.VMEM((8, d), F32),
            pltpu.VMEM((8, d), F32),
            pltpu.VMEM((NCTX, 8, d), F32),
            pltpu.VMEM((8, d), F32),
            pltpu.VMEM((NTP - 1, 8, d), F32),
            dma(3),
            dma(3),
            dma(NCTX),
            dma(NCTX),
            dma(NCTX),
            dma(NCTX),
            dma(NCTX),
            dma(NCTX),
            dma(3),
            dma(3),
        ],
        compiler_params=pltpu.CompilerParams(
            collective_id=5, has_side_effects=True, vmem_limit_bytes=VMEM_LIMIT
        ),
        name="reduce_gradients",
    )(*operands)


def sequence_starts(lengths, positions):
    ends = jnp.cumsum(lengths).astype(jnp.int32)
    before = jnp.where(ends[None, :] <= positions[:, None], lengths[None, :], 0)
    return jnp.sum(before, axis=1).astype(jnp.int32)


def rotary_lanes(offsets):
    rates = 1.0 / 10000.0 ** (jnp.arange(0, ROT, 2).astype(F32) / ROT)
    angles = offsets.astype(F32)[:, None] * rates[None, :]
    cosine, sine = jnp.cos(angles), jnp.sin(angles)
    zeros = jnp.zeros_like(sine)
    rest = jnp.zeros((offsets.shape[0], HEAD_DIM - ROT), F32)
    tables = (
        jnp.concatenate([cosine, cosine, rest + 1.0], axis=1),
        jnp.concatenate([-sine, zeros, rest], axis=1),
        jnp.concatenate([zeros, sine, rest], axis=1),
    )
    return jnp.stack([jnp.concatenate([table, table], axis=1) for table in tables])


def pack_attention(items):
    q, k, v = items
    half = HEAD_DIM
    return jnp.concatenate([q, k[:, :half], v[:, :half], k[:, half:], v[:, half:]], axis=1)


def local(
    block_input,
    output_grad,
    sequence_lengths,
    norm_gain,
    norm_bias,
    attention_weight,
    attention_bias,
    output_weight,
    up_weight,
    up_bias,
    down_weight,
    branch_bias,
):
    s = lax.axis_index("section")
    c = lax.axis_index("ctx")
    own = (
        pack_attention([attention_weight[0, k] for k in range(3)]),
        pack_attention([attention_bias[:, k] for k in range(3)]),
        output_weight[0],
        up_weight[0],
        up_bias,
        down_weight[0],
        branch_bias,
        norm_gain[0],
        norm_bias[0],
    )
    received = swap(own)
    first = [jnp.where(s == 0, a, b) for a, b in zip(own, received)]
    second = [jnp.where(s == 0, b, a) for a, b in zip(own, received)]

    x = lax.dynamic_index_in_dim(block_input, s, 0, keepdims=False)
    g = lax.dynamic_index_in_dim(output_grad, s, 0, keepdims=False)
    lengths = lax.dynamic_index_in_dim(sequence_lengths, s, 0, keepdims=False)
    steps = jnp.arange(BLK, dtype=jnp.int32)
    positions = jnp.concatenate([c * BLK + steps, (NCTX - 1 - c) * BLK + steps])
    starts = sequence_starts(lengths, positions)
    rot = rotary_lanes(positions - starts)
    rot = jnp.stack([rot[:, :BLK], rot[:, BLK:]])
    place = jnp.stack([positions.reshape(2, BLK), starts.reshape(2, BLK)], axis=1)

    early, *kept_first = layer_forward(0, x, first, rot, place)
    late, *kept_second = layer_forward(1, early, second, rot, place)
    middle, gw1, gv1 = layer_backward(1, g, kept_second, second, rot, place)
    given, gw0, gv0 = layer_backward(0, middle, kept_first, first, rot, place)

    wide, small, rows = reduce_gradients(
        (gw0, gw1),
        (gv0, gv1),
        (jnp.concatenate([early, given], axis=0), jnp.concatenate([late, middle], axis=0)),
    )
    packed = wide[1152:1536]
    half = HEAD_DIM
    query = packed[0:128]
    key = jnp.concatenate([packed[128 : 128 + half], packed[256 : 256 + half]], axis=0)
    value = jnp.concatenate([packed[128 + half : 256], packed[256 + half :]], axis=0)
    bias = small[6, 0:384]
    bias_parts = jnp.stack(
        [
            bias[0:128],
            jnp.concatenate([bias[128 : 128 + half], bias[256 : 256 + half]]),
            jnp.concatenate([bias[128 + half : 256], bias[256 + half :]]),
        ]
    )
    return (
        rows[None, :, 0:OWN],
        rows[None, :, OWN:],
        small[None, 0:2],
        small[None, 2:4],
        jnp.stack([query.T, key.T, value.T])[None],
        bias_parts[None],
        wide[None, 0:128],
        wide[None, 128:640],
        small[5:6],
        wide[None, 640:1152],
        small[4:5],
    )


def solution(mesh):
    placed = (
        P(None, ("ctx", "tp"), None),
        P(None, ("ctx", "tp"), None),
        P(),
        P("section", None, None),
        P("section", None, None),
        P("section", None, None, "tp"),
        P("section", None, "tp"),
        P("section", "tp", None),
        P("section", None, "tp"),
        P("section", "tp"),
        P("section", "tp", None),
        P("section", None),
    )
    return jax.shard_map(
        local,
        mesh=mesh,
        in_specs=placed,
        out_specs=(
            P("section", None, ("ctx", "tp"), None),
            P("section", None, ("ctx", "tp"), None),
            P("section", None, None),
            P("section", None, None),
            P("section", None, None, "tp"),
            P("section", None, "tp"),
            P("section", "tp", None),
            P("section", None, "tp"),
            P("section", "tp"),
            P("section", "tp", None),
            P("section", None),
        ),
        check_vma=False,
    )
```

```python
from types import SimpleNamespace

import jax
import jax.numpy as jnp
from jax import lax
from jax.experimental import pallas as pl
from jax.experimental.pallas import tpu as pltpu
from jax.sharding import PartitionSpec as P

HEAD_DIM = 64
ROT = 16
MESH = pl.DeviceIdType.MESH
F32 = jnp.float32
BF16 = jnp.bfloat16
VMEM_LIMIT = 56 * 1024 * 1024
NCTX = 16
NTP = 4
BLK = 512
OWN = 128
D = 512
LANES = 128
MASKED = -1e30
LOWEST = -1e29


def dot_nn(a, b):
    return lax.dot_general(a, b, (((1,), (0,)), ((), ())), preferred_element_type=F32)


def dot_nt(a, b):
    return lax.dot_general(a, b, (((1,), (1,)), ((), ())), preferred_element_type=F32)


def dot_tn(a, b):
    return lax.dot_general(a, b, (((0,), (0,)), ((), ())), preferred_element_type=F32)


def phi(v):
    return 0.5 * (1.0 + lax.erf(v * (0.5**0.5)))


def gelu(v):
    return v * phi(v)


def gelu_slope(v):
    return phi(v) + v * jnp.exp(-0.5 * v * v) * 0.3989422804014327


def normed(rows):
    centre = rows - jnp.mean(rows, axis=-1, keepdims=True)
    spread = jnp.mean(centre * centre, axis=-1, keepdims=True)
    inverse = lax.rsqrt(spread + 1e-05)
    return centre * inverse, inverse


def remote(src, dst, send, recv, peer):
    return pltpu.make_async_remote_copy(
        src_ref=src, dst_ref=dst, send_sem=send, recv_sem=recv, device_id=peer, device_id_type=MESH
    )


def lanes(shape):
    return lax.broadcasted_iota(jnp.int32, shape, 1)


def turn(tile, cosine, sine):
    back = pltpu.roll(tile, LANES - 8, 1)
    ahead = pltpu.roll(tile, 8, 1)
    other = jnp.where(lanes(tile.shape) % HEAD_DIM < 8, back, ahead)
    return tile * cosine + other * sine


def turn_left(tile, cosine, sine):
    return jnp.where(lanes(tile.shape) < HEAD_DIM, turn(tile, cosine, sine), tile)


def my_head(tile, group, half):
    swapped = pltpu.roll(tile, HEAD_DIM, 1)
    chosen = jnp.where(group == half, tile, swapped)
    return jnp.where(lanes(tile.shape) // HEAD_DIM == half, chosen, 0.0)


def two_head_tile(rows, group):
    blank = jnp.zeros_like(rows)
    first = jnp.where(group == 0, rows, blank)
    second = jnp.where(group == 0, blank, rows)
    return jnp.concatenate([first, second], axis=0).T


def top_block(d):
    return jnp.maximum(d, NCTX - 1 - d)


def needs_mask(key_block, query_block):
    return (key_block == 0) | (key_block == query_block) | (query_block == NCTX - 1)


def span(index, size):
    return pl.ds(pl.multiple_of(index * size, size), size)


OUTPUTS = (
    ("out_rows", (2, OWN, D), BF16),
    ("out_grads", (2, OWN, D), BF16),
    ("out_ff", (2 * D, D), F32),
    ("out_wo", (OWN, D), F32),
    ("out_att", (3, D, OWN), F32),
    ("out_small", (8, D), F32),
)

SCRATCH = (
    ("watt", (2, D, 384), BF16),
    ("wo", (2, NTP, OWN, D), BF16),
    ("wup", (2, D, D), BF16),
    ("wdn", (2, D, D), BF16),
    ("vecs", (2, 8, D), F32),
    ("xown", (2, OWN, D), BF16),
    ("fo", (2, OWN, D), BF16),
    ("xg", (2, NTP, OWN, D), BF16),
    ("qpad", (2, 2, BLK, LANES), BF16),
    ("kvall", (2, NCTX, BLK, LANES), BF16),
    ("ot", (2, 2, HEAD_DIM, BLK), F32),
    ("lse", (2, 2, 1, BLK), F32),
    ("hid", (2, NTP, OWN, D), BF16),
    ("kvs", (2, 2, BLK, LANES), BF16),
    ("qs", (2, BLK, LANES), BF16),
    ("qin", (2, BLK, LANES), BF16),
    ("oout", (2, 2, BLK, LANES), BF16),
    ("oin", (2, BLK, LANES), BF16),
    ("oa", (2, NTP, OWN, LANES), BF16),
    ("ob", (2, NTP, OWN, LANES), BF16),
    ("ffs", (2, NTP - 1, OWN, D), BF16),
    ("ffr", (2, NTP - 1, OWN, D), BF16),
    ("gown", (2, OWN, D), BF16),
    ("go", (2, OWN, D), BF16),
    ("gg", (2, NTP, OWN, D), BF16),
    ("dos", (2, NTP, OWN, LANES), BF16),
    ("doa", (2, NTP, OWN, LANES), BF16),
    ("dob", (2, NTP, OWN, LANES), BF16),
    ("dkvo", (2, NCTX, BLK, LANES), BF16),
    ("dkvi", (2, NCTX, BLK, LANES), BF16),
    ("dqs", (2, BLK, LANES), BF16),
    ("dqi", (2, BLK, LANES), BF16),
    ("dxs", (2, NTP - 1, OWN, D), BF16),
    ("dxr", (2, NTP - 1, OWN, D), BF16),
    ("gwp", (2, 2 * D, D), BF16),
    ("gwq", (2, D, D), BF16),
    ("gv", (2, 8, D), F32),
    ("kvt", (LANES, BLK), BF16),
    ("acc", (2, LANES, BLK), F32),
    ("top", (2, 1, BLK), F32),
    ("ffo", (OWN, D), F32),
    ("dopad", (2, BLK, LANES), BF16),
    ("delta", (2, 1, BLK), F32),
    ("dqt", (2, LANES, BLK), F32),
    ("dkva", (BLK, LANES), F32),
    ("ain", (NTP, OWN, D), BF16),
    ("fin", (NTP, OWN, D), BF16),
    ("ugs", (NTP, OWN, D), BF16),
    ("dxh", (NTP, OWN, D), F32),
    ("dproj", (BLK, 384), BF16),
    ("crp", (2 * D, D), BF16),
    ("crq", (D, D), BF16),
    ("crv", (8, D), F32),
    ("sump", (NCTX, 64, D), BF16),
    ("sumq", (NCTX, 32, D), BF16),
    ("inp", (NCTX, 64, D), BF16),
    ("inq", (NCTX, 32, D), BF16),
    ("minep", (64, D), BF16),
    ("mineq", (32, D), BF16),
    ("gatp", (NCTX, 64, D), BF16),
    ("gatq", (NCTX, 32, D), BF16),
    ("allq", (D, D), F32),
    ("vec", (8, D), F32),
    ("vec_in", (NCTX, 8, D), F32),
    ("vec_tp", (8, D), F32),
    ("vec_tp_in", (NTP - 1, 8, D), F32),
)

INPUTS = ("xin", "gin", "own_watt", "own_wo", "own_wup", "own_wdn", "own_vecs", "rot", "place")

SEMAPHORES = {}
COPIES = 0
for name, count in (
    ("weights", 4),
    ("wo", 3),
    ("wo_pass", 1),
    ("rows", 1),
    ("grads", 1),
    ("cross", 3),
    ("ps", NCTX),
    ("pg", NCTX),
    ("qs", NCTX),
    ("qg", NCTX),
    ("vc", NCTX),
    ("vt", 3),
) + tuple(
    (f"{kind}{layer}", count)
    for layer in range(2)
    for kind, count in (
        ("x", 3),
        ("kv", NCTX),
        ("q", 1),
        ("oa", 3),
        ("ob", 4),
        ("ow", 1),
        ("ff", 3),
        ("g", 3),
        ("doa", 3),
        ("dob", 4),
        ("dkv", NCTX),
        ("dq", 1),
        ("dx", 3),
    )
):
    SEMAPHORES[name] = COPIES
    COPIES += count


def step_kernel(*refs):
    names = INPUTS + tuple(n for n, _, _ in OUTPUTS) + tuple(n for n, _, _ in SCRATCH)
    r_ = SimpleNamespace(**dict(zip(names, refs)))
    send_sems, recv_sems, load_sems = refs[len(names) :]
    s = lax.axis_index("section")
    c = lax.axis_index("ctx")
    t = lax.axis_index("tp")
    group = c // (NCTX // 2)
    partner = NCTX - 1 - c
    core = {"section": 1 - s}

    def ring(r):
        return lax.rem(t + r, NTP)

    def copy(kind, src, dst, peer, send=0, recv=None):
        base = SEMAPHORES[kind]
        recv = send if recv is None else recv
        return remote(src, dst, send_sems.at[base + send], recv_sems.at[base + recv], peer)

    sent = []

    def start(item):
        item.start()
        sent.append(item)
        return item

    def start_all(items):
        return [start(item) for item in items]

    peers = [core]
    peers += [{"tp": ring(r)} for r in range(1, NTP)]
    peers += [{"ctx": lax.rem(c + r, NCTX)} for r in range(1, NCTX)]
    peers += [{"ctx": partner, "tp": ring(r)} for r in range(1, NTP)]
    barrier = pltpu.get_barrier_semaphore()
    for peer in peers:
        pl.semaphore_signal(barrier, inc=1, device_id=peer, device_id_type=MESH)

    loads = [
        pltpu.make_async_copy(src, dst, load_sems.at[i])
        for i, (src, dst) in enumerate(
            (
                (r_.own_watt, r_.watt.at[s]),
                (r_.own_vecs, r_.vecs.at[s]),
                (r_.own_wup, r_.wup.at[s]),
                (r_.own_wdn, r_.wdn.at[s]),
                (r_.own_wo, r_.wo.at[s, t]),
            )
        )
    ]
    for load in loads:
        load.start()
    r_.xown[0] = r_.xin[s]
    r_.gown[1] = r_.gin[s]
    pl.semaphore_wait(barrier, len(peers))

    def gather_rows(kind, own, full):
        full[t] = own[...]
        return start_all(
            [copy(kind, own, full.at[t], {"tp": ring(r)}, r - 1) for r in range(1, NTP)]
        )

    x_copies = gather_rows("x0", r_.xown.at[0], r_.xg.at[0])
    weight_copies = start_all(
        [
            copy("weights", r_.own_vecs, r_.vecs.at[s], core, 0),
            copy("weights", r_.own_watt, r_.watt.at[s], core, 1),
            copy("weights", r_.own_wup, r_.wup.at[s], core, 2),
            copy("weights", r_.own_wdn, r_.wdn.at[s], core, 3),
        ]
    )
    wo_copies = start_all(
        [copy("wo", r_.own_wo, r_.wo.at[s, t], {"tp": ring(r)}, r - 1) for r in range(1, NTP)]
    )
    g_copies = gather_rows("g1", r_.gown.at[1], r_.gg.at[1])

    def vector(layer, row, width=D):
        return r_.vecs[layer, row : row + 1, 0:width]

    def norm_outputs(layer, xhat):
        first = xhat * vector(layer, 0) + vector(layer, 2)
        second = xhat * vector(layer, 1) + vector(layer, 3)
        return first.astype(BF16), second.astype(BF16)

    def key_mask(key_block, shape, slot):
        key = key_block * BLK + lax.broadcasted_iota(jnp.int32, shape, 0)
        return (key <= r_.place[slot, 0:1, :]) & (key >= r_.place[slot, 1:2, :])

    def visit_both(key_block, visit):
        @pl.loop(0, 2)
        def _(slot):
            query_block = jnp.where(slot == 0, c, partner)
            reached = key_block <= query_block
            edge = needs_mask(key_block, query_block)

            @pl.when(reached & edge)
            def _():
                visit(key_block, slot, True)

            @pl.when(reached & jnp.logical_not(edge))
            def _():
                visit(key_block, slot, False)


    def key_send(layer, r):
        d = lax.rem(c + r, NCTX)
        return c <= top_block(d), copy(
            f"kv{layer}",
            r_.kvs.at[layer, d // (NCTX // 2)],
            r_.kvall.at[layer, c],
            {"ctx": d},
            d,
            c,
        )

    def forward(layer, gathers, before_keys, after_keys, before_out):
        def project(part):
            xhat, _ = normed(r_.xg[layer, part].astype(F32))
            attention_in, _ = norm_outputs(layer, xhat)
            pre = dot_nn(attention_in, r_.watt[layer]) + vector(layer, 6, 384)
            rows = span(part, OWN)
            cosine, sine = r_.rot[0, 0, rows, :], r_.rot[0, 1, rows, :]
            query = turn(pre[:, 0:128], cosine, sine) * 0.125
            r_.qs[layer, rows, :] = query.astype(BF16)
            r_.kvs[layer, 0, rows, :] = turn_left(pre[:, 128:256], cosine, sine).astype(BF16)
            r_.kvs[layer, 1, rows, :] = turn_left(pre[:, 256:384], cosine, sine).astype(BF16)

        before_keys()
        project(t)
        for r, item in enumerate(gathers):
            item.wait_recv()
            project(lax.rem(t + NTP - 1 - r, NTP))

        query_copy = start(copy(f"q{layer}", r_.qs.at[layer], r_.qin.at[layer], {"ctx": partner}))

        @pl.loop(1, NCTX)
        def _(r):
            wanted, item = key_send(layer, r)

            @pl.when(wanted)
            def _():
                item.start()

        r_.kvall[layer, c] = r_.kvs[layer, group]
        after_keys()

        def feed_forward(part):
            xhat, _ = normed(r_.xg[layer, part].astype(F32))
            _, feed_in = norm_outputs(layer, xhat)
            hidden = gelu(dot_nn(feed_in, r_.wup[layer]) + vector(layer, 5)).astype(BF16)
            r_.hid[layer, part] = hidden
            return dot_nn(hidden, r_.wdn[layer])

        def feed_send(r):
            return copy(
                f"ff{layer}",
                r_.ffs.at[layer, r - 1],
                r_.ffr.at[layer, r - 1],
                {"tp": ring(r)},
                r - 1,
            )

        @pl.loop(1, NTP)
        def _(r):
            r_.ffs[layer, r - 1] = feed_forward(ring(r)).astype(BF16)
            feed_send(r).start()

        feed_copies = [feed_send(r) for r in range(1, NTP)]
        sent.extend(feed_copies)
        r_.ffo[...] = feed_forward(t)

        r_.qpad[layer, 0] = my_head(r_.qs[layer].astype(F32), group, 0).astype(BF16)
        query_copy.wait_recv()
        r_.qpad[layer, 1] = my_head(r_.qin[layer].astype(F32), group, 0).astype(BF16)
        r_.acc[...] = jnp.zeros_like(r_.acc)
        r_.top[...] = jnp.full_like(r_.top, LOWEST)

        def visit(key_block, slot, masked):
            scores = dot_nt(r_.kvall[layer, key_block], r_.qpad[layer, slot])
            if masked:
                scores = jnp.where(key_mask(key_block, scores.shape, slot), scores, MASKED)
            old = r_.top[slot]
            new = jnp.maximum(old, jnp.max(scores, axis=0, keepdims=True))
            weights = jnp.exp(scores - new).astype(BF16)
            r_.top[slot] = new
            r_.acc[slot] = r_.acc[slot] * jnp.exp(old - new) + dot_nn(r_.kvt[...], weights)

        @pl.loop(0, NCTX)
        def _(r):
            key_block = lax.rem(c + NCTX - r, NCTX)

            @pl.when(key_block <= top_block(c))
            def _():
                @pl.when(r > 0)
                def _():
                    copy(
                        f"kv{layer}",
                        r_.kvs.at[layer, 0],
                        r_.kvall.at[layer, key_block],
                        {"ctx": partner},
                        0,
                        key_block,
                    ).wait_recv()

                turned = r_.kvall[layer, key_block].astype(F32).T
                row = lax.broadcasted_iota(jnp.int32, turned.shape, 0)
                r_.kvt[...] = jnp.where(row < HEAD_DIM, 1.0, turned).astype(BF16)
                visit_both(key_block, visit)

        def finish(slot):
            total = r_.acc[slot, 0:HEAD_DIM, :]
            mean = r_.acc[slot, HEAD_DIM:, :] / total
            r_.ot[layer, slot] = mean
            r_.lse[layer, slot] = r_.top[slot] + jnp.log(total[0:1])
            r_.oout[layer, slot] = two_head_tile(mean, group).astype(BF16)

        finish(1)
        far = start_all(
            [
                copy(
                    f"ob{layer}",
                    r_.oout.at[layer, 1, span(ring(r), OWN), :],
                    r_.ob.at[layer, t],
                    {"ctx": partner, "tp": ring(r)},
                    r,
                )
                for r in range(NTP)
            ]
        )
        finish(0)
        near = start_all(
            [
                copy(
                    f"oa{layer}",
                    r_.oout.at[layer, 0, span(ring(r), OWN), :],
                    r_.oa.at[layer, t],
                    {"tp": ring(r)},
                    r - 1,
                )
                for r in range(1, NTP)
            ]
        )
        r_.oa[layer, t] = r_.oout[layer, 0, span(t, OWN), :]
        start(copy(f"ow{layer}", r_.oout.at[layer, 1], r_.oin.at[layer], {"ctx": partner}))

        result = r_.xown[layer].astype(F32) + vector(layer, 4) + r_.ffo[...]
        for r, item in enumerate(feed_copies):
            item.wait_recv()
            result = result + r_.ffr[layer, r].astype(F32)
        for item in far + near:
            item.wait_recv()
        before_out()
        heads = jnp.concatenate(
            [r_.oa[layer, p] + r_.ob[layer, p] for p in range(NTP)], axis=1
        )
        result = result + dot_nn(heads, r_.wo[layer].reshape(D, D))
        r_.fo[layer] = result.astype(BF16)


    def send_attention_grads(layer):
        tile = dot_nt(r_.gown[layer], r_.wo[layer].reshape(D, D)).astype(BF16)
        for p in range(NTP):
            r_.dos[layer, p] = tile[:, p * LANES : (p + 1) * LANES]
        far = start_all(
            [
                copy(
                    f"dob{layer}",
                    r_.dos.at[layer, ring(r)],
                    r_.dob.at[layer, t],
                    {"ctx": partner, "tp": ring(r)},
                    r,
                )
                for r in range(NTP)
            ]
        )
        near = start_all(
            [
                copy(
                    f"doa{layer}",
                    r_.dos.at[layer, ring(r)],
                    r_.doa.at[layer, t],
                    {"tp": ring(r)},
                    r - 1,
                )
                for r in range(1, NTP)
            ]
        )
        r_.doa[layer, t] = r_.dos[layer, t]
        return near + far

    def key_grad_send(layer, key_block):
        return copy(
            f"dkv{layer}",
            r_.dkvo.at[layer, key_block],
            r_.dkvi.at[layer, c],
            {"ctx": key_block},
            key_block,
            c,
        )

    def backward(layer, grad_copies, gathers, beside, after_feed):
        for item in grad_copies:
            item.wait_recv()

        def prepare(slot, tile):
            padded = my_head(tile.reshape(BLK, LANES).astype(F32), group, 1)
            r_.dopad[slot] = padded.astype(BF16)
            r_.delta[slot] = jnp.sum(
                padded.T[HEAD_DIM:, :] * r_.ot[layer, slot], axis=0, keepdims=True
            )

        prepare(0, r_.doa[layer])
        prepare(1, r_.dob[layer])
        r_.dqt[...] = jnp.zeros_like(r_.dqt)

        def visit(key_block, slot, masked):
            keys = r_.kvall[layer, key_block]
            queries, grads = r_.qpad[layer, slot], r_.dopad[slot]
            scores = dot_nt(keys, queries)
            weights = jnp.exp(scores - r_.lse[layer, slot])
            if masked:
                weights = jnp.where(key_mask(key_block, scores.shape, slot), weights, 0.0)
            weight_grad = dot_nt(keys, grads)
            score_grad = (weights * (weight_grad - r_.delta[slot])).astype(BF16)
            r_.dkva[...] += dot_nn(weights.astype(BF16), grads) + dot_nn(score_grad, queries)
            r_.dqt[slot] += dot_nn(r_.kvt[...], score_grad)

        @pl.loop(1, NCTX + 1)
        def _(r):
            key_block = lax.rem(c + r, NCTX)

            @pl.when(key_block <= top_block(c))
            def _():
                r_.kvt[...] = r_.kvall[layer, key_block].astype(F32).T.astype(BF16)
                r_.dkva[...] = jnp.zeros_like(r_.dkva)
                visit_both(key_block, visit)
                r_.dkvo[layer, key_block] = r_.dkva[...].astype(BF16)

                @pl.when(r < NCTX)
                def _():
                    key_grad_send(layer, key_block).start()

        def query_grad(slot):
            tile = two_head_tile(r_.dqt[slot, 0:HEAD_DIM, :] * 0.125, group)
            return turn(tile, r_.rot[slot, 0], -r_.rot[slot, 1]).astype(BF16)

        r_.dqs[layer] = query_grad(1)
        query_copy = start(copy(f"dq{layer}", r_.dqs.at[layer], r_.dqi.at[layer], {"ctx": partner}))
        r_.dproj[:, 0:128] = query_grad(0)

        for item in gathers:
            item.wait_recv()
        r_.gv[layer] = jnp.zeros((8, D), F32)
        own_sum = jnp.sum(r_.gown[layer].astype(F32), axis=0, keepdims=True)
        r_.gv[layer, 4:5, :] = own_sum

        def add_vector(row, value):
            r_.gv[layer, row : row + 1, :] += jnp.sum(value, axis=0, keepdims=True)

        @pl.loop(0, NTP)
        def _(part):
            xhat, _ = normed(r_.xg[layer, part].astype(F32))
            attention_in, feed_in = norm_outputs(layer, xhat)
            r_.ain[part] = attention_in
            r_.fin[part] = feed_in
            up_pre = dot_nn(feed_in, r_.wup[layer]) + vector(layer, 5)
            hidden_grad = dot_nt(r_.gg[layer, part], r_.wdn[layer])
            up_grad = (hidden_grad * gelu_slope(up_pre)).astype(BF16)
            r_.ugs[part] = up_grad
            add_vector(5, up_grad.astype(F32))
            feed_grad = dot_nt(up_grad, r_.wup[layer])
            add_vector(1, xhat * feed_grad)
            add_vector(3, feed_grad)
            r_.dxh[part] = feed_grad * vector(layer, 1)

        full_grad = r_.gg[layer].reshape(BLK, D)
        up_terms = dot_tn(r_.fin[...].reshape(BLK, D), r_.ugs[...].reshape(BLK, D))
        r_.gwp[layer, 0:D, :] = up_terms.astype(BF16)
        r_.gwp[layer, D:, :] = dot_tn(r_.hid[layer].reshape(BLK, D), full_grad).astype(BF16)
        after_feed()
        out_copy = copy(f"ow{layer}", r_.oout.at[layer, 1], r_.oin.at[layer], {"ctx": partner})
        out_copy.wait_recv()
        attention = r_.oout[layer, 0] + r_.oin[layer]
        r_.gwq[layer, 0:128, :] = dot_tn(attention, full_grad).astype(BF16)
        beside()

        def key_grad(half):
            r_.dkva[...] = jnp.zeros_like(r_.dkva)

            @pl.loop(0, NCTX // 2)
            def _(step):
                source = half * (NCTX // 2) + step

                @pl.when(source == c)
                def _():
                    r_.dkva[...] += r_.dkvo[layer, c].astype(F32)

                @pl.when((c <= top_block(source)) & (source != c))
                def _():
                    copy(
                        f"dkv{layer}",
                        r_.dkvo.at[layer, 0],
                        r_.dkvi.at[layer, source],
                        {"ctx": partner},
                        0,
                        source,
                    ).wait_recv()
                    r_.dkva[...] += r_.dkvi[layer, source].astype(F32)

            return turn_left(r_.dkva[...], r_.rot[0, 0], -r_.rot[0, 1]).astype(BF16)

        r_.dproj[:, 128:256] = key_grad(0)
        r_.dproj[:, 256:384] = key_grad(1)
        query_copy.wait_recv()
        r_.dproj[:, 0:128] += r_.dqi[layer]

        def input_part(part):
            xhat, _ = normed(r_.xg[layer, part].astype(F32))
            grad = dot_nt(r_.dproj[span(part, OWN), :], r_.watt[layer])
            add_vector(0, xhat * grad)
            add_vector(2, grad)
            return r_.dxh[part] + grad * vector(layer, 0)

        scatters = []
        for r in range(1, NTP):
            r_.dxs[layer, r - 1] = input_part(ring(r)).astype(BF16)
            item = copy(
                f"dx{layer}",
                r_.dxs.at[layer, r - 1],
                r_.dxr.at[layer, r - 1],
                {"tp": ring(r)},
                r - 1,
            )
            scatters.append(start(item))
        total = input_part(t)
        bias_sum = jnp.sum(r_.dproj[...].astype(F32), axis=0, keepdims=True)
        r_.gv[layer, 6:7, 0:384] = bias_sum
        terms = dot_tn(r_.dproj[...], r_.ain[...].reshape(BLK, D))
        r_.gwq[layer, 128:, :] = terms.astype(BF16)
        for r, item in enumerate(scatters):
            item.wait_recv()
            total = total + r_.dxr[layer, r].astype(F32)
        xhat, inverse = normed(r_.xown[layer].astype(F32))
        along = jnp.mean(total * xhat, axis=-1, keepdims=True)
        centred = total - jnp.mean(total, axis=-1, keepdims=True) - xhat * along
        r_.go[layer] = (r_.gown[layer].astype(F32) + centred * inverse).astype(BF16)


    def cross_copy(which, layer):
        src = (r_.gwp, r_.gwq, r_.gv)[which].at[layer]
        return copy("cross", src, (r_.crp, r_.crq, r_.crv)[which], core, which)

    def cross_start(which, layer):
        @pl.when(s != layer)
        def _():
            cross_copy(which, layer).start()

    wide_parts = (
        (r_.gwp, r_.crp, r_.sump, r_.inp, r_.minep, r_.gatp, "ps", "pg", 64),
        (r_.gwq, r_.crq, r_.sumq, r_.inq, r_.mineq, r_.gatq, "qs", "qg", 32),
    )

    def scatter_copy(which, r):
        _, _, sums, arrived, _, _, kind, _, _ = wide_parts[which]
        d = lax.rem(c + r, NCTX)
        return copy(kind, sums.at[d], arrived.at[r], {"ctx": d}, r)

    def gather_copy(which, r):
        _, _, _, _, mine, full, _, kind, _ = wide_parts[which]
        return copy(kind, mine, full.at[c], {"ctx": lax.rem(c + r, NCTX)}, r)

    def scatter_terms(which, layer):
        terms, crossed, sums, _, _, _, _, _, chunk = wide_parts[which]

        @pl.when(s == layer)
        def _():
            cross_copy(which, layer).wait_recv()

            @pl.loop(0, NCTX)
            def _(j):
                rows = span(j, chunk)
                pair = terms[layer, rows, :].astype(F32) + crossed[rows, :].astype(F32)
                sums[j] = pair.astype(BF16)

            @pl.loop(1, NCTX)
            def _(r):
                scatter_copy(which, r).start()

    def store_chunk(which, j, value):
        chunk = wide_parts[which][-1]
        target = (r_.out_ff, r_.allq)[which]
        target[span(j, chunk), :] = value

    def gather_sums(which, layer):
        _, _, sums, arrived, mine, _, _, _, _ = wide_parts[which]

        @pl.when(s == layer)
        def _():
            total = sums[c].astype(F32)
            for r in range(1, NCTX):
                scatter_copy(which, r).wait_recv()
                total = total + arrived[r].astype(F32)
            mine[...] = total.astype(BF16)

            @pl.loop(1, NCTX)
            def _(r):
                gather_copy(which, r).start()

            store_chunk(which, c, total)

    def store_sums(which, layer):
        _, _, _, _, mine, full, _, kind, _ = wide_parts[which]

        @pl.when(s == layer)
        def _():
            @pl.loop(1, NCTX)
            def _(r):
                source = lax.rem(c + NCTX - r, NCTX)
                copy(kind, mine, full.at[source], core, r).wait_recv()
                store_chunk(which, source, full[source].astype(F32))

    def vector_copy(r):
        return copy("vc", r_.vec, r_.vec_in.at[r], {"ctx": lax.rem(c + r, NCTX)}, r)

    def vector_tp_copy(r):
        return copy("vt", r_.vec_tp, r_.vec_tp_in.at[r - 1], {"tp": ring(r)}, r - 1)

    def vector_first(layer):
        @pl.when(s == layer)
        def _():
            cross_copy(2, layer).wait_recv()
            r_.vec[...] = r_.gv[layer] + r_.crv[...]

            @pl.loop(1, NCTX)
            def _(r):
                vector_copy(r).start()

    def vector_second(layer):
        @pl.when(s == layer)
        def _():
            total = r_.vec[...]
            for r in range(1, NCTX):
                vector_copy(r).wait_recv()
                total = total + r_.vec_in[r]
            r_.vec_tp[...] = total
            for r in range(1, NTP):
                vector_tp_copy(r).start()

    def vector_last(layer):
        @pl.when(s == layer)
        def _():
            total = r_.vec_tp[...]
            shared = total
            for r in range(1, NTP):
                vector_tp_copy(r).wait_recv()
                shared = shared + r_.vec_tp_in[r - 1]
            row = lax.broadcasted_iota(jnp.int32, shared.shape, 0)
            r_.out_small[...] = jnp.where(row < 5, shared, total)

    def store_attention():
        r_.out_wo[...] = r_.allq[0:128, :]
        turned = r_.allq[128:, :].T
        first, second = turned[:, 128:256], turned[:, 256:384]
        left = lanes(first.shape) < HEAD_DIM
        r_.out_att[0] = turned[:, 0:128]
        r_.out_att[1] = jnp.where(left, first, pltpu.roll(second, HEAD_DIM, 1))
        r_.out_att[2] = jnp.where(left, pltpu.roll(first, HEAD_DIM, 1), second)


    def nothing():
        pass

    def wait_first_weights():
        for load in loads:
            load.wait()
        weight_copies[0].wait_recv()
        weight_copies[1].wait_recv()

    def wait_other_weights():
        weight_copies[2].wait_recv()
        weight_copies[3].wait_recv()
        for item in wo_copies:
            item.wait_recv()
        start(wo_pass)

    wo_pass = copy("wo_pass", r_.wo.at[s], r_.wo.at[s], core)
    forward(0, x_copies, wait_first_weights, wait_other_weights, wo_pass.wait_recv)
    r_.xown[1] = r_.fo[0]
    x_copies = gather_rows("x1", r_.xown.at[1], r_.xg.at[1])
    grad_copies = send_attention_grads(1)
    forward(1, x_copies, nothing, nothing, nothing)

    rows_copy = start(copy("rows", r_.fo.at[1 - s], r_.out_rows.at[s], core))
    r_.out_rows[s] = r_.fo[s]

    backward(1, grad_copies, g_copies, nothing, lambda: cross_start(0, 1))
    r_.gown[0] = r_.go[1]
    g_copies = gather_rows("g0", r_.gown.at[0], r_.gg.at[0])
    grad_copies = send_attention_grads(0)
    cross_start(1, 1)
    cross_start(2, 1)
    scatter_terms(0, 1)

    def beside_last():
        scatter_terms(1, 1)
        vector_first(1)
        gather_sums(0, 1)
        scatter_terms(0, 0)

    backward(0, grad_copies, g_copies, beside_last, lambda: cross_start(0, 0))
    cross_start(1, 0)
    cross_start(2, 0)
    grads_copy = start(copy("grads", r_.go.at[1 - s], r_.out_grads.at[s], core))
    r_.out_grads[s] = r_.go[s]
    scatter_terms(1, 0)
    vector_first(0)
    gather_sums(0, 0)
    gather_sums(1, 1)
    vector_second(1)
    vector_second(0)
    gather_sums(1, 0)
    for layer in (1, 0):
        store_sums(0, layer)
        vector_last(layer)
        store_sums(1, layer)
    store_attention()
    rows_copy.wait_recv()
    grads_copy.wait_recv()


    for item in sent:
        item.wait_send()
    for layer in range(2):

        @pl.loop(1, NCTX)
        def _(r):
            wanted, item = key_send(layer, r)

            @pl.when(wanted)
            def _():
                item.wait_send()

            key_block = lax.rem(c + r, NCTX)

            @pl.when(key_block <= top_block(c))
            def _():
                key_grad_send(layer, key_block).wait_send()

        @pl.when(s != layer)
        def _():
            for which in range(3):
                cross_copy(which, layer).wait_send()

    @pl.loop(1, NCTX)
    def _(r):
        for which in range(2):
            scatter_copy(which, r).wait_send()
            gather_copy(which, r).wait_send()
        vector_copy(r).wait_send()

    for r in range(1, NTP):
        vector_tp_copy(r).wait_send()


def run_step(operands):
    vmem = pl.BlockSpec(memory_space=pltpu.VMEM)
    anywhere = pl.BlockSpec(memory_space=pl.ANY)
    dma = pltpu.SemaphoreType.DMA
    return pl.pallas_call(
        step_kernel,
        out_shape=[jax.ShapeDtypeStruct(shape, kind) for _, shape, kind in OUTPUTS],
        in_specs=[anywhere if name.startswith("own_") else vmem for name in INPUTS],
        out_specs=[vmem] * len(OUTPUTS),
        scratch_shapes=[pltpu.VMEM(shape, kind) for _, shape, kind in SCRATCH]
        + [dma((COPIES,)), dma((COPIES,)), dma((5,))],
        compiler_params=pltpu.CompilerParams(
            collective_id=0, has_side_effects=True, vmem_limit_bytes=VMEM_LIMIT
        ),
        name="train_step",
    )(*operands)


def sequence_starts(lengths, positions):
    ends = jnp.cumsum(lengths).astype(jnp.int32)
    before = jnp.where(ends[None, :] <= positions[:, None], lengths[None, :], 0)
    return jnp.sum(before, axis=1).astype(jnp.int32)


def rotary_lanes(offsets):
    rates = 1.0 / 10000.0 ** (jnp.arange(0, ROT, 2).astype(F32) / ROT)
    rest = jnp.zeros((HEAD_DIM - ROT,), F32)
    rates = jnp.concatenate([rates, rates, rest] * 2)
    signs = jnp.where(jnp.arange(LANES) % HEAD_DIM < ROT // 2, -1.0, 1.0)
    angles = offsets.astype(F32)[..., None] * rates
    return jnp.stack([jnp.cos(angles), jnp.sin(angles) * signs], axis=1)


def pack_attention(items):
    q, k, v = items
    half = HEAD_DIM
    return jnp.concatenate([q, k[:, :half], v[:, :half], k[:, half:], v[:, half:]], axis=1)


def local(
    block_input,
    output_grad,
    sequence_lengths,
    norm_gain,
    norm_bias,
    attention_weight,
    attention_bias,
    output_weight,
    up_weight,
    up_bias,
    down_weight,
    branch_bias,
):
    s = lax.axis_index("section")
    c = lax.axis_index("ctx")
    packed_bias = pack_attention([attention_bias[:, k] for k in range(3)])
    vectors = jnp.concatenate(
        [
            norm_gain[0],
            norm_bias[0],
            branch_bias,
            up_bias,
            jnp.pad(packed_bias, ((0, 0), (0, D - 384))),
            jnp.zeros((1, D), F32),
        ]
    )
    lengths = jnp.where(s == 0, sequence_lengths[0], sequence_lengths[1])
    steps = jnp.arange(BLK, dtype=jnp.int32)
    positions = jnp.stack([c * BLK + steps, (NCTX - 1 - c) * BLK + steps])
    starts = sequence_starts(lengths, positions.reshape(-1)).reshape(2, BLK)
    rows, grads, ff, wo, att, small = run_step(
        (
            block_input,
            output_grad,
            pack_attention([attention_weight[0, k] for k in range(3)]),
            output_weight[0],
            up_weight[0],
            down_weight[0],
            vectors,
            rotary_lanes(positions - starts),
            jnp.stack([positions, starts], axis=1),
        )
    )
    half = HEAD_DIM
    bias = small[6, 0:384]
    bias_parts = jnp.stack(
        [
            bias[0:128],
            jnp.concatenate([bias[128 : 128 + half], bias[256 : 256 + half]]),
            jnp.concatenate([bias[128 + half : 256], bias[256 + half :]]),
        ]
    )
    return (
        rows[None],
        grads[None],
        small[None, 0:2],
        small[None, 2:4],
        att[None],
        bias_parts[None],
        wo[None],
        ff[None, 0:D],
        small[5:6],
        ff[None, D:],
        small[4:5],
    )


def solution(mesh):
    placed = (
        P(None, ("ctx", "tp"), None),
        P(None, ("ctx", "tp"), None),
        P(),
        P("section", None, None),
        P("section", None, None),
        P("section", None, None, "tp"),
        P("section", None, "tp"),
        P("section", "tp", None),
        P("section", None, "tp"),
        P("section", "tp"),
        P("section", "tp", None),
        P("section", None),
    )
    return jax.shard_map(
        local,
        mesh=mesh,
        in_specs=placed,
        out_specs=(
            P("section", None, ("ctx", "tp"), None),
            P("section", None, ("ctx", "tp"), None),
            P("section", None, None),
            P("section", None, None),
            P("section", None, None, "tp"),
            P("section", None, "tp"),
            P("section", "tp", None),
            P("section", None, "tp"),
            P("section", "tp"),
            P("section", "tp", None),
            P("section", None),
        ),
        check_vma=False,
    )
```

```python
from types import SimpleNamespace

import jax
import jax.numpy as jnp
from jax import lax
from jax.experimental import pallas as pl
from jax.experimental.pallas import tpu as pltpu
from jax.sharding import PartitionSpec as P

HEAD_DIM = 64
ROT = 16
MESH = pl.DeviceIdType.MESH
F32 = jnp.float32
BF16 = jnp.bfloat16
VMEM_LIMIT = 56 * 1024 * 1024
NCTX = 16
NTP = 4
BLK = 512
OWN = 128
D = 512
LANES = 128
STEPS = (
    (0, 1), (1, 0), (0, 3), (3, 0), (1, 1), (3, 3), (1, 3), (3, 1),
    (0, 2), (2, 0), (1, 2), (3, 2), (2, 1), (2, 3), (2, 2),
)
AHEAD = 5
MASKED = -1e30
LOWEST = -1e29


def dot_nn(a, b):
    return lax.dot_general(a, b, (((1,), (0,)), ((), ())), preferred_element_type=F32)


def dot_nt(a, b):
    return lax.dot_general(a, b, (((1,), (1,)), ((), ())), preferred_element_type=F32)


def dot_tn(a, b):
    return lax.dot_general(a, b, (((0,), (0,)), ((), ())), preferred_element_type=F32)


def phi(v):
    return 0.5 * (1.0 + lax.erf(v * (0.5**0.5)))


def gelu(v):
    return v * phi(v)


def gelu_slope(v):
    return phi(v) + v * jnp.exp(-0.5 * v * v) * 0.3989422804014327


def normed(rows):
    centre = rows - jnp.mean(rows, axis=-1, keepdims=True)
    spread = jnp.mean(centre * centre, axis=-1, keepdims=True)
    inverse = lax.rsqrt(spread + 1e-05)
    return centre * inverse, inverse


def remote(src, dst, send, recv, peer):
    return pltpu.make_async_remote_copy(
        src_ref=src, dst_ref=dst, send_sem=send, recv_sem=recv, device_id=peer, device_id_type=MESH
    )


def lanes(shape):
    return lax.broadcasted_iota(jnp.int32, shape, 1)


def turn(tile, cosine, sine):
    back = pltpu.roll(tile, LANES - 8, 1)
    ahead = pltpu.roll(tile, 8, 1)
    other = jnp.where(lanes(tile.shape) % HEAD_DIM < 8, back, ahead)
    return tile * cosine + other * sine


def turn_left(tile, cosine, sine):
    return jnp.where(lanes(tile.shape) < HEAD_DIM, turn(tile, cosine, sine), tile)


def my_head(tile, group, half):
    swapped = pltpu.roll(tile, HEAD_DIM, 1)
    chosen = jnp.where(group == half, tile, swapped)
    return jnp.where(lanes(tile.shape) // HEAD_DIM == half, chosen, 0.0)


def two_head_tile(rows, group):
    blank = jnp.zeros_like(rows)
    first = jnp.where(group == 0, rows, blank)
    second = jnp.where(group == 0, blank, rows)
    return jnp.concatenate([first, second], axis=0).T


def top_block(d):
    return jnp.maximum(d, NCTX - 1 - d)


def needs_mask(key_block, query_block):
    return (key_block == 0) | (key_block == query_block) | (query_block == NCTX - 1)


def wrap(index, count):
    return jnp.where(index >= count, index - count, index)


def stepped(c, index, sign):
    z, y = c // 4, c % 4
    dz, dy = 0, 0
    for k, (along_z, along_y) in enumerate(STEPS):
        dz = jnp.where(index == k, along_z, dz)
        dy = jnp.where(index == k, along_y, dy)
    return wrap(z + (dz if sign > 0 else 4 - dz), 4) * 4 + wrap(y + (dy if sign > 0 else 4 - dy), 4)


def second_group(d):
    return jnp.where(d >= NCTX // 2, 1, 0)


def span(index, size):
    return pl.ds(pl.multiple_of(index * size, size), size)


OUTPUTS = (
    ("out_rows", (1, 2, OWN, D), BF16),
    ("out_grads", (1, 2, OWN, D), BF16),
    ("out_gain", (1, 2, D), F32),
    ("out_norm_bias", (1, 2, D), F32),
    ("out_att", (1, 3, D, OWN), F32),
    ("out_att_bias", (1, 3, OWN), F32),
    ("out_wo", (1, OWN, D), F32),
    ("out_up", (1, D, D), F32),
    ("out_up_bias", (1, D), F32),
    ("out_dn", (1, D, D), F32),
    ("out_branch", (1, D), F32),
)

SCRATCH = (
    ("watt", (2, D, 384), BF16),
    ("wo", (2, NTP, OWN, D), BF16),
    ("wup", (2, D, D), BF16),
    ("wdn", (2, D, D), BF16),
    ("vecs", (2, 8, D), F32),
    ("vown", (8, D), F32),
    ("place", (2, 2, BLK), jnp.int32),
    ("cosine", (2, BLK, LANES), F32),
    ("sine", (2, BLK, LANES), F32),
    ("xown", (2, OWN, D), BF16),
    ("fo", (2, OWN, D), BF16),
    ("xg", (2, NTP, OWN, D), BF16),
    ("qpad", (2, 2, BLK, LANES), BF16),
    ("kvall", (2, NCTX, BLK, LANES), BF16),
    ("ot", (2, 2, HEAD_DIM, BLK), F32),
    ("lse", (2, 2, 1, BLK), F32),
    ("hid", (2, NTP, OWN, D), BF16),
    ("kvs", (2, 2, BLK, LANES), BF16),
    ("qs", (2, BLK, LANES), BF16),
    ("qin", (2, BLK, LANES), BF16),
    ("oout", (2, 2, BLK, LANES), BF16),
    ("oin", (2, BLK, LANES), BF16),
    ("oa", (2, NTP, OWN, LANES), BF16),
    ("ob", (2, NTP, OWN, LANES), BF16),
    ("ffs", (2, NTP - 1, OWN, D), BF16),
    ("ffr", (2, NTP - 1, OWN, D), BF16),
    ("gown", (2, OWN, D), BF16),
    ("go", (2, OWN, D), BF16),
    ("gg", (2, NTP, OWN, D), BF16),
    ("dos", (2, NTP, OWN, LANES), BF16),
    ("doa", (2, NTP, OWN, LANES), BF16),
    ("dob", (2, NTP, OWN, LANES), BF16),
    ("dkvo", (2, NCTX, BLK, LANES), BF16),
    ("dkvi", (2, NCTX, BLK, LANES), BF16),
    ("dqs", (2, BLK, LANES), BF16),
    ("dqi", (2, BLK, LANES), BF16),
    ("dxs", (2, NTP - 1, OWN, D), BF16),
    ("dxr", (2, NTP - 1, OWN, D), BF16),
    ("gwp", (2, 2 * D, D), BF16),
    ("gwq", (2, D, D), BF16),
    ("gv", (2, 8, D), F32),
    ("kvt", (LANES, BLK), BF16),
    ("acc", (2, LANES, BLK), F32),
    ("top", (2, 1, BLK), F32),
    ("ffo", (OWN, D), F32),
    ("dopad", (2, BLK, LANES), BF16),
    ("delta", (2, 1, BLK), F32),
    ("dqt", (2, LANES, BLK), F32),
    ("dkva", (BLK, LANES), F32),
    ("ain", (NTP, OWN, D), BF16),
    ("fin", (NTP, OWN, D), BF16),
    ("ugs", (NTP, OWN, D), BF16),
    ("dxh", (NTP, OWN, D), F32),
    ("dproj", (BLK, 384), BF16),
    ("crp", (2 * D, D), BF16),
    ("crq", (D, D), BF16),
    ("crv", (8, D), F32),
    ("sump", (NCTX, 64, D), BF16),
    ("sumq", (NCTX, 32, D), BF16),
    ("inp", (NCTX, 64, D), BF16),
    ("inq", (NCTX, 32, D), BF16),
    ("minep", (64, D), BF16),
    ("mineq", (32, D), BF16),
    ("gatp", (NCTX, 64, D), BF16),
    ("gatq", (NCTX, 32, D), BF16),
    ("allq", (D, D), F32),
    ("vec", (8, D), F32),
    ("vec_in", (NCTX, 8, D), F32),
    ("vec_tp", (8, D), F32),
    ("vec_tp_in", (NTP - 1, 8, D), F32),
)

INPUTS = (
    ("xin", pltpu.VMEM),
    ("gin", pltpu.VMEM),
    ("lengths", pltpu.SMEM),
    ("gains", pltpu.VMEM),
    ("biases", pltpu.VMEM),
    ("own_watt", pl.ANY),
    ("att_bias", pltpu.VMEM),
    ("own_wo", pl.ANY),
    ("own_wup", pl.ANY),
    ("up_bias", pltpu.VMEM),
    ("own_wdn", pl.ANY),
    ("branch_bias", pltpu.VMEM),
)

SEMAPHORES = {}
COPIES = 0
for name, count in (
    ("weights", 6),
    ("wo", 3),
    ("wo_pass", 1),
    ("rows", 1),
    ("grads", 1),
    ("cross", 3),
    ("ps", NCTX),
    ("pg", NCTX),
    ("qs", NCTX),
    ("qg", NCTX),
    ("vc", NCTX),
    ("vt", 3),
) + tuple(
    (f"{kind}{layer}", count)
    for layer in range(2)
    for kind, count in (
        ("x", 3),
        ("kv", NCTX),
        ("q", 1),
        ("oa", 3),
        ("ob", 4),
        ("ow", 1),
        ("ff", 3),
        ("g", 3),
        ("doa", 3),
        ("dob", 4),
        ("dkv", NCTX),
        ("dq", 1),
        ("dx", 3),
    )
):
    SEMAPHORES[name] = COPIES
    COPIES += count


def step_kernel(*refs):
    names = tuple(n for n, _ in INPUTS) + tuple(n for n, _, _ in OUTPUTS) + tuple(n for n, _, _ in SCRATCH)
    r_ = SimpleNamespace(**dict(zip(names, refs)))
    send_sems, recv_sems, load_sems = refs[len(names) :]
    s = lax.axis_index("section")
    c = lax.axis_index("ctx")
    t = lax.axis_index("tp")
    group = second_group(c)
    partner = NCTX - 1 - c
    core = {"section": 1 - s, "ctx": c, "tp": t}

    def at_ctx(d):
        return {"section": s, "ctx": d, "tp": t}

    def at_tp(d):
        return {"section": s, "ctx": c, "tp": d}

    def at_partner(d):
        return {"section": s, "ctx": partner, "tp": d}

    def ring(r):
        return wrap(t + r, NTP)

    def copy(kind, src, dst, peer, send=0, recv=None):
        base = SEMAPHORES[kind]
        recv = send if recv is None else recv
        return remote(src, dst, send_sems.at[base + send], recv_sems.at[base + recv], peer)

    sent = []

    def start(item):
        item.start()
        sent.append(item)
        return item

    def start_all(items):
        return [start(item) for item in items]

    peers = [core]
    peers += [at_tp(ring(r)) for r in range(1, NTP)]
    peers += [at_ctx(wrap(c + r, NCTX)) for r in range(1, NCTX)]
    peers += [at_partner(ring(r)) for r in range(1, NTP)]
    barrier = pltpu.get_barrier_semaphore()
    for peer in peers:
        pl.semaphore_signal(barrier, inc=1, device_id=peer, device_id_type=MESH)

    own_weights = [
        (r_.own_watt.at[0, k], r_.watt.at[s, :, k * LANES : (k + 1) * LANES]) for k in range(3)
    ]
    own_weights += [(r_.own_wup.at[0], r_.wup.at[s]), (r_.own_wdn.at[0], r_.wdn.at[s])]
    loads = [
        pltpu.make_async_copy(src, dst, load_sems.at[i])
        for i, (src, dst) in enumerate(own_weights + [(r_.own_wo.at[0], r_.wo.at[s, t])])
    ]
    for load in loads:
        load.start()
    r_.vown[...] = jnp.zeros((8, D), F32)
    r_.vown[0:2, :] = r_.gains[0]
    r_.vown[2:4, :] = r_.biases[0]
    r_.vown[4:5, :] = r_.branch_bias[...]
    r_.vown[5:6, :] = r_.up_bias[...]
    for k in range(3):
        r_.vown[6:7, k * LANES : (k + 1) * LANES] = r_.att_bias[0, k : k + 1, :]
    r_.vecs[s] = r_.vown[...]
    rate_row = lax.broadcasted_iota(jnp.int32, (ROT // 2, 1), 0)
    rates = jnp.zeros((ROT // 2, 1), F32)
    for i in range(ROT // 2):
        rates = jnp.where(rate_row == i, 1.0 / 10000.0 ** (2 * i / ROT), rates)
    for slot, block in ((0, c), (1, partner)):
        place = block * BLK + lanes((1, BLK))
        first = jnp.zeros((1, BLK), jnp.int32)
        end = 0
        for k in range(r_.lengths.shape[1]):
            length = jnp.where(s == 0, r_.lengths[0, k], r_.lengths[1, k])
            end = end + length
            first = first + jnp.where(place >= end, length, 0)
        r_.place[slot, 0:1, :] = place
        r_.place[slot, 1:2, :] = first
        angles = (place - first).astype(F32) * rates
        cosine, sine = jnp.cos(angles), jnp.sin(angles)
        still = jnp.zeros((HEAD_DIM - ROT, BLK), F32)
        cosine = jnp.concatenate([cosine, cosine, still + 1.0], axis=0)
        sine = jnp.concatenate([-sine, sine, still], axis=0)
        r_.cosine[slot] = jnp.concatenate([cosine, cosine], axis=0).T
        r_.sine[slot] = jnp.concatenate([sine, sine], axis=0).T
    r_.xown[0] = r_.xin[s]
    r_.gown[1] = r_.gin[s]
    pl.semaphore_wait(barrier, len(peers))

    def gather_rows(kind, own, full):
        full[t] = own[...]
        return start_all(
            [copy(kind, own, full.at[t], at_tp(ring(r)), r - 1) for r in range(1, NTP)]
        )

    x_copies = gather_rows("x0", r_.xown.at[0], r_.xg.at[0])
    weight_copies = start_all(
        [
            copy("weights", src, dst, core, i)
            for i, (src, dst) in enumerate([(r_.vown, r_.vecs.at[s])] + own_weights)
        ]
    )

    def vector(layer, row, width=D):
        return r_.vecs[layer, row : row + 1, 0:width]

    def norm_outputs(layer, xhat):
        first = xhat * vector(layer, 0) + vector(layer, 2)
        second = xhat * vector(layer, 1) + vector(layer, 3)
        return first.astype(BF16), second.astype(BF16)

    def key_mask(key_block, shape, slot):
        key = key_block * BLK + lax.broadcasted_iota(jnp.int32, shape, 0)
        return (key <= r_.place[slot, 0:1, :]) & (key >= r_.place[slot, 1:2, :])

    def visit_both(key_block, visit):
        @pl.loop(0, 2)
        def _(slot):
            query_block = jnp.where(slot == 0, c, partner)
            reached = key_block <= query_block
            edge = needs_mask(key_block, query_block)

            @pl.when(reached & edge)
            def _():
                visit(key_block, slot, True)

            @pl.when(reached & jnp.logical_not(edge))
            def _():
                visit(key_block, slot, False)


    def key_send(layer, index, part=None):
        d = stepped(c, index, 1)
        rows = pl.ds(0, BLK) if part is None else span(part, OWN)
        return c <= top_block(d), copy(
            f"kv{layer}",
            r_.kvs.at[layer, second_group(d), rows, :],
            r_.kvall.at[layer, c, rows, :],
            at_ctx(d),
            d,
            c,
        )

    def forward(layer, gathers, before_keys, after_keys, beside_keys, before_out):
        def project(part):
            xhat, _ = normed(r_.xg[layer, part].astype(F32))
            attention_in, _ = norm_outputs(layer, xhat)
            pre = dot_nn(attention_in, r_.watt[layer]) + vector(layer, 6, 384)
            rows = span(part, OWN)
            cosine, sine = r_.cosine[0, rows, :], r_.sine[0, rows, :]
            query = turn(pre[:, 0:128], cosine, sine) * 0.125
            r_.qs[layer, rows, :] = query.astype(BF16)
            key, value = turn(pre[:, 128:256], cosine, sine), pre[:, 256:384]
            left = lanes(key.shape) < HEAD_DIM
            first = jnp.where(left, key, pltpu.roll(value, HEAD_DIM, 1))
            second = jnp.where(left, pltpu.roll(key, HEAD_DIM, 1), value)
            r_.kvs[layer, 0, rows, :] = first.astype(BF16)
            r_.kvs[layer, 1, rows, :] = second.astype(BF16)

            copy(
                f"q{layer}",
                r_.qs.at[layer, rows, :],
                r_.qin.at[layer, rows, :],
                at_ctx(partner),
            ).start()

            @pl.loop(0, AHEAD)
            def _(index):
                send_keys(index, part)

        def send_keys(index, part=None):
            wanted, item = key_send(layer, index, part)

            @pl.when(wanted)
            def _():
                item.start()

        before_keys()
        project(t)
        for r, item in enumerate(gathers):
            item.wait_recv()
            project(wrap(t + NTP - 1 - r, NTP))

        query_copy = copy(f"q{layer}", r_.qs.at[layer], r_.qin.at[layer], at_ctx(partner))
        sent.append(query_copy)

        r_.kvall[layer, c] = r_.kvs[layer, group]
        after_keys()

        def feed_forward(part):
            xhat, _ = normed(r_.xg[layer, part].astype(F32))
            _, feed_in = norm_outputs(layer, xhat)
            hidden = gelu(dot_nn(feed_in, r_.wup[layer]) + vector(layer, 5)).astype(BF16)
            r_.hid[layer, part] = hidden
            return dot_nn(hidden, r_.wdn[layer])

        def feed_send(r):
            return copy(
                f"ff{layer}",
                r_.ffs.at[layer, r - 1],
                r_.ffr.at[layer, r - 1],
                at_tp(ring(r)),
                r - 1,
            )

        feed_copies = [feed_send(r) for r in range(1, NTP)]
        sent.extend(feed_copies)

        def feed_all():
            @pl.loop(1, NTP)
            def _(r):
                r_.ffs[layer, r - 1] = feed_forward(ring(r)).astype(BF16)
                feed_send(r).start()

            r_.ffo[...] = feed_forward(t)

        r_.qpad[layer, 0] = my_head(r_.qs[layer].astype(F32), group, 0).astype(BF16)
        query_copy.wait_recv()
        r_.qpad[layer, 1] = my_head(r_.qin[layer].astype(F32), group, 0).astype(BF16)
        r_.acc[...] = jnp.zeros_like(r_.acc)
        r_.top[...] = jnp.full_like(r_.top, LOWEST)

        def visit(key_block, slot, masked):
            scores = dot_nt(r_.kvall[layer, key_block], r_.qpad[layer, slot])
            if masked:
                scores = jnp.where(key_mask(key_block, scores.shape, slot), scores, MASKED)
            old = r_.top[slot]
            new = jnp.maximum(old, jnp.max(scores, axis=0, keepdims=True))
            weights = jnp.exp(scores - new).astype(BF16)
            r_.top[slot] = new
            r_.acc[slot] = r_.acc[slot] * jnp.exp(old - new) + dot_nn(r_.kvt[...], weights)

        @pl.loop(0, NCTX)
        def _(r):
            key_block = jnp.where(r == 0, c, stepped(c, r - 1, -1))

            @pl.when((r > 0) & (r + AHEAD < NCTX))
            def _():
                send_keys(r + AHEAD - 1)

            @pl.when(r == 1)
            def _():
                feed_all()

            @pl.when(r == 6)
            def _():
                beside_keys()

            @pl.when(key_block <= top_block(c))
            def _():
                @pl.when(r > 0)
                def _():
                    copy(
                        f"kv{layer}",
                        r_.kvs.at[layer, 0],
                        r_.kvall.at[layer, key_block],
                        at_ctx(partner),
                        0,
                        key_block,
                    ).wait_recv()

                turned = r_.kvall[layer, key_block].astype(F32).T
                row = lax.broadcasted_iota(jnp.int32, turned.shape, 0)
                r_.kvt[...] = jnp.where(row < HEAD_DIM, 1.0, turned).astype(BF16)
                visit_both(key_block, visit)

        def finish(slot):
            total = r_.acc[slot, 0:HEAD_DIM, :]
            mean = r_.acc[slot, HEAD_DIM:, :] / total
            r_.ot[layer, slot] = mean
            r_.lse[layer, slot] = r_.top[slot] + jnp.log(total[0:1])
            r_.oout[layer, slot] = two_head_tile(mean, group).astype(BF16)

        finish(1)
        far = start_all(
            [
                copy(
                    f"ob{layer}",
                    r_.oout.at[layer, 1, span(ring(r), OWN), :],
                    r_.ob.at[layer, t],
                    at_partner(ring(r)),
                    r,
                )
                for r in range(NTP)
            ]
        )
        finish(0)
        near = start_all(
            [
                copy(
                    f"oa{layer}",
                    r_.oout.at[layer, 0, span(ring(r), OWN), :],
                    r_.oa.at[layer, t],
                    at_tp(ring(r)),
                    r - 1,
                )
                for r in range(1, NTP)
            ]
        )
        r_.oa[layer, t] = r_.oout[layer, 0, span(t, OWN), :]
        start(copy(f"ow{layer}", r_.oout.at[layer, 1], r_.oin.at[layer], at_ctx(partner)))

        result = r_.xown[layer].astype(F32) + vector(layer, 4) + r_.ffo[...]
        for r, item in enumerate(feed_copies):
            item.wait_recv()
            result = result + r_.ffr[layer, r].astype(F32)
        for item in far + near:
            item.wait_recv()
        before_out()
        heads = jnp.concatenate(
            [r_.oa[layer, p] + r_.ob[layer, p] for p in range(NTP)], axis=1
        )
        result = result + dot_nn(heads, r_.wo[layer].reshape(D, D))
        r_.fo[layer] = result.astype(BF16)


    def send_attention_grads(layer):
        tile = dot_nt(r_.gown[layer], r_.wo[layer].reshape(D, D)).astype(BF16)
        for p in range(NTP):
            r_.dos[layer, p] = tile[:, p * LANES : (p + 1) * LANES]
        far = start_all(
            [
                copy(
                    f"dob{layer}",
                    r_.dos.at[layer, ring(r)],
                    r_.dob.at[layer, t],
                    at_partner(ring(r)),
                    r,
                )
                for r in range(NTP)
            ]
        )
        near = start_all(
            [
                copy(
                    f"doa{layer}",
                    r_.dos.at[layer, ring(r)],
                    r_.doa.at[layer, t],
                    at_tp(ring(r)),
                    r - 1,
                )
                for r in range(1, NTP)
            ]
        )
        r_.doa[layer, t] = r_.dos[layer, t]
        return near + far

    def key_grad_send(layer, key_block):
        return copy(
            f"dkv{layer}",
            r_.dkvo.at[layer, key_block],
            r_.dkvi.at[layer, c],
            at_ctx(key_block),
            key_block,
            c,
        )

    def add_vector(layer, row, value):
        r_.gv[layer, row : row + 1, :] += jnp.sum(value, axis=0, keepdims=True)

    def feed_backward(layer, gathers):
        for item in gathers:
            item.wait_recv()
        r_.gv[layer] = jnp.zeros((8, D), F32)
        own_sum = jnp.sum(r_.gown[layer].astype(F32), axis=0, keepdims=True)
        r_.gv[layer, 4:5, :] = own_sum

        @pl.loop(0, NTP)
        def _(part):
            xhat, _ = normed(r_.xg[layer, part].astype(F32))
            attention_in, feed_in = norm_outputs(layer, xhat)
            r_.ain[part] = attention_in
            r_.fin[part] = feed_in
            up_pre = dot_nn(feed_in, r_.wup[layer]) + vector(layer, 5)
            hidden_grad = dot_nt(r_.gg[layer, part], r_.wdn[layer])
            up_grad = (hidden_grad * gelu_slope(up_pre)).astype(BF16)
            r_.ugs[part] = up_grad
            add_vector(layer, 5, up_grad.astype(F32))
            feed_grad = dot_nt(up_grad, r_.wup[layer])
            add_vector(layer, 1, xhat * feed_grad)
            add_vector(layer, 3, feed_grad)
            r_.dxh[part] = feed_grad * vector(layer, 1)

        full_grad = r_.gg[layer].reshape(BLK, D)
        up_terms = dot_tn(r_.fin[...].reshape(BLK, D), r_.ugs[...].reshape(BLK, D))
        r_.gwp[layer, 0:D, :] = up_terms.astype(BF16)
        r_.gwp[layer, D:, :] = dot_tn(r_.hid[layer].reshape(BLK, D), full_grad).astype(BF16)

    def backward(layer, grad_copies, before_keys, beside_keys, after_keys, before_end):
        before_keys()
        for item in grad_copies:
            item.wait_recv()

        def prepare(slot, tile):
            padded = my_head(tile.reshape(BLK, LANES).astype(F32), group, 1)
            r_.dopad[slot] = padded.astype(BF16)
            r_.delta[slot] = jnp.sum(
                padded.T[HEAD_DIM:, :] * r_.ot[layer, slot], axis=0, keepdims=True
            )

        prepare(0, r_.doa[layer])
        prepare(1, r_.dob[layer])
        r_.dqt[...] = jnp.zeros_like(r_.dqt)

        def visit(key_block, slot, masked):
            keys = r_.kvall[layer, key_block]
            queries, grads = r_.qpad[layer, slot], r_.dopad[slot]
            scores = dot_nt(keys, queries)
            weights = jnp.exp(scores - r_.lse[layer, slot])
            if masked:
                weights = jnp.where(key_mask(key_block, scores.shape, slot), weights, 0.0)
            weight_grad = dot_nt(keys, grads)
            score_grad = (weights * (weight_grad - r_.delta[slot])).astype(BF16)
            r_.dkva[...] += dot_nn(weights.astype(BF16), grads) + dot_nn(score_grad, queries)
            r_.dqt[slot] += dot_nn(r_.kvt[...], score_grad)

        @pl.loop(0, NCTX)
        def _(r):
            key_block = jnp.where(r == NCTX - 1, c, stepped(c, r, 1))

            @pl.when(key_block <= top_block(c))
            def _():
                r_.kvt[...] = r_.kvall[layer, key_block].astype(F32).T.astype(BF16)
                r_.dkva[...] = jnp.zeros_like(r_.dkva)
                visit_both(key_block, visit)
                r_.dkvo[layer, key_block] = r_.dkva[...].astype(BF16)

                @pl.when(r < NCTX - 1)
                def _():
                    key_grad_send(layer, key_block).start()

        def query_grad(slot):
            tile = two_head_tile(r_.dqt[slot, 0:HEAD_DIM, :] * 0.125, group)
            return turn(tile, r_.cosine[slot], -r_.sine[slot]).astype(BF16)

        r_.dqs[layer] = query_grad(1)
        query_copy = start(copy(f"dq{layer}", r_.dqs.at[layer], r_.dqi.at[layer], at_ctx(partner)))
        r_.dproj[:, 0:128] = query_grad(0)

        beside_keys()
        out_copy = copy(f"ow{layer}", r_.oout.at[layer, 1], r_.oin.at[layer], at_ctx(partner))
        out_copy.wait_recv()
        attention = r_.oout[layer, 0] + r_.oin[layer]
        full_grad = r_.gg[layer].reshape(BLK, D)
        r_.gwq[layer, 0:128, :] = dot_tn(attention, full_grad).astype(BF16)

        def key_grad(half):
            r_.dkva[...] = jnp.zeros_like(r_.dkva)

            @pl.loop(0, NCTX // 2)
            def _(step):
                source = half * (NCTX // 2) + step

                @pl.when(source == c)
                def _():
                    r_.dkva[...] += r_.dkvo[layer, c].astype(F32)

                @pl.when((c <= top_block(source)) & (source != c))
                def _():
                    copy(
                        f"dkv{layer}",
                        r_.dkvo.at[layer, 0],
                        r_.dkvi.at[layer, source],
                        at_ctx(partner),
                        0,
                        source,
                    ).wait_recv()
                    r_.dkva[...] += r_.dkvi[layer, source].astype(F32)

            return turn_left(r_.dkva[...], r_.cosine[0], -r_.sine[0])

        first, second = key_grad(0), key_grad(1)
        left = lanes(first.shape) < HEAD_DIM
        key = jnp.where(left, first, pltpu.roll(second, HEAD_DIM, 1))
        value = jnp.where(left, pltpu.roll(first, HEAD_DIM, 1), second)
        r_.dproj[:, 128:256] = key.astype(BF16)
        r_.dproj[:, 256:384] = value.astype(BF16)
        after_keys()
        query_copy.wait_recv()
        r_.dproj[:, 0:128] += r_.dqi[layer]

        def input_part(part):
            xhat, _ = normed(r_.xg[layer, part].astype(F32))
            grad = dot_nt(r_.dproj[span(part, OWN), :], r_.watt[layer])
            add_vector(layer, 0, xhat * grad)
            add_vector(layer, 2, grad)
            return r_.dxh[part] + grad * vector(layer, 0)

        scatters = []
        for r in range(1, NTP):
            r_.dxs[layer, r - 1] = input_part(ring(r)).astype(BF16)
            item = copy(
                f"dx{layer}",
                r_.dxs.at[layer, r - 1],
                r_.dxr.at[layer, r - 1],
                at_tp(ring(r)),
                r - 1,
            )
            scatters.append(start(item))
        total = input_part(t)
        bias_sum = jnp.sum(r_.dproj[...].astype(F32), axis=0, keepdims=True)
        r_.gv[layer, 6:7, 0:384] = bias_sum
        terms = dot_tn(r_.dproj[...], r_.ain[...].reshape(BLK, D))
        r_.gwq[layer, 128:, :] = terms.astype(BF16)
        before_end()
        for r, item in enumerate(scatters):
            item.wait_recv()
            total = total + r_.dxr[layer, r].astype(F32)
        xhat, inverse = normed(r_.xown[layer].astype(F32))
        along = jnp.mean(total * xhat, axis=-1, keepdims=True)
        centred = total - jnp.mean(total, axis=-1, keepdims=True) - xhat * along
        r_.go[layer] = (r_.gown[layer].astype(F32) + centred * inverse).astype(BF16)


    def cross_copy(which, layer):
        src = (r_.gwp, r_.gwq, r_.gv)[which].at[layer]
        return copy("cross", src, (r_.crp, r_.crq, r_.crv)[which], core, which)

    def cross_start(which, layer):
        @pl.when(s != layer)
        def _():
            cross_copy(which, layer).start()

    wide_parts = (
        (r_.gwp, r_.crp, r_.sump, r_.inp, r_.minep, r_.gatp, "ps", "pg", 64),
        (r_.gwq, r_.crq, r_.sumq, r_.inq, r_.mineq, r_.gatq, "qs", "qg", 32),
    )

    def scatter_copy(which, r):
        _, _, sums, arrived, _, _, kind, _, _ = wide_parts[which]
        d = wrap(c + r, NCTX)
        return copy(kind, sums.at[d], arrived.at[r], at_ctx(d), r)

    def gather_copy(which, r):
        _, _, _, _, mine, full, _, kind, _ = wide_parts[which]
        return copy(kind, mine, full.at[c], at_ctx(wrap(c + r, NCTX)), r)

    def scatter_terms(which, layer):
        terms, crossed, sums, _, _, _, _, _, chunk = wide_parts[which]

        @pl.when(s == layer)
        def _():
            cross_copy(which, layer).wait_recv()

            @pl.loop(0, NCTX)
            def _(j):
                rows = span(j, chunk)
                pair = terms[layer, rows, :].astype(F32) + crossed[rows, :].astype(F32)
                sums[j] = pair.astype(BF16)

            @pl.loop(1, NCTX)
            def _(r):
                scatter_copy(which, r).start()

    def store_chunk(which, j, value):
        chunk = wide_parts[which][-1]
        if which == 1:
            r_.allq[span(j, chunk), :] = value
            return
        half = D // chunk

        @pl.when(j < half)
        def _():
            r_.out_up[0, span(j, chunk), :] = value

        @pl.when(j >= half)
        def _():
            r_.out_dn[0, span(j - half, chunk), :] = value

    def gather_sums(which, layer):
        _, _, sums, arrived, mine, _, _, _, _ = wide_parts[which]

        @pl.when(s == layer)
        def _():
            total = sums[c].astype(F32)
            for r in range(1, NCTX):
                scatter_copy(which, r).wait_recv()
                total = total + arrived[r].astype(F32)
            mine[...] = total.astype(BF16)

            @pl.loop(1, NCTX)
            def _(r):
                gather_copy(which, r).start()

            store_chunk(which, c, total)

    def store_sums(which, layer):
        _, _, _, _, mine, full, _, kind, _ = wide_parts[which]

        @pl.when(s == layer)
        def _():
            @pl.loop(1, NCTX)
            def _(r):
                source = wrap(c + NCTX - r, NCTX)
                copy(kind, mine, full.at[source], core, r).wait_recv()
                store_chunk(which, source, full[source].astype(F32))

    def vector_copy(r):
        return copy("vc", r_.vec, r_.vec_in.at[r], at_ctx(wrap(c + r, NCTX)), r)

    def vector_tp_copy(r):
        return copy("vt", r_.vec_tp, r_.vec_tp_in.at[r - 1], at_tp(ring(r)), r - 1)

    def vector_first(layer):
        @pl.when(s == layer)
        def _():
            cross_copy(2, layer).wait_recv()
            r_.vec[...] = r_.gv[layer] + r_.crv[...]

            @pl.loop(1, NCTX)
            def _(r):
                vector_copy(r).start()

    def vector_second(layer):
        @pl.when(s == layer)
        def _():
            total = r_.vec[...]
            for r in range(1, NCTX):
                vector_copy(r).wait_recv()
                total = total + r_.vec_in[r]
            r_.vec_tp[...] = total
            for r in range(1, NTP):
                vector_tp_copy(r).start()

    def vector_last(layer):
        @pl.when(s == layer)
        def _():
            total = r_.vec_tp[...]
            shared = total
            for r in range(1, NTP):
                vector_tp_copy(r).wait_recv()
                shared = shared + r_.vec_tp_in[r - 1]
            r_.out_gain[0] = shared[0:2, :]
            r_.out_norm_bias[0] = shared[2:4, :]
            r_.out_branch[...] = shared[4:5, :]
            r_.out_up_bias[...] = total[5:6, :]
            for k in range(3):
                bias = total[6:7, k * LANES : (k + 1) * LANES]
                r_.out_att_bias[0, k : k + 1, :] = bias

    def store_attention():
        r_.out_wo[0] = r_.allq[0:128, :]
        turned = r_.allq[128:, :].T
        for k in range(3):
            r_.out_att[0, k] = turned[:, k * LANES : (k + 1) * LANES]


    def nothing():
        pass

    def wait_first_weights():
        for load in loads:
            load.wait()
        for item in weight_copies[:4]:
            item.wait_recv()

    wo_copies, g_copies = [], []

    def start_later_gathers():
        for r in range(1, NTP):
            item = copy("wo", r_.own_wo.at[0], r_.wo.at[s, t], at_tp(ring(r)), r - 1)
            wo_copies.append(start(item))
        g_copies.extend(gather_rows("g1", r_.gown.at[1], r_.gg.at[1]))
        for item in weight_copies[4:]:
            item.wait_recv()

    def pass_output_weight():
        for item in wo_copies:
            item.wait_recv()
        start(wo_pass)

    wo_pass = copy("wo_pass", r_.wo.at[s], r_.wo.at[s], core)
    forward(
        0,
        x_copies,
        wait_first_weights,
        start_later_gathers,
        pass_output_weight,
        wo_pass.wait_recv,
    )
    r_.xown[1] = r_.fo[0]
    x_copies = gather_rows("x1", r_.xown.at[1], r_.xg.at[1])
    grad_copies = send_attention_grads(1)

    def feed_ahead():
        feed_backward(1, g_copies)
        cross_start(0, 1)

    forward(1, x_copies, nothing, nothing, feed_ahead, nothing)

    rows_copy = start(copy("rows", r_.fo.at[1 - s], r_.out_rows.at[0, s], core))
    r_.out_rows[0, s] = r_.fo[s]

    def late_sums(layer):
        cross_start(1, layer)
        cross_start(2, layer)

    backward(
        1,
        grad_copies,
        lambda: scatter_terms(0, 1),
        lambda: gather_sums(0, 1),
        nothing,
        lambda: late_sums(1),
    )
    r_.gown[0] = r_.go[1]
    grad_copies = send_attention_grads(0)
    g_copies = gather_rows("g0", r_.gown.at[0], r_.gg.at[0])

    def finish_second():
        scatter_terms(1, 1)
        vector_first(1)

    def feed_last():
        feed_backward(0, g_copies)
        cross_start(0, 0)
        gather_sums(1, 1)
        vector_second(1)

    def before_last():
        late_sums(0)
        gather_sums(0, 0)
        scatter_terms(1, 0)
        vector_first(0)

    backward(0, grad_copies, finish_second, feed_last, lambda: scatter_terms(0, 0), before_last)
    grads_copy = start(copy("grads", r_.go.at[1 - s], r_.out_grads.at[0, s], core))
    r_.out_grads[0, s] = r_.go[s]
    gather_sums(1, 0)
    vector_second(0)
    for layer in (1, 0):
        store_sums(0, layer)
        vector_last(layer)
        store_sums(1, layer)
    store_attention()
    rows_copy.wait_recv()
    grads_copy.wait_recv()


    for item in sent:
        item.wait_send()
    for layer in range(2):

        @pl.loop(1, NCTX)
        def _(r):
            wanted, item = key_send(layer, r - 1)

            @pl.when(wanted)
            def _():
                item.wait_send()

            key_block = wrap(c + r, NCTX)

            @pl.when(key_block <= top_block(c))
            def _():
                key_grad_send(layer, key_block).wait_send()

        @pl.when(s != layer)
        def _():
            for which in range(3):
                cross_copy(which, layer).wait_send()

    @pl.loop(1, NCTX)
    def _(r):
        for which in range(2):
            scatter_copy(which, r).wait_send()
            gather_copy(which, r).wait_send()
        vector_copy(r).wait_send()

    for r in range(1, NTP):
        vector_tp_copy(r).wait_send()


def run_step(operands):
    vmem = pl.BlockSpec(memory_space=pltpu.VMEM)
    dma = pltpu.SemaphoreType.DMA
    return pl.pallas_call(
        step_kernel,
        out_shape=[jax.ShapeDtypeStruct(shape, kind) for _, shape, kind in OUTPUTS],
        in_specs=[pl.BlockSpec(memory_space=space) for _, space in INPUTS],
        out_specs=[vmem] * len(OUTPUTS),
        scratch_shapes=[pltpu.VMEM(shape, kind) for _, shape, kind in SCRATCH]
        + [dma((COPIES,)), dma((COPIES,)), dma((6,))],
        compiler_params=pltpu.CompilerParams(
            collective_id=0, has_side_effects=True, vmem_limit_bytes=VMEM_LIMIT
        ),
        name="train_step",
    )(*operands)


def hand_over_kernel(*refs):
    count = len(refs) // 2
    for source, result in zip(refs[:count], refs[count:]):
        result[...] = source[...]


def hand_over(arrays):
    vmem = [pl.BlockSpec(memory_space=pltpu.VMEM)] * len(arrays)
    return pl.pallas_call(
        hand_over_kernel,
        out_shape=[jax.ShapeDtypeStruct(a.shape, a.dtype) for a in arrays],
        in_specs=vmem,
        out_specs=vmem,
        compiler_params=pltpu.CompilerParams(vmem_limit_bytes=VMEM_LIMIT),
        name="hand_over",
    )(*arrays)


def local(
    block_input,
    output_grad,
    sequence_lengths,
    norm_gain,
    norm_bias,
    attention_weight,
    attention_bias,
    output_weight,
    up_weight,
    up_bias,
    down_weight,
    branch_bias,
):
    results = run_step(
        (
            block_input,
            output_grad,
            sequence_lengths,
            norm_gain,
            norm_bias,
            attention_weight,
            attention_bias,
            output_weight,
            up_weight,
            up_bias,
            down_weight,
            branch_bias,
        )
    )
    return tuple(hand_over(results))


def solution(mesh):
    placed = (
        P(None, ("ctx", "tp"), None),
        P(None, ("ctx", "tp"), None),
        P(),
        P("section", None, None),
        P("section", None, None),
        P("section", None, None, "tp"),
        P("section", None, "tp"),
        P("section", "tp", None),
        P("section", None, "tp"),
        P("section", "tp"),
        P("section", "tp", None),
        P("section", None),
    )
    return jax.shard_map(
        local,
        mesh=mesh,
        in_specs=placed,
        out_specs=(
            P("section", None, ("ctx", "tp"), None),
            P("section", None, ("ctx", "tp"), None),
            P("section", None, None),
            P("section", None, None),
            P("section", None, None, "tp"),
            P("section", None, "tp"),
            P("section", "tp", None),
            P("section", None, "tp"),
            P("section", "tp"),
            P("section", "tp", None),
            P("section", None),
        ),
        check_vma=False,
    )
```

```python
from types import SimpleNamespace

import jax
import jax.numpy as jnp
from jax import lax
from jax.experimental import pallas as pl
from jax.experimental.pallas import tpu as pltpu
from jax.sharding import PartitionSpec as P

HEAD_DIM = 64
ROT = 16
MESH = pl.DeviceIdType.MESH
F32 = jnp.float32
BF16 = jnp.bfloat16
VMEM_LIMIT = 56 * 1024 * 1024
NCTX = 16
NTP = 4
BLK = 512
OWN = 128
D = 512
LANES = 128
STEPS = (
    (0, 1), (1, 0), (0, 3), (3, 0), (1, 1), (3, 3), (1, 3), (3, 1),
    (0, 2), (2, 0), (1, 2), (3, 2), (2, 1), (2, 3), (2, 2),
)
AHEAD = 8
MASKED = -1e30
LOWEST = -1e29


def dot_nn(a, b):
    return lax.dot_general(a, b, (((1,), (0,)), ((), ())), preferred_element_type=F32)


def dot_nt(a, b):
    return lax.dot_general(a, b, (((1,), (1,)), ((), ())), preferred_element_type=F32)


def dot_tn(a, b):
    return lax.dot_general(a, b, (((0,), (0,)), ((), ())), preferred_element_type=F32)


def phi(v):
    return 0.5 * (1.0 + lax.erf(v * (0.5**0.5)))


def gelu(v):
    return v * phi(v)


def gelu_slope(v):
    return phi(v) + v * jnp.exp(-0.5 * v * v) * 0.3989422804014327


def normed(rows):
    centre = rows - jnp.mean(rows, axis=-1, keepdims=True)
    spread = jnp.mean(centre * centre, axis=-1, keepdims=True)
    inverse = lax.rsqrt(spread + 1e-05)
    return centre * inverse, inverse


def remote(src, dst, send, recv, peer):
    return pltpu.make_async_remote_copy(
        src_ref=src, dst_ref=dst, send_sem=send, recv_sem=recv, device_id=peer, device_id_type=MESH
    )


def lanes(shape):
    return lax.broadcasted_iota(jnp.int32, shape, 1)


def turn(tile, cosine, sine):
    back = pltpu.roll(tile, LANES - 8, 1)
    ahead = pltpu.roll(tile, 8, 1)
    other = jnp.where(lanes(tile.shape) % HEAD_DIM < 8, back, ahead)
    return tile * cosine + other * sine


def turn_left(tile, cosine, sine):
    return jnp.where(lanes(tile.shape) < HEAD_DIM, turn(tile, cosine, sine), tile)


def my_head(tile, group, half):
    swapped = pltpu.roll(tile, HEAD_DIM, 1)
    chosen = jnp.where(group == half, tile, swapped)
    return jnp.where(lanes(tile.shape) // HEAD_DIM == half, chosen, 0.0)


def two_head_tile(rows, group):
    blank = jnp.zeros_like(rows)
    first = jnp.where(group == 0, rows, blank)
    second = jnp.where(group == 0, blank, rows)
    return jnp.concatenate([first, second], axis=0).T


def top_block(d):
    return jnp.maximum(d, NCTX - 1 - d)


def needs_mask(key_block, query_block):
    return (key_block == 0) | (key_block == query_block) | (query_block == NCTX - 1)


def wrap(index, count):
    return jnp.where(index >= count, index - count, index)


def stepped(c, index, sign):
    z, y = c // 4, c % 4
    dz, dy = 0, 0
    for k, (along_z, along_y) in enumerate(STEPS):
        dz = jnp.where(index == k, along_z, dz)
        dy = jnp.where(index == k, along_y, dy)
    return wrap(z + (dz if sign > 0 else 4 - dz), 4) * 4 + wrap(y + (dy if sign > 0 else 4 - dy), 4)


def second_group(d):
    return jnp.where(d >= NCTX // 2, 1, 0)


def span(index, size):
    return pl.ds(pl.multiple_of(index * size, size), size)


OUTPUTS = (
    ("out_rows", (1, 2, OWN, D), BF16),
    ("out_grads", (1, 2, OWN, D), BF16),
    ("out_gain", (1, 2, D), F32),
    ("out_norm_bias", (1, 2, D), F32),
    ("out_p", (NCTX, 64, D), BF16),
    ("out_q", (NCTX, 32, D), BF16),
    ("out_att_bias", (1, 3, OWN), F32),
    ("out_up_bias", (1, D), F32),
    ("out_branch", (1, D), F32),
)

SCRATCH = (
    ("watt", (2, D, 384), BF16),
    ("wo", (2, NTP, OWN, D), BF16),
    ("wup", (2, D, D), BF16),
    ("wdn", (2, D, D), BF16),
    ("vecs", (2, 8, D), F32),
    ("vown", (8, D), F32),
    ("place", (2, 2, BLK), jnp.int32),
    ("cosine", (2, BLK, LANES), F32),
    ("sine", (2, BLK, LANES), F32),
    ("xown", (2, OWN, D), BF16),
    ("fo", (2, OWN, D), BF16),
    ("xg", (2, NTP, OWN, D), BF16),
    ("qpad", (2, 2, BLK, LANES), BF16),
    ("kvall", (2, NCTX, BLK, LANES), BF16),
    ("ot", (2, 2, HEAD_DIM, BLK), F32),
    ("lse", (2, 2, 1, BLK), F32),
    ("hid", (2, NTP, OWN, D), BF16),
    ("kvs", (2, 2, BLK, LANES), BF16),
    ("qs", (2, BLK, LANES), BF16),
    ("qin", (2, BLK, LANES), BF16),
    ("oout", (2, 2, BLK, LANES), BF16),
    ("oin", (2, BLK, LANES), BF16),
    ("oa", (2, NTP, OWN, LANES), BF16),
    ("ob", (2, NTP, OWN, LANES), BF16),
    ("ffs", (2, NTP - 1, OWN, D), BF16),
    ("ffr", (2, NTP - 1, OWN, D), BF16),
    ("gown", (2, OWN, D), BF16),
    ("go", (2, OWN, D), BF16),
    ("gg", (2, NTP, OWN, D), BF16),
    ("dos", (2, NTP, OWN, LANES), BF16),
    ("doa", (2, NTP, OWN, LANES), BF16),
    ("dob", (2, NTP, OWN, LANES), BF16),
    ("dkvo", (2, NCTX, BLK, LANES), BF16),
    ("dkvi", (2, NCTX, BLK, LANES), BF16),
    ("dqs", (2, BLK, LANES), BF16),
    ("dqi", (2, BLK, LANES), BF16),
    ("dxs", (2, NTP - 1, OWN, D), BF16),
    ("dxr", (2, NTP - 1, OWN, D), BF16),
    ("gwp", (2, 2 * D, D), BF16),
    ("gwq", (2, D, D), BF16),
    ("gv", (2, 8, D), F32),
    ("kvt", (LANES, BLK), BF16),
    ("acc", (2, LANES, BLK), F32),
    ("top", (2, 1, BLK), F32),
    ("ffo", (OWN, D), F32),
    ("dopad", (2, BLK, LANES), BF16),
    ("delta", (2, 1, BLK), F32),
    ("dqt", (2, LANES, BLK), F32),
    ("dkva", (BLK, LANES), F32),
    ("ain", (NTP, OWN, D), BF16),
    ("fin", (NTP, OWN, D), BF16),
    ("ugs", (NTP, OWN, D), BF16),
    ("dxh", (NTP, OWN, D), F32),
    ("dproj", (BLK, 384), BF16),
    ("crp", (2 * D, D), BF16),
    ("crq", (D, D), BF16),
    ("crv", (8, D), F32),
    ("sump", (NCTX, 64, D), BF16),
    ("sumq", (NCTX, 32, D), BF16),
    ("inp", (NCTX, 64, D), BF16),
    ("inq", (NCTX, 32, D), BF16),
    ("vec", (8, D), F32),
    ("vec_in", (NCTX, 8, D), F32),
    ("vec_tp", (8, D), F32),
    ("vec_tp_in", (NTP - 1, 8, D), F32),
)

INPUTS = (
    ("xin", pltpu.VMEM),
    ("gin", pltpu.VMEM),
    ("lengths", pltpu.SMEM),
    ("gains", pltpu.VMEM),
    ("biases", pltpu.VMEM),
    ("own_watt", pl.ANY),
    ("att_bias", pltpu.VMEM),
    ("own_wo", pl.ANY),
    ("own_wup", pl.ANY),
    ("up_bias", pltpu.VMEM),
    ("own_wdn", pl.ANY),
    ("branch_bias", pltpu.VMEM),
)

SEMAPHORES = {}
COPIES = 0
for name, count in (
    ("weights", 6),
    ("wo", 3),
    ("wo_pass", 1),
    ("rows", 1),
    ("grads", 1),
    ("cross", 3),
    ("ps", NCTX),
    ("pg", NCTX),
    ("qs", NCTX),
    ("qg", NCTX),
    ("vc", NCTX),
    ("vt", 3),
) + tuple(
    (f"{kind}{layer}", count)
    for layer in range(2)
    for kind, count in (
        ("x", 3),
        ("kv", NCTX),
        ("q", 1),
        ("oa", 3),
        ("ob", 4),
        ("ow", 1),
        ("ff", 3),
        ("g", 3),
        ("doa", 3),
        ("dob", 4),
        ("dkv", NCTX),
        ("dq", 1),
        ("dx", 3),
    )
):
    SEMAPHORES[name] = COPIES
    COPIES += count


def step_kernel(*refs):
    names = tuple(n for n, _ in INPUTS) + tuple(n for n, _, _ in OUTPUTS) + tuple(n for n, _, _ in SCRATCH)
    r_ = SimpleNamespace(**dict(zip(names, refs)))
    send_sems, recv_sems, load_sems = refs[len(names) :]
    s = lax.axis_index("section")
    c = lax.axis_index("ctx")
    t = lax.axis_index("tp")
    group = second_group(c)
    partner = NCTX - 1 - c
    core = {"section": 1 - s, "ctx": c, "tp": t}

    def at_ctx(d):
        return {"section": s, "ctx": d, "tp": t}

    def at_tp(d):
        return {"section": s, "ctx": c, "tp": d}

    def at_partner(d):
        return {"section": s, "ctx": partner, "tp": d}

    def ring(r):
        return wrap(t + r, NTP)

    def copy(kind, src, dst, peer, send=0, recv=None):
        base = SEMAPHORES[kind]
        recv = send if recv is None else recv
        return remote(src, dst, send_sems.at[base + send], recv_sems.at[base + recv], peer)

    sent = []

    def start(item):
        item.start()
        sent.append(item)
        return item

    def start_all(items):
        return [start(item) for item in items]

    peers = [core]
    peers += [at_tp(ring(r)) for r in range(1, NTP)]
    peers += [at_ctx(wrap(c + r, NCTX)) for r in range(1, NCTX)]
    peers += [at_partner(ring(r)) for r in range(1, NTP)]
    barrier = pltpu.get_barrier_semaphore()
    for peer in peers:
        pl.semaphore_signal(barrier, inc=1, device_id=peer, device_id_type=MESH)

    own_weights = [
        (r_.own_watt.at[0, k], r_.watt.at[s, :, k * LANES : (k + 1) * LANES]) for k in range(3)
    ]
    own_weights += [(r_.own_wup.at[0], r_.wup.at[s]), (r_.own_wdn.at[0], r_.wdn.at[s])]
    loads = [
        pltpu.make_async_copy(src, dst, load_sems.at[i])
        for i, (src, dst) in enumerate(own_weights + [(r_.own_wo.at[0], r_.wo.at[s, t])])
    ]
    for load in loads:
        load.start()
    r_.vown[...] = jnp.zeros((8, D), F32)
    r_.vown[0:2, :] = r_.gains[0]
    r_.vown[2:4, :] = r_.biases[0]
    r_.vown[4:5, :] = r_.branch_bias[...]
    r_.vown[5:6, :] = r_.up_bias[...]
    for k in range(3):
        r_.vown[6:7, k * LANES : (k + 1) * LANES] = r_.att_bias[0, k : k + 1, :]
    r_.vecs[s] = r_.vown[...]
    r_.xown[0] = r_.xin[s]
    r_.gown[1] = r_.gin[s]
    pl.semaphore_wait(barrier, len(peers))

    def gather_rows(kind, own, full):
        full[t] = own[...]
        return start_all(
            [copy(kind, own, full.at[t], at_tp(ring(r)), r - 1) for r in range(1, NTP)]
        )

    x_copies = gather_rows("x0", r_.xown.at[0], r_.xg.at[0])
    weight_copies = start_all(
        [
            copy("weights", src, dst, core, i)
            for i, (src, dst) in enumerate([(r_.vown, r_.vecs.at[s])] + own_weights)
        ]
    )

    rate_row = lax.broadcasted_iota(jnp.int32, (ROT // 2, 1), 0)
    rates = jnp.zeros((ROT // 2, 1), F32)
    for i in range(ROT // 2):
        rates = jnp.where(rate_row == i, 1.0 / 10000.0 ** (2 * i / ROT), rates)
    for slot, block in ((0, c), (1, partner)):
        place = block * BLK + lanes((1, BLK))
        first = jnp.zeros((1, BLK), jnp.int32)
        end = 0
        for k in range(r_.lengths.shape[1]):
            length = jnp.where(s == 0, r_.lengths[0, k], r_.lengths[1, k])
            end = end + length
            first = first + jnp.where(place >= end, length, 0)
        r_.place[slot, 0:1, :] = place
        r_.place[slot, 1:2, :] = first
        angles = (place - first).astype(F32) * rates
        cosine, sine = jnp.cos(angles), jnp.sin(angles)
        still = jnp.zeros((HEAD_DIM - ROT, BLK), F32)
        cosine = jnp.concatenate([cosine, cosine, still + 1.0], axis=0)
        sine = jnp.concatenate([-sine, sine, still], axis=0)
        r_.cosine[slot] = jnp.concatenate([cosine, cosine], axis=0).T
        r_.sine[slot] = jnp.concatenate([sine, sine], axis=0).T

    def vector(layer, row, width=D):
        return r_.vecs[layer, row : row + 1, 0:width]

    def norm_outputs(layer, xhat):
        first = xhat * vector(layer, 0) + vector(layer, 2)
        second = xhat * vector(layer, 1) + vector(layer, 3)
        return first.astype(BF16), second.astype(BF16)

    def key_mask(key_block, shape, slot):
        key = key_block * BLK + lax.broadcasted_iota(jnp.int32, shape, 0)
        return (key <= r_.place[slot, 0:1, :]) & (key >= r_.place[slot, 1:2, :])

    def visit_both(key_block, visit):
        @pl.loop(0, 2)
        def _(slot):
            query_block = jnp.where(slot == 0, c, partner)
            reached = key_block <= query_block
            edge = needs_mask(key_block, query_block)

            @pl.when(reached & edge)
            def _():
                visit(key_block, slot, True)

            @pl.when(reached & jnp.logical_not(edge))
            def _():
                visit(key_block, slot, False)


    def key_send(layer, index, part=None):
        d = stepped(c, index, 1)
        rows = pl.ds(0, BLK) if part is None else span(part, OWN)
        return c <= top_block(d), copy(
            f"kv{layer}",
            r_.kvs.at[layer, second_group(d), rows, :],
            r_.kvall.at[layer, c, rows, :],
            at_ctx(d),
            d,
            c,
        )

    def forward(layer, gathers, before_keys, after_keys, beside_keys, before_out):
        def project(part):
            xhat, _ = normed(r_.xg[layer, part].astype(F32))
            attention_in, _ = norm_outputs(layer, xhat)
            pre = dot_nn(attention_in, r_.watt[layer]) + vector(layer, 6, 384)
            rows = span(part, OWN)
            cosine, sine = r_.cosine[0, rows, :], r_.sine[0, rows, :]
            query = turn(pre[:, 0:128], cosine, sine) * 0.125
            r_.qs[layer, rows, :] = query.astype(BF16)
            key, value = turn(pre[:, 128:256], cosine, sine), pre[:, 256:384]
            left = lanes(key.shape) < HEAD_DIM
            first = jnp.where(left, key, pltpu.roll(value, HEAD_DIM, 1))
            second = jnp.where(left, pltpu.roll(key, HEAD_DIM, 1), value)
            r_.kvs[layer, 0, rows, :] = first.astype(BF16)
            r_.kvs[layer, 1, rows, :] = second.astype(BF16)

            copy(
                f"q{layer}",
                r_.qs.at[layer, rows, :],
                r_.qin.at[layer, rows, :],
                at_ctx(partner),
            ).start()

            @pl.loop(0, AHEAD)
            def _(index):
                send_keys(index, part)

        def send_keys(index, part=None):
            wanted, item = key_send(layer, index, part)

            @pl.when(wanted)
            def _():
                item.start()

        before_keys()
        project(t)
        for r, item in enumerate(gathers):
            item.wait_recv()
            project(wrap(t + NTP - 1 - r, NTP))

        query_copy = copy(f"q{layer}", r_.qs.at[layer], r_.qin.at[layer], at_ctx(partner))
        sent.append(query_copy)

        r_.kvall[layer, c] = r_.kvs[layer, group]
        after_keys()

        def feed_forward(part):
            xhat, _ = normed(r_.xg[layer, part].astype(F32))
            _, feed_in = norm_outputs(layer, xhat)
            hidden = gelu(dot_nn(feed_in, r_.wup[layer]) + vector(layer, 5)).astype(BF16)
            r_.hid[layer, part] = hidden
            return dot_nn(hidden, r_.wdn[layer])

        def feed_send(r):
            return copy(
                f"ff{layer}",
                r_.ffs.at[layer, r - 1],
                r_.ffr.at[layer, r - 1],
                at_tp(ring(r)),
                r - 1,
            )

        feed_copies = [feed_send(r) for r in range(1, NTP)]
        sent.extend(feed_copies)

        def feed_all():
            @pl.loop(1, NTP)
            def _(r):
                r_.ffs[layer, r - 1] = feed_forward(ring(r)).astype(BF16)
                feed_send(r).start()

            r_.ffo[...] = feed_forward(t)

        r_.qpad[layer, 0] = my_head(r_.qs[layer].astype(F32), group, 0).astype(BF16)
        query_copy.wait_recv()
        r_.qpad[layer, 1] = my_head(r_.qin[layer].astype(F32), group, 0).astype(BF16)
        r_.acc[...] = jnp.zeros_like(r_.acc)
        r_.top[...] = jnp.full_like(r_.top, LOWEST)

        def visit(key_block, slot, masked):
            scores = dot_nt(r_.kvall[layer, key_block], r_.qpad[layer, slot])
            if masked:
                scores = jnp.where(key_mask(key_block, scores.shape, slot), scores, MASKED)
            old = r_.top[slot]
            new = jnp.maximum(old, jnp.max(scores, axis=0, keepdims=True))
            weights = jnp.exp(scores - new).astype(BF16)
            r_.top[slot] = new
            r_.acc[slot] = r_.acc[slot] * jnp.exp(old - new) + dot_nn(r_.kvt[...], weights)

        @pl.loop(0, NCTX)
        def _(r):
            key_block = jnp.where(r == 0, c, stepped(c, r - 1, -1))

            @pl.when((r > 0) & (r + AHEAD < NCTX))
            def _():
                send_keys(r + AHEAD - 1)

            @pl.when(r == 1)
            def _():
                feed_all()

            @pl.when(r == 6)
            def _():
                beside_keys()

            @pl.when(key_block <= top_block(c))
            def _():
                @pl.when(r > 0)
                def _():
                    copy(
                        f"kv{layer}",
                        r_.kvs.at[layer, 0],
                        r_.kvall.at[layer, key_block],
                        at_ctx(partner),
                        0,
                        key_block,
                    ).wait_recv()

                turned = r_.kvall[layer, key_block].astype(F32).T
                row = lax.broadcasted_iota(jnp.int32, turned.shape, 0)
                r_.kvt[...] = jnp.where(row < HEAD_DIM, 1.0, turned).astype(BF16)
                visit_both(key_block, visit)

        def finish(slot):
            total = r_.acc[slot, 0:HEAD_DIM, :]
            mean = r_.acc[slot, HEAD_DIM:, :] / total
            r_.ot[layer, slot] = mean
            r_.lse[layer, slot] = r_.top[slot] + jnp.log(total[0:1])
            r_.oout[layer, slot] = two_head_tile(mean, group).astype(BF16)

        finish(1)
        far = start_all(
            [
                copy(
                    f"ob{layer}",
                    r_.oout.at[layer, 1, span(ring(r), OWN), :],
                    r_.ob.at[layer, t],
                    at_partner(ring(r)),
                    r,
                )
                for r in range(NTP)
            ]
        )
        finish(0)
        near = start_all(
            [
                copy(
                    f"oa{layer}",
                    r_.oout.at[layer, 0, span(ring(r), OWN), :],
                    r_.oa.at[layer, t],
                    at_tp(ring(r)),
                    r - 1,
                )
                for r in range(1, NTP)
            ]
        )
        r_.oa[layer, t] = r_.oout[layer, 0, span(t, OWN), :]
        start(copy(f"ow{layer}", r_.oout.at[layer, 1], r_.oin.at[layer], at_ctx(partner)))

        result = r_.xown[layer].astype(F32) + vector(layer, 4) + r_.ffo[...]
        for r, item in enumerate(feed_copies):
            item.wait_recv()
            result = result + r_.ffr[layer, r].astype(F32)
        for item in far + near:
            item.wait_recv()
        before_out()
        heads = jnp.concatenate(
            [r_.oa[layer, p] + r_.ob[layer, p] for p in range(NTP)], axis=1
        )
        result = result + dot_nn(heads, r_.wo[layer].reshape(D, D))
        r_.fo[layer] = result.astype(BF16)


    def send_attention_grads(layer):
        tile = dot_nt(r_.gown[layer], r_.wo[layer].reshape(D, D)).astype(BF16)
        for p in range(NTP):
            r_.dos[layer, p] = tile[:, p * LANES : (p + 1) * LANES]
        far = start_all(
            [
                copy(
                    f"dob{layer}",
                    r_.dos.at[layer, ring(r)],
                    r_.dob.at[layer, t],
                    at_partner(ring(r)),
                    r,
                )
                for r in range(NTP)
            ]
        )
        near = start_all(
            [
                copy(
                    f"doa{layer}",
                    r_.dos.at[layer, ring(r)],
                    r_.doa.at[layer, t],
                    at_tp(ring(r)),
                    r - 1,
                )
                for r in range(1, NTP)
            ]
        )
        r_.doa[layer, t] = r_.dos[layer, t]
        return near + far

    def key_grad_send(layer, key_block):
        return copy(
            f"dkv{layer}",
            r_.dkvo.at[layer, key_block],
            r_.dkvi.at[layer, c],
            at_ctx(key_block),
            key_block,
            c,
        )

    def add_vector(layer, row, value):
        r_.gv[layer, row : row + 1, :] += jnp.sum(value, axis=0, keepdims=True)

    def feed_backward(layer, gathers):
        for item in gathers:
            item.wait_recv()
        r_.gv[layer] = jnp.zeros((8, D), F32)
        own_sum = jnp.sum(r_.gown[layer].astype(F32), axis=0, keepdims=True)
        r_.gv[layer, 4:5, :] = own_sum

        @pl.loop(0, NTP)
        def _(part):
            xhat, _ = normed(r_.xg[layer, part].astype(F32))
            attention_in, feed_in = norm_outputs(layer, xhat)
            r_.ain[part] = attention_in
            r_.fin[part] = feed_in
            up_pre = dot_nn(feed_in, r_.wup[layer]) + vector(layer, 5)
            hidden_grad = dot_nt(r_.gg[layer, part], r_.wdn[layer])
            up_grad = (hidden_grad * gelu_slope(up_pre)).astype(BF16)
            r_.ugs[part] = up_grad
            add_vector(layer, 5, up_grad.astype(F32))
            feed_grad = dot_nt(up_grad, r_.wup[layer])
            add_vector(layer, 1, xhat * feed_grad)
            add_vector(layer, 3, feed_grad)
            r_.dxh[part] = feed_grad * vector(layer, 1)

        full_grad = r_.gg[layer].reshape(BLK, D)
        up_terms = dot_tn(r_.fin[...].reshape(BLK, D), r_.ugs[...].reshape(BLK, D))
        r_.gwp[layer, 0:D, :] = up_terms.astype(BF16)
        r_.gwp[layer, D:, :] = dot_tn(r_.hid[layer].reshape(BLK, D), full_grad).astype(BF16)

    def backward(layer, grad_copies, before_keys, among_keys, beside_keys, after_keys, before_end):
        before_keys()
        for item in grad_copies:
            item.wait_recv()

        def prepare(slot, tile):
            padded = my_head(tile.reshape(BLK, LANES).astype(F32), group, 1)
            r_.dopad[slot] = padded.astype(BF16)
            r_.delta[slot] = jnp.sum(
                padded.T[HEAD_DIM:, :] * r_.ot[layer, slot], axis=0, keepdims=True
            )

        prepare(0, r_.doa[layer])
        prepare(1, r_.dob[layer])
        r_.dqt[...] = jnp.zeros_like(r_.dqt)

        def visit(key_block, slot, masked):
            keys = r_.kvall[layer, key_block]
            queries, grads = r_.qpad[layer, slot], r_.dopad[slot]
            scores = dot_nt(keys, queries)
            weights = jnp.exp(scores - r_.lse[layer, slot])
            if masked:
                weights = jnp.where(key_mask(key_block, scores.shape, slot), weights, 0.0)
            weight_grad = dot_nt(keys, grads)
            score_grad = (weights * (weight_grad - r_.delta[slot])).astype(BF16)
            r_.dkva[...] += dot_nn(weights.astype(BF16), grads) + dot_nn(score_grad, queries)
            r_.dqt[slot] += dot_nn(r_.kvt[...], score_grad)

        @pl.loop(0, NCTX)
        def _(r):
            key_block = jnp.where(r == NCTX - 1, c, stepped(c, r, 1))

            @pl.when(r == AHEAD)
            def _():
                among_keys()

            @pl.when(key_block <= top_block(c))
            def _():
                r_.kvt[...] = r_.kvall[layer, key_block].astype(F32).T.astype(BF16)
                r_.dkva[...] = jnp.zeros_like(r_.dkva)
                visit_both(key_block, visit)
                r_.dkvo[layer, key_block] = r_.dkva[...].astype(BF16)

                @pl.when(r < NCTX - 1)
                def _():
                    key_grad_send(layer, key_block).start()

        def query_grad(slot):
            tile = two_head_tile(r_.dqt[slot, 0:HEAD_DIM, :] * 0.125, group)
            return turn(tile, r_.cosine[slot], -r_.sine[slot]).astype(BF16)

        r_.dqs[layer] = query_grad(1)
        query_copy = start(copy(f"dq{layer}", r_.dqs.at[layer], r_.dqi.at[layer], at_ctx(partner)))
        r_.dproj[:, 0:128] = query_grad(0)

        beside_keys()
        out_copy = copy(f"ow{layer}", r_.oout.at[layer, 1], r_.oin.at[layer], at_ctx(partner))
        out_copy.wait_recv()
        attention = r_.oout[layer, 0] + r_.oin[layer]
        full_grad = r_.gg[layer].reshape(BLK, D)
        r_.gwq[layer, 0:128, :] = dot_tn(attention, full_grad).astype(BF16)

        def key_grad(half):
            r_.dkva[...] = jnp.zeros_like(r_.dkva)

            @pl.loop(0, NCTX // 2)
            def _(step):
                source = half * (NCTX // 2) + step

                @pl.when(source == c)
                def _():
                    r_.dkva[...] += r_.dkvo[layer, c].astype(F32)

                @pl.when((c <= top_block(source)) & (source != c))
                def _():
                    copy(
                        f"dkv{layer}",
                        r_.dkvo.at[layer, 0],
                        r_.dkvi.at[layer, source],
                        at_ctx(partner),
                        0,
                        source,
                    ).wait_recv()
                    r_.dkva[...] += r_.dkvi[layer, source].astype(F32)

            return turn_left(r_.dkva[...], r_.cosine[0], -r_.sine[0])

        first, second = key_grad(0), key_grad(1)
        left = lanes(first.shape) < HEAD_DIM
        key = jnp.where(left, first, pltpu.roll(second, HEAD_DIM, 1))
        value = jnp.where(left, pltpu.roll(first, HEAD_DIM, 1), second)
        r_.dproj[:, 128:256] = key.astype(BF16)
        r_.dproj[:, 256:384] = value.astype(BF16)
        after_keys()
        query_copy.wait_recv()
        r_.dproj[:, 0:128] += r_.dqi[layer]

        def input_part(part):
            xhat, _ = normed(r_.xg[layer, part].astype(F32))
            grad = dot_nt(r_.dproj[span(part, OWN), :], r_.watt[layer])
            add_vector(layer, 0, xhat * grad)
            add_vector(layer, 2, grad)
            return r_.dxh[part] + grad * vector(layer, 0)

        scatters = []
        for r in range(1, NTP):
            r_.dxs[layer, r - 1] = input_part(ring(r)).astype(BF16)
            item = copy(
                f"dx{layer}",
                r_.dxs.at[layer, r - 1],
                r_.dxr.at[layer, r - 1],
                at_tp(ring(r)),
                r - 1,
            )
            scatters.append(start(item))
        total = input_part(t)
        bias_sum = jnp.sum(r_.dproj[...].astype(F32), axis=0, keepdims=True)
        r_.gv[layer, 6:7, 0:384] = bias_sum
        terms = dot_tn(r_.dproj[...], r_.ain[...].reshape(BLK, D))
        r_.gwq[layer, 128:, :] = terms.astype(BF16)
        before_end()
        for r, item in enumerate(scatters):
            item.wait_recv()
            total = total + r_.dxr[layer, r].astype(F32)
        xhat, inverse = normed(r_.xown[layer].astype(F32))
        along = jnp.mean(total * xhat, axis=-1, keepdims=True)
        centred = total - jnp.mean(total, axis=-1, keepdims=True) - xhat * along
        r_.go[layer] = (r_.gown[layer].astype(F32) + centred * inverse).astype(BF16)


    def cross_copy(which, layer):
        src = (r_.gwp, r_.gwq, r_.gv)[which].at[layer]
        return copy("cross", src, (r_.crp, r_.crq, r_.crv)[which], core, which)

    def cross_start(which, layer):
        @pl.when(s != layer)
        def _():
            cross_copy(which, layer).start()

    wide_parts = (
        (r_.gwp, r_.crp, r_.sump, r_.inp, r_.out_p, "ps", "pg", 64),
        (r_.gwq, r_.crq, r_.sumq, r_.inq, r_.out_q, "qs", "qg", 32),
    )

    def scatter_copy(which, r):
        _, _, sums, arrived, _, kind, _, _ = wide_parts[which]
        d = wrap(c + r, NCTX)
        return copy(kind, sums.at[d], arrived.at[r], at_ctx(d), r)

    def gather_copy(which, r):
        _, _, _, _, full, _, kind, _ = wide_parts[which]
        return copy(kind, full.at[c], full.at[c], at_ctx(wrap(c + r, NCTX)), r)

    def scatter_terms(which, layer):
        terms, crossed, sums, _, _, _, _, chunk = wide_parts[which]

        @pl.when(s == layer)
        def _():
            cross_copy(which, layer).wait_recv()

            @pl.loop(0, NCTX)
            def _(j):
                rows = span(j, chunk)
                pair = terms[layer, rows, :].astype(F32) + crossed[rows, :].astype(F32)
                sums[j] = pair.astype(BF16)

            @pl.loop(1, NCTX)
            def _(r):
                scatter_copy(which, r).start()

    def gather_sums(which, layer):
        _, _, sums, arrived, full, _, _, _ = wide_parts[which]

        @pl.when(s == layer)
        def _():
            total = sums[c].astype(F32)
            for r in range(1, NCTX):
                scatter_copy(which, r).wait_recv()
                total = total + arrived[r].astype(F32)
            full[c] = total.astype(BF16)

            @pl.loop(1, NCTX)
            def _(r):
                gather_copy(which, r).start()

    def await_sums(which, layer):
        _, _, _, _, full, _, kind, _ = wide_parts[which]

        @pl.when(s == layer)
        def _():
            @pl.loop(1, NCTX)
            def _(r):
                source = wrap(c + NCTX - r, NCTX)
                copy(kind, full.at[c], full.at[source], core, r).wait_recv()

    def vector_copy(r):
        return copy("vc", r_.vec, r_.vec_in.at[r], at_ctx(wrap(c + r, NCTX)), r)

    def vector_tp_copy(r):
        return copy("vt", r_.vec_tp, r_.vec_tp_in.at[r - 1], at_tp(ring(r)), r - 1)

    def vector_first(layer):
        @pl.when(s == layer)
        def _():
            cross_copy(2, layer).wait_recv()
            r_.vec[...] = r_.gv[layer] + r_.crv[...]

            @pl.loop(1, NCTX)
            def _(r):
                vector_copy(r).start()

    def vector_second(layer):
        @pl.when(s == layer)
        def _():
            total = r_.vec[...]
            for r in range(1, NCTX):
                vector_copy(r).wait_recv()
                total = total + r_.vec_in[r]
            r_.vec_tp[...] = total
            for r in range(1, NTP):
                vector_tp_copy(r).start()

    def vector_last(layer):
        @pl.when(s == layer)
        def _():
            total = r_.vec_tp[...]
            shared = total
            for r in range(1, NTP):
                vector_tp_copy(r).wait_recv()
                shared = shared + r_.vec_tp_in[r - 1]
            r_.out_gain[0] = shared[0:2, :]
            r_.out_norm_bias[0] = shared[2:4, :]
            r_.out_branch[...] = shared[4:5, :]
            r_.out_up_bias[...] = total[5:6, :]
            for k in range(3):
                bias = total[6:7, k * LANES : (k + 1) * LANES]
                r_.out_att_bias[0, k : k + 1, :] = bias


    def nothing():
        pass

    def wait_first_weights():
        for load in loads:
            load.wait()
        for item in weight_copies[:4]:
            item.wait_recv()

    wo_copies, g_copies = [], []

    def start_later_gathers():
        for r in range(1, NTP):
            item = copy("wo", r_.own_wo.at[0], r_.wo.at[s, t], at_tp(ring(r)), r - 1)
            wo_copies.append(start(item))
        g_copies.extend(gather_rows("g1", r_.gown.at[1], r_.gg.at[1]))
        for item in weight_copies[4:]:
            item.wait_recv()

    def pass_output_weight():
        for item in wo_copies:
            item.wait_recv()
        start(wo_pass)

    wo_pass = copy("wo_pass", r_.wo.at[s], r_.wo.at[s], core)
    forward(
        0,
        x_copies,
        wait_first_weights,
        start_later_gathers,
        pass_output_weight,
        wo_pass.wait_recv,
    )
    r_.xown[1] = r_.fo[0]
    x_copies = gather_rows("x1", r_.xown.at[1], r_.xg.at[1])
    grad_copies = send_attention_grads(1)

    def feed_ahead():
        feed_backward(1, g_copies)
        cross_start(0, 1)

    forward(1, x_copies, nothing, nothing, feed_ahead, nothing)

    rows_copy = start(copy("rows", r_.fo.at[1 - s], r_.out_rows.at[0, s], core))
    r_.out_rows[0, s] = r_.fo[s]

    def late_sums(layer):
        cross_start(1, layer)
        cross_start(2, layer)

    backward(
        1,
        grad_copies,
        lambda: scatter_terms(0, 1),
        nothing,
        lambda: gather_sums(0, 1),
        nothing,
        lambda: late_sums(1),
    )
    r_.gown[0] = r_.go[1]
    grad_copies = send_attention_grads(0)
    g_copies = gather_rows("g0", r_.gown.at[0], r_.gg.at[0])

    def finish_second():
        scatter_terms(1, 1)
        vector_first(1)

    def feed_last():
        feed_backward(0, g_copies)
        cross_start(0, 0)

    def sums_beside():
        scatter_terms(0, 0)
        gather_sums(1, 1)
        vector_second(1)

    def before_last():
        late_sums(0)
        scatter_terms(1, 0)
        vector_first(0)

    backward(
        0,
        grad_copies,
        finish_second,
        feed_last,
        sums_beside,
        lambda: gather_sums(0, 0),
        before_last,
    )
    grads_copy = start(copy("grads", r_.go.at[1 - s], r_.out_grads.at[0, s], core))
    r_.out_grads[0, s] = r_.go[s]
    gather_sums(1, 0)
    vector_second(0)
    for layer in (1, 0):
        await_sums(0, layer)
        vector_last(layer)
        await_sums(1, layer)
    rows_copy.wait_recv()
    grads_copy.wait_recv()


    for item in sent:
        item.wait_send()
    for layer in range(2):

        @pl.loop(1, NCTX)
        def _(r):
            wanted, item = key_send(layer, r - 1)

            @pl.when(wanted)
            def _():
                item.wait_send()

            key_block = wrap(c + r, NCTX)

            @pl.when(key_block <= top_block(c))
            def _():
                key_grad_send(layer, key_block).wait_send()

        @pl.when(s != layer)
        def _():
            for which in range(3):
                cross_copy(which, layer).wait_send()

    @pl.loop(1, NCTX)
    def _(r):
        for which in range(2):
            scatter_copy(which, r).wait_send()
            gather_copy(which, r).wait_send()
        vector_copy(r).wait_send()

    for r in range(1, NTP):
        vector_tp_copy(r).wait_send()


def run_step(operands):
    vmem = pl.BlockSpec(memory_space=pltpu.VMEM)
    dma = pltpu.SemaphoreType.DMA
    return pl.pallas_call(
        step_kernel,
        out_shape=[jax.ShapeDtypeStruct(shape, kind) for _, shape, kind in OUTPUTS],
        in_specs=[pl.BlockSpec(memory_space=space) for _, space in INPUTS],
        out_specs=[vmem] * len(OUTPUTS),
        scratch_shapes=[pltpu.VMEM(shape, kind) for _, shape, kind in SCRATCH]
        + [dma((COPIES,)), dma((COPIES,)), dma((6,))],
        compiler_params=pltpu.CompilerParams(
            collective_id=0, has_side_effects=True, vmem_limit_bytes=VMEM_LIMIT
        ),
        name="train_step",
    )(*operands)


RESULTS = (
    ((1, 2, OWN, D), BF16),
    ((1, 2, OWN, D), BF16),
    ((1, 2, D), F32),
    ((1, 2, D), F32),
    ((1, 3, D, OWN), F32),
    ((1, 3, OWN), F32),
    ((1, OWN, D), F32),
    ((1, D, D), F32),
    ((1, D), F32),
    ((1, D, D), F32),
    ((1, D), F32),
)


def hand_over_kernel(
    rows_in, grads_in, gain_in, norm_bias_in, p_in, q_in, att_bias_in, up_bias_in, branch_in, *results
):
    rows, grads, gain, norm_bias, att, att_bias, wo, up, up_bias, dn, branch = results
    rows[...] = rows_in[...]
    grads[...] = grads_in[...]
    gain[...] = gain_in[...]
    norm_bias[...] = norm_bias_in[...]
    att_bias[...] = att_bias_in[...]
    up_bias[...] = up_bias_in[...]
    branch[...] = branch_in[...]
    up[0] = p_in[0:8].astype(F32).reshape(D, D)
    dn[0] = p_in[8:16].astype(F32).reshape(D, D)
    wo[0] = q_in[0:4].astype(F32).reshape(OWN, D)
    turned = q_in[4:16].astype(F32).reshape(384, D).T
    for k in range(3):
        att[0, k] = turned[:, k * LANES : (k + 1) * LANES]


def hand_over(arrays):
    vmem = pl.BlockSpec(memory_space=pltpu.VMEM)
    return pl.pallas_call(
        hand_over_kernel,
        out_shape=[jax.ShapeDtypeStruct(shape, kind) for shape, kind in RESULTS],
        in_specs=[vmem] * len(arrays),
        out_specs=[vmem] * len(RESULTS),
        compiler_params=pltpu.CompilerParams(vmem_limit_bytes=VMEM_LIMIT),
        name="hand_over",
    )(*arrays)


def local(
    block_input,
    output_grad,
    sequence_lengths,
    norm_gain,
    norm_bias,
    attention_weight,
    attention_bias,
    output_weight,
    up_weight,
    up_bias,
    down_weight,
    branch_bias,
):
    results = run_step(
        (
            block_input,
            output_grad,
            sequence_lengths,
            norm_gain,
            norm_bias,
            attention_weight,
            attention_bias,
            output_weight,
            up_weight,
            up_bias,
            down_weight,
            branch_bias,
        )
    )
    return tuple(hand_over(results))


def solution(mesh):
    placed = (
        P(None, ("ctx", "tp"), None),
        P(None, ("ctx", "tp"), None),
        P(),
        P("section", None, None),
        P("section", None, None),
        P("section", None, None, "tp"),
        P("section", None, "tp"),
        P("section", "tp", None),
        P("section", None, "tp"),
        P("section", "tp"),
        P("section", "tp", None),
        P("section", None),
    )
    return jax.shard_map(
        local,
        mesh=mesh,
        in_specs=placed,
        out_specs=(
            P("section", None, ("ctx", "tp"), None),
            P("section", None, ("ctx", "tp"), None),
            P("section", None, None),
            P("section", None, None),
            P("section", None, None, "tp"),
            P("section", None, "tp"),
            P("section", "tp", None),
            P("section", None, "tp"),
            P("section", "tp"),
            P("section", "tp", None),
            P("section", None),
        ),
        check_vma=False,
    )
```

```python
from types import SimpleNamespace

import jax
import jax.numpy as jnp
from jax import lax
from jax.experimental import pallas as pl
from jax.experimental.pallas import tpu as pltpu
from jax.sharding import PartitionSpec as P

HEAD_DIM = 64
ROT = 16
MESH = pl.DeviceIdType.MESH
F32 = jnp.float32
BF16 = jnp.bfloat16
VMEM_LIMIT = 56 * 1024 * 1024
NCTX = 16
NTP = 4
BLK = 512
OWN = 128
D = 512
LANES = 128
STEPS = (
    (0, 1), (1, 0), (0, 3), (3, 0), (1, 1), (3, 3), (1, 3), (3, 1),
    (0, 2), (2, 0), (1, 2), (3, 2), (2, 1), (2, 3), (2, 2),
)
AHEAD = 8
MASKED = -1e30
LOWEST = -1e29


def dot_nn(a, b):
    return lax.dot_general(a, b, (((1,), (0,)), ((), ())), preferred_element_type=F32)


def dot_nt(a, b):
    return lax.dot_general(a, b, (((1,), (1,)), ((), ())), preferred_element_type=F32)


def dot_tn(a, b):
    return lax.dot_general(a, b, (((0,), (0,)), ((), ())), preferred_element_type=F32)


def phi(v):
    return 0.5 * (1.0 + lax.erf(v * (0.5**0.5)))


def gelu(v):
    return v * phi(v)


def gelu_slope(v):
    return phi(v) + v * jnp.exp(-0.5 * v * v) * 0.3989422804014327


def normed(rows):
    centre = rows - jnp.mean(rows, axis=-1, keepdims=True)
    spread = jnp.mean(centre * centre, axis=-1, keepdims=True)
    inverse = lax.rsqrt(spread + 1e-05)
    return centre * inverse, inverse


def remote(src, dst, send, recv, peer):
    return pltpu.make_async_remote_copy(
        src_ref=src, dst_ref=dst, send_sem=send, recv_sem=recv, device_id=peer, device_id_type=MESH
    )


def lanes(shape):
    return lax.broadcasted_iota(jnp.int32, shape, 1)


def turn(tile, cosine, sine):
    back = pltpu.roll(tile, LANES - 8, 1)
    ahead = pltpu.roll(tile, 8, 1)
    other = jnp.where(lanes(tile.shape) % HEAD_DIM < 8, back, ahead)
    return tile * cosine + other * sine


def turn_left(tile, cosine, sine):
    return jnp.where(lanes(tile.shape) < HEAD_DIM, turn(tile, cosine, sine), tile)


def my_head(tile, group, half):
    swapped = pltpu.roll(tile, HEAD_DIM, 1)
    chosen = jnp.where(group == half, tile, swapped)
    return jnp.where(lanes(tile.shape) // HEAD_DIM == half, chosen, 0.0)


def two_head_tile(rows, group):
    blank = jnp.zeros_like(rows)
    first = jnp.where(group == 0, rows, blank)
    second = jnp.where(group == 0, blank, rows)
    return jnp.concatenate([first, second], axis=0).T


def top_block(d):
    return jnp.maximum(d, NCTX - 1 - d)


def needs_mask(key_block, query_block):
    return (key_block == 0) | (key_block == query_block) | (query_block == NCTX - 1)


def wrap(index, count):
    return jnp.where(index >= count, index - count, index)


def stepped(c, index, sign):
    z, y = c // 4, c % 4
    dz, dy = 0, 0
    for k, (along_z, along_y) in enumerate(STEPS):
        dz = jnp.where(index == k, along_z, dz)
        dy = jnp.where(index == k, along_y, dy)
    return wrap(z + (dz if sign > 0 else 4 - dz), 4) * 4 + wrap(y + (dy if sign > 0 else 4 - dy), 4)


def second_group(d):
    return jnp.where(d >= NCTX // 2, 1, 0)


def span(index, size):
    return pl.ds(pl.multiple_of(index * size, size), size)


OUTPUTS = (
    ("out_rows", (1, 2, OWN, D), BF16),
    ("out_grads", (1, 2, OWN, D), BF16),
    ("out_gain", (1, 2, D), F32),
    ("out_norm_bias", (1, 2, D), F32),
    ("out_p", (NCTX, 64, D), BF16),
    ("out_q", (NCTX, 32, D), BF16),
    ("out_att_bias", (3, 1, OWN), F32),
    ("out_up_bias", (1, D), F32),
    ("out_branch", (1, D), F32),
)

SCRATCH = (
    ("watt", (2, D, 384), BF16),
    ("wo", (2, NTP, OWN, D), BF16),
    ("wup", (2, D, D), BF16),
    ("wdn", (2, D, D), BF16),
    ("vecs", (2, 8, D), F32),
    ("vown", (8, D), F32),
    ("place", (2, 2, BLK), jnp.int32),
    ("cosine", (2, BLK, LANES), F32),
    ("sine", (2, BLK, LANES), F32),
    ("xown", (2, OWN, D), BF16),
    ("fo", (2, OWN, D), BF16),
    ("xg", (2, NTP, OWN, D), BF16),
    ("qpad", (2, 2, BLK, LANES), BF16),
    ("kvall", (2, NCTX, BLK, LANES), BF16),
    ("ot", (2, 2, HEAD_DIM, BLK), F32),
    ("lse", (2, 2, 1, BLK), F32),
    ("hid", (2, NTP, OWN, D), BF16),
    ("kvs", (2, 2, BLK, LANES), BF16),
    ("qs", (2, BLK, LANES), BF16),
    ("qin", (2, BLK, LANES), BF16),
    ("oout", (2, 2, BLK, LANES), BF16),
    ("oin", (2, BLK, LANES), BF16),
    ("oa", (2, NTP, OWN, LANES), BF16),
    ("ob", (2, NTP, OWN, LANES), BF16),
    ("ffs", (2, NTP - 1, OWN, D), BF16),
    ("ffr", (2, NTP - 1, OWN, D), BF16),
    ("gown", (2, OWN, D), BF16),
    ("go", (2, OWN, D), BF16),
    ("gg", (2, NTP, OWN, D), BF16),
    ("dos", (2, NTP, OWN, LANES), BF16),
    ("doa", (2, NTP, OWN, LANES), BF16),
    ("dob", (2, NTP, OWN, LANES), BF16),
    ("dkvo", (2, NCTX, BLK, LANES), BF16),
    ("dkvi", (2, NCTX, BLK, LANES), BF16),
    ("dqs", (2, BLK, LANES), BF16),
    ("dqi", (2, BLK, LANES), BF16),
    ("dxs", (2, NTP - 1, OWN, D), BF16),
    ("dxr", (2, NTP - 1, OWN, D), BF16),
    ("gwp", (2, 2 * D, D), BF16),
    ("gwq", (2, D, D), BF16),
    ("gv", (2, 8, D), F32),
    ("kvt", (LANES, BLK), BF16),
    ("acc", (2, LANES, BLK), F32),
    ("top", (2, 1, BLK), F32),
    ("ffo", (OWN, D), F32),
    ("dopad", (2, BLK, LANES), BF16),
    ("delta", (2, 1, BLK), F32),
    ("dqt", (2, LANES, BLK), F32),
    ("dkva", (BLK, LANES), F32),
    ("ain", (NTP, OWN, D), BF16),
    ("fin", (NTP, OWN, D), BF16),
    ("ugs", (NTP, OWN, D), BF16),
    ("dxh", (NTP, OWN, D), F32),
    ("dproj", (BLK, 384), BF16),
    ("crp", (2 * D, D), BF16),
    ("crq", (D, D), BF16),
    ("crv", (8, D), F32),
    ("sump", (NCTX, 64, D), BF16),
    ("sumq", (NCTX, 32, D), BF16),
    ("inp", (NCTX, 64, D), BF16),
    ("inq", (NCTX, 32, D), BF16),
    ("vec", (8, D), F32),
    ("vec_in", (NCTX, 8, D), F32),
    ("vec_tp", (8, D), F32),
    ("vec_tp_in", (NTP - 1, 8, D), F32),
)

INPUTS = (
    ("xin", pltpu.VMEM),
    ("gin", pltpu.VMEM),
    ("lengths", pltpu.SMEM),
    ("gains", pltpu.VMEM),
    ("biases", pltpu.VMEM),
    ("own_watt", pl.ANY),
    ("att_bias", pltpu.VMEM),
    ("own_wo", pl.ANY),
    ("own_wup", pl.ANY),
    ("up_bias", pltpu.VMEM),
    ("own_wdn", pl.ANY),
    ("branch_bias", pltpu.VMEM),
)

SEMAPHORES = {}
COPIES = 0
for name, count in (
    ("weights", 6),
    ("wo", 3),
    ("wo_pass", 1),
    ("rows", 1),
    ("grads", 1),
    ("cross", 3),
    ("ps", NCTX),
    ("pg", NCTX),
    ("qs", NCTX),
    ("qg", NCTX),
    ("vc", NCTX),
    ("vt", 3),
) + tuple(
    (f"{kind}{layer}", count)
    for layer in range(2)
    for kind, count in (
        ("x", 3),
        ("kv", NCTX),
        ("q", 1),
        ("oa", 3),
        ("ob", 4),
        ("ow", 1),
        ("ff", 3),
        ("g", 3),
        ("doa", 3),
        ("dob", 4),
        ("dkv", NCTX),
        ("dq", 1),
        ("dx", 3),
    )
):
    SEMAPHORES[name] = COPIES
    COPIES += count


def step_kernel(*refs):
    names = tuple(n for n, _ in INPUTS) + tuple(n for n, _, _ in OUTPUTS) + tuple(n for n, _, _ in SCRATCH)
    r_ = SimpleNamespace(**dict(zip(names, refs)))
    send_sems, recv_sems, load_sems = refs[len(names) :]
    s = lax.axis_index("section")
    c = lax.axis_index("ctx")
    t = lax.axis_index("tp")
    group = second_group(c)
    partner = NCTX - 1 - c
    core = {"section": 1 - s, "ctx": c, "tp": t}

    def at_ctx(d):
        return {"section": s, "ctx": d, "tp": t}

    def at_tp(d):
        return {"section": s, "ctx": c, "tp": d}

    def at_partner(d):
        return {"section": s, "ctx": partner, "tp": d}

    def ring(r):
        return wrap(t + r, NTP)

    def copy(kind, src, dst, peer, send=0, recv=None):
        base = SEMAPHORES[kind]
        recv = send if recv is None else recv
        return remote(src, dst, send_sems.at[base + send], recv_sems.at[base + recv], peer)

    sent = []

    def start(item):
        item.start()
        sent.append(item)
        return item

    def start_all(items):
        return [start(item) for item in items]

    peers = [core]
    peers += [at_tp(ring(r)) for r in range(1, NTP)]
    peers += [at_ctx(wrap(c + r, NCTX)) for r in range(1, NCTX)]
    peers += [at_partner(ring(r)) for r in range(1, NTP)]
    barrier = pltpu.get_barrier_semaphore()
    for peer in peers:
        pl.semaphore_signal(barrier, inc=1, device_id=peer, device_id_type=MESH)

    own_weights = [
        (r_.own_watt.at[0, k], r_.watt.at[s, :, k * LANES : (k + 1) * LANES]) for k in range(3)
    ]
    own_weights += [(r_.own_wup.at[0], r_.wup.at[s]), (r_.own_wdn.at[0], r_.wdn.at[s])]
    loads = [
        pltpu.make_async_copy(src, dst, load_sems.at[i])
        for i, (src, dst) in enumerate(own_weights + [(r_.own_wo.at[0], r_.wo.at[s, t])])
    ]
    for load in loads:
        load.start()
    r_.vown[...] = jnp.zeros((8, D), F32)
    r_.vown[0:2, :] = r_.gains[0]
    r_.vown[2:4, :] = r_.biases[0]
    r_.vown[4:5, :] = r_.branch_bias[...]
    r_.vown[5:6, :] = r_.up_bias[...]
    for k in range(3):
        r_.vown[6:7, k * LANES : (k + 1) * LANES] = r_.att_bias[k]
    r_.vecs[s] = r_.vown[...]
    r_.xown[0] = r_.xin[s]
    r_.gown[1] = r_.gin[s]
    pl.semaphore_wait(barrier, len(peers))

    def gather_rows(kind, own, full):
        full[t] = own[...]
        return start_all(
            [copy(kind, own, full.at[t], at_tp(ring(r)), r - 1) for r in range(1, NTP)]
        )

    x_copies = gather_rows("x0", r_.xown.at[0], r_.xg.at[0])
    weight_copies = start_all(
        [
            copy("weights", src, dst, core, i)
            for i, (src, dst) in enumerate([(r_.vown, r_.vecs.at[s])] + own_weights)
        ]
    )

    rate_row = lax.broadcasted_iota(jnp.int32, (ROT // 2, 1), 0)
    rates = jnp.zeros((ROT // 2, 1), F32)
    for i in range(ROT // 2):
        rates = jnp.where(rate_row == i, 1.0 / 10000.0 ** (2 * i / ROT), rates)
    for slot, block in ((0, c), (1, partner)):
        place = block * BLK + lanes((1, BLK))
        first = jnp.zeros((1, BLK), jnp.int32)
        end = 0
        for k in range(r_.lengths.shape[1]):
            length = jnp.where(s == 0, r_.lengths[0, k], r_.lengths[1, k])
            end = end + length
            first = first + jnp.where(place >= end, length, 0)
        r_.place[slot, 0:1, :] = place
        r_.place[slot, 1:2, :] = first
        angles = (place - first).astype(F32) * rates
        cosine, sine = jnp.cos(angles), jnp.sin(angles)
        still = jnp.zeros((HEAD_DIM - ROT, BLK), F32)
        cosine = jnp.concatenate([cosine, cosine, still + 1.0], axis=0)
        sine = jnp.concatenate([-sine, sine, still], axis=0)
        r_.cosine[slot] = jnp.concatenate([cosine, cosine], axis=0).T
        r_.sine[slot] = jnp.concatenate([sine, sine], axis=0).T

    def vector(layer, row, width=D):
        return r_.vecs[layer, row : row + 1, 0:width]

    def norm_outputs(layer, xhat):
        first = xhat * vector(layer, 0) + vector(layer, 2)
        second = xhat * vector(layer, 1) + vector(layer, 3)
        return first.astype(BF16), second.astype(BF16)

    def key_mask(key_block, shape, slot):
        key = key_block * BLK + lax.broadcasted_iota(jnp.int32, shape, 0)
        return (key <= r_.place[slot, 0:1, :]) & (key >= r_.place[slot, 1:2, :])

    def visit_both(key_block, visit):
        @pl.loop(0, 2)
        def _(slot):
            query_block = jnp.where(slot == 0, c, partner)
            reached = key_block <= query_block
            edge = needs_mask(key_block, query_block)

            @pl.when(reached & edge)
            def _():
                visit(key_block, slot, True)

            @pl.when(reached & jnp.logical_not(edge))
            def _():
                visit(key_block, slot, False)


    def key_send(layer, index, part=None):
        d = stepped(c, index, 1)
        rows = pl.ds(0, BLK) if part is None else span(part, OWN)
        return c <= top_block(d), copy(
            f"kv{layer}",
            r_.kvs.at[layer, second_group(d), rows, :],
            r_.kvall.at[layer, c, rows, :],
            at_ctx(d),
            d,
            c,
        )

    def forward(layer, gathers, before_keys, after_keys, beside_keys, before_out):
        def project(part):
            xhat, _ = normed(r_.xg[layer, part].astype(F32))
            attention_in, _ = norm_outputs(layer, xhat)
            pre = dot_nn(attention_in, r_.watt[layer]) + vector(layer, 6, 384)
            rows = span(part, OWN)
            cosine, sine = r_.cosine[0, rows, :], r_.sine[0, rows, :]
            query = turn(pre[:, 0:128], cosine, sine) * 0.125
            r_.qs[layer, rows, :] = query.astype(BF16)
            key, value = turn(pre[:, 128:256], cosine, sine), pre[:, 256:384]
            left = lanes(key.shape) < HEAD_DIM
            first = jnp.where(left, key, pltpu.roll(value, HEAD_DIM, 1))
            second = jnp.where(left, pltpu.roll(key, HEAD_DIM, 1), value)
            r_.kvs[layer, 0, rows, :] = first.astype(BF16)
            r_.kvs[layer, 1, rows, :] = second.astype(BF16)

            copy(
                f"q{layer}",
                r_.qs.at[layer, rows, :],
                r_.qin.at[layer, rows, :],
                at_ctx(partner),
            ).start()

            @pl.loop(0, AHEAD)
            def _(index):
                send_keys(index, part)

        def send_keys(index, part=None):
            wanted, item = key_send(layer, index, part)

            @pl.when(wanted)
            def _():
                item.start()

        before_keys()
        project(t)
        for r, item in enumerate(gathers):
            item.wait_recv()
            project(wrap(t + NTP - 1 - r, NTP))

        query_copy = copy(f"q{layer}", r_.qs.at[layer], r_.qin.at[layer], at_ctx(partner))
        sent.append(query_copy)

        r_.kvall[layer, c] = r_.kvs[layer, group]
        after_keys()

        def feed_forward(part):
            xhat, _ = normed(r_.xg[layer, part].astype(F32))
            _, feed_in = norm_outputs(layer, xhat)
            hidden = gelu(dot_nn(feed_in, r_.wup[layer]) + vector(layer, 5)).astype(BF16)
            r_.hid[layer, part] = hidden
            return dot_nn(hidden, r_.wdn[layer])

        def feed_send(r):
            return copy(
                f"ff{layer}",
                r_.ffs.at[layer, r - 1],
                r_.ffr.at[layer, r - 1],
                at_tp(ring(r)),
                r - 1,
            )

        feed_copies = [feed_send(r) for r in range(1, NTP)]
        sent.extend(feed_copies)

        def feed_all():
            @pl.loop(1, NTP)
            def _(r):
                r_.ffs[layer, r - 1] = feed_forward(ring(r)).astype(BF16)
                feed_send(r).start()

            r_.ffo[...] = feed_forward(t)

        r_.qpad[layer, 0] = my_head(r_.qs[layer].astype(F32), group, 0).astype(BF16)
        query_copy.wait_recv()
        r_.qpad[layer, 1] = my_head(r_.qin[layer].astype(F32), group, 0).astype(BF16)
        r_.acc[...] = jnp.zeros_like(r_.acc)
        r_.top[...] = jnp.full_like(r_.top, LOWEST)

        def visit(key_block, slot, masked):
            scores = dot_nt(r_.kvall[layer, key_block], r_.qpad[layer, slot])
            if masked:
                scores = jnp.where(key_mask(key_block, scores.shape, slot), scores, MASKED)
            old = r_.top[slot]
            new = jnp.maximum(old, jnp.max(scores, axis=0, keepdims=True))
            weights = jnp.exp(scores - new).astype(BF16)
            r_.top[slot] = new
            r_.acc[slot] = r_.acc[slot] * jnp.exp(old - new) + dot_nn(r_.kvt[...], weights)

        @pl.loop(0, NCTX)
        def _(r):
            key_block = jnp.where(r == 0, c, stepped(c, r - 1, -1))

            @pl.when((r > 0) & (r + AHEAD < NCTX))
            def _():
                send_keys(r + AHEAD - 1)

            @pl.when(r == 1)
            def _():
                feed_all()

            @pl.when(r == 6)
            def _():
                beside_keys()

            @pl.when(key_block <= top_block(c))
            def _():
                @pl.when(r > 0)
                def _():
                    copy(
                        f"kv{layer}",
                        r_.kvs.at[layer, 0],
                        r_.kvall.at[layer, key_block],
                        at_ctx(partner),
                        0,
                        key_block,
                    ).wait_recv()

                turned = r_.kvall[layer, key_block].astype(F32).T
                row = lax.broadcasted_iota(jnp.int32, turned.shape, 0)
                r_.kvt[...] = jnp.where(row < HEAD_DIM, 1.0, turned).astype(BF16)
                visit_both(key_block, visit)

        def finish(slot):
            total = r_.acc[slot, 0:HEAD_DIM, :]
            mean = r_.acc[slot, HEAD_DIM:, :] / total
            r_.ot[layer, slot] = mean
            r_.lse[layer, slot] = r_.top[slot] + jnp.log(total[0:1])
            r_.oout[layer, slot] = two_head_tile(mean, group).astype(BF16)

        finish(1)
        far = start_all(
            [
                copy(
                    f"ob{layer}",
                    r_.oout.at[layer, 1, span(ring(r), OWN), :],
                    r_.ob.at[layer, t],
                    at_partner(ring(r)),
                    r,
                )
                for r in range(NTP)
            ]
        )
        finish(0)
        near = start_all(
            [
                copy(
                    f"oa{layer}",
                    r_.oout.at[layer, 0, span(ring(r), OWN), :],
                    r_.oa.at[layer, t],
                    at_tp(ring(r)),
                    r - 1,
                )
                for r in range(1, NTP)
            ]
        )
        r_.oa[layer, t] = r_.oout[layer, 0, span(t, OWN), :]
        start(copy(f"ow{layer}", r_.oout.at[layer, 1], r_.oin.at[layer], at_ctx(partner)))

        result = r_.xown[layer].astype(F32) + vector(layer, 4) + r_.ffo[...]
        for r, item in enumerate(feed_copies):
            item.wait_recv()
            result = result + r_.ffr[layer, r].astype(F32)
        for item in far + near:
            item.wait_recv()
        before_out()
        heads = jnp.concatenate(
            [r_.oa[layer, p] + r_.ob[layer, p] for p in range(NTP)], axis=1
        )
        result = result + dot_nn(heads, r_.wo[layer].reshape(D, D))
        r_.fo[layer] = result.astype(BF16)


    def send_attention_grads(layer):
        tile = dot_nt(r_.gown[layer], r_.wo[layer].reshape(D, D)).astype(BF16)
        for p in range(NTP):
            r_.dos[layer, p] = tile[:, p * LANES : (p + 1) * LANES]
        far = start_all(
            [
                copy(
                    f"dob{layer}",
                    r_.dos.at[layer, ring(r)],
                    r_.dob.at[layer, t],
                    at_partner(ring(r)),
                    r,
                )
                for r in range(NTP)
            ]
        )
        near = start_all(
            [
                copy(
                    f"doa{layer}",
                    r_.dos.at[layer, ring(r)],
                    r_.doa.at[layer, t],
                    at_tp(ring(r)),
                    r - 1,
                )
                for r in range(1, NTP)
            ]
        )
        r_.doa[layer, t] = r_.dos[layer, t]
        return near + far

    def key_grad_send(layer, key_block):
        return copy(
            f"dkv{layer}",
            r_.dkvo.at[layer, key_block],
            r_.dkvi.at[layer, c],
            at_ctx(key_block),
            key_block,
            c,
        )

    def add_vector(layer, row, value):
        r_.gv[layer, row : row + 1, :] += jnp.sum(value, axis=0, keepdims=True)

    def feed_backward(layer, gathers):
        for item in gathers:
            item.wait_recv()
        r_.gv[layer] = jnp.zeros((8, D), F32)
        own_sum = jnp.sum(r_.gown[layer].astype(F32), axis=0, keepdims=True)
        r_.gv[layer, 4:5, :] = own_sum

        @pl.loop(0, NTP)
        def _(part):
            xhat, _ = normed(r_.xg[layer, part].astype(F32))
            attention_in, feed_in = norm_outputs(layer, xhat)
            r_.ain[part] = attention_in
            r_.fin[part] = feed_in
            up_pre = dot_nn(feed_in, r_.wup[layer]) + vector(layer, 5)
            hidden_grad = dot_nt(r_.gg[layer, part], r_.wdn[layer])
            up_grad = (hidden_grad * gelu_slope(up_pre)).astype(BF16)
            r_.ugs[part] = up_grad
            add_vector(layer, 5, up_grad.astype(F32))
            feed_grad = dot_nt(up_grad, r_.wup[layer])
            add_vector(layer, 1, xhat * feed_grad)
            add_vector(layer, 3, feed_grad)
            r_.dxh[part] = feed_grad * vector(layer, 1)

        full_grad = r_.gg[layer].reshape(BLK, D)
        up_terms = dot_tn(r_.fin[...].reshape(BLK, D), r_.ugs[...].reshape(BLK, D))
        r_.gwp[layer, 0:D, :] = up_terms.astype(BF16)
        r_.gwp[layer, D:, :] = dot_tn(r_.hid[layer].reshape(BLK, D), full_grad).astype(BF16)

    def backward(layer, grad_copies, before_keys, among_keys, beside_keys, after_keys, before_end):
        before_keys()
        for item in grad_copies:
            item.wait_recv()

        def prepare(slot, tile):
            padded = my_head(tile.reshape(BLK, LANES).astype(F32), group, 1)
            r_.dopad[slot] = padded.astype(BF16)
            r_.delta[slot] = jnp.sum(
                padded.T[HEAD_DIM:, :] * r_.ot[layer, slot], axis=0, keepdims=True
            )

        prepare(0, r_.doa[layer])
        prepare(1, r_.dob[layer])
        r_.dqt[...] = jnp.zeros_like(r_.dqt)

        def visit(key_block, slot, masked):
            keys = r_.kvall[layer, key_block]
            queries, grads = r_.qpad[layer, slot], r_.dopad[slot]
            scores = dot_nt(keys, queries)
            weights = jnp.exp(scores - r_.lse[layer, slot])
            if masked:
                weights = jnp.where(key_mask(key_block, scores.shape, slot), weights, 0.0)
            weight_grad = dot_nt(keys, grads)
            score_grad = (weights * (weight_grad - r_.delta[slot])).astype(BF16)
            r_.dkva[...] += dot_nn(weights.astype(BF16), grads) + dot_nn(score_grad, queries)
            r_.dqt[slot] += dot_nn(r_.kvt[...], score_grad)

        @pl.loop(0, NCTX)
        def _(r):
            key_block = jnp.where(r == NCTX - 1, c, stepped(c, r, 1))

            @pl.when(r == AHEAD)
            def _():
                among_keys()

            @pl.when(key_block <= top_block(c))
            def _():
                r_.kvt[...] = r_.kvall[layer, key_block].astype(F32).T.astype(BF16)
                r_.dkva[...] = jnp.zeros_like(r_.dkva)
                visit_both(key_block, visit)
                r_.dkvo[layer, key_block] = r_.dkva[...].astype(BF16)

                @pl.when(r < NCTX - 1)
                def _():
                    key_grad_send(layer, key_block).start()

        def query_grad(slot):
            tile = two_head_tile(r_.dqt[slot, 0:HEAD_DIM, :] * 0.125, group)
            return turn(tile, r_.cosine[slot], -r_.sine[slot]).astype(BF16)

        r_.dqs[layer] = query_grad(1)
        query_copy = start(copy(f"dq{layer}", r_.dqs.at[layer], r_.dqi.at[layer], at_ctx(partner)))
        r_.dproj[:, 0:128] = query_grad(0)

        beside_keys()
        out_copy = copy(f"ow{layer}", r_.oout.at[layer, 1], r_.oin.at[layer], at_ctx(partner))
        out_copy.wait_recv()
        attention = r_.oout[layer, 0] + r_.oin[layer]
        full_grad = r_.gg[layer].reshape(BLK, D)
        r_.gwq[layer, 0:128, :] = dot_tn(attention, full_grad).astype(BF16)

        def key_grad(half):
            r_.dkva[...] = jnp.zeros_like(r_.dkva)

            @pl.loop(0, NCTX // 2)
            def _(step):
                source = half * (NCTX // 2) + step

                @pl.when(source == c)
                def _():
                    r_.dkva[...] += r_.dkvo[layer, c].astype(F32)

                @pl.when((c <= top_block(source)) & (source != c))
                def _():
                    copy(
                        f"dkv{layer}",
                        r_.dkvo.at[layer, 0],
                        r_.dkvi.at[layer, source],
                        at_ctx(partner),
                        0,
                        source,
                    ).wait_recv()
                    r_.dkva[...] += r_.dkvi[layer, source].astype(F32)

            return turn_left(r_.dkva[...], r_.cosine[0], -r_.sine[0])

        first, second = key_grad(0), key_grad(1)
        left = lanes(first.shape) < HEAD_DIM
        key = jnp.where(left, first, pltpu.roll(second, HEAD_DIM, 1))
        value = jnp.where(left, pltpu.roll(first, HEAD_DIM, 1), second)
        r_.dproj[:, 128:256] = key.astype(BF16)
        r_.dproj[:, 256:384] = value.astype(BF16)
        after_keys()
        query_copy.wait_recv()
        r_.dproj[:, 0:128] += r_.dqi[layer]

        def input_part(part):
            xhat, _ = normed(r_.xg[layer, part].astype(F32))
            grad = dot_nt(r_.dproj[span(part, OWN), :], r_.watt[layer])
            add_vector(layer, 0, xhat * grad)
            add_vector(layer, 2, grad)
            return r_.dxh[part] + grad * vector(layer, 0)

        scatters = []
        for r in range(1, NTP):
            r_.dxs[layer, r - 1] = input_part(ring(r)).astype(BF16)
            item = copy(
                f"dx{layer}",
                r_.dxs.at[layer, r - 1],
                r_.dxr.at[layer, r - 1],
                at_tp(ring(r)),
                r - 1,
            )
            scatters.append(start(item))
        total = input_part(t)
        bias_sum = jnp.sum(r_.dproj[...].astype(F32), axis=0, keepdims=True)
        r_.gv[layer, 6:7, 0:384] = bias_sum
        terms = dot_tn(r_.dproj[...], r_.ain[...].reshape(BLK, D))
        r_.gwq[layer, 128:, :] = terms.astype(BF16)
        before_end()
        for r, item in enumerate(scatters):
            item.wait_recv()
            total = total + r_.dxr[layer, r].astype(F32)
        xhat, inverse = normed(r_.xown[layer].astype(F32))
        along = jnp.mean(total * xhat, axis=-1, keepdims=True)
        centred = total - jnp.mean(total, axis=-1, keepdims=True) - xhat * along
        r_.go[layer] = (r_.gown[layer].astype(F32) + centred * inverse).astype(BF16)


    def cross_copy(which, layer):
        src = (r_.gwp, r_.gwq, r_.gv)[which].at[layer]
        return copy("cross", src, (r_.crp, r_.crq, r_.crv)[which], core, which)

    def cross_start(which, layer):
        @pl.when(s != layer)
        def _():
            cross_copy(which, layer).start()

    wide_parts = (
        (r_.gwp, r_.crp, r_.sump, r_.inp, r_.out_p, "ps", "pg", 64),
        (r_.gwq, r_.crq, r_.sumq, r_.inq, r_.out_q, "qs", "qg", 32),
    )

    def scatter_copy(which, r):
        _, _, sums, arrived, _, kind, _, _ = wide_parts[which]
        d = wrap(c + r, NCTX)
        return copy(kind, sums.at[d], arrived.at[r], at_ctx(d), r)

    def gather_copy(which, r):
        _, _, _, _, full, _, kind, _ = wide_parts[which]
        return copy(kind, full.at[c], full.at[c], at_ctx(wrap(c + r, NCTX)), r)

    def scatter_terms(which, layer):
        terms, crossed, sums, _, _, _, _, chunk = wide_parts[which]

        @pl.when(s == layer)
        def _():
            cross_copy(which, layer).wait_recv()

            @pl.loop(0, NCTX)
            def _(j):
                rows = span(j, chunk)
                pair = terms[layer, rows, :].astype(F32) + crossed[rows, :].astype(F32)
                sums[j] = pair.astype(BF16)

            @pl.loop(1, NCTX)
            def _(r):
                scatter_copy(which, r).start()

    def gather_sums(which, layer):
        _, _, sums, arrived, full, _, _, _ = wide_parts[which]

        @pl.when(s == layer)
        def _():
            total = sums[c].astype(F32)
            for r in range(1, NCTX):
                scatter_copy(which, r).wait_recv()
                total = total + arrived[r].astype(F32)
            full[c] = total.astype(BF16)

            @pl.loop(1, NCTX)
            def _(r):
                gather_copy(which, r).start()

    def await_sums(which, layer):
        _, _, _, _, full, _, kind, _ = wide_parts[which]

        @pl.when(s == layer)
        def _():
            @pl.loop(1, NCTX)
            def _(r):
                source = wrap(c + NCTX - r, NCTX)
                copy(kind, full.at[c], full.at[source], core, r).wait_recv()

    def vector_copy(r):
        return copy("vc", r_.vec, r_.vec_in.at[r], at_ctx(wrap(c + r, NCTX)), r)

    def vector_tp_copy(r):
        return copy("vt", r_.vec_tp, r_.vec_tp_in.at[r - 1], at_tp(ring(r)), r - 1)

    def vector_first(layer):
        @pl.when(s == layer)
        def _():
            cross_copy(2, layer).wait_recv()
            r_.vec[...] = r_.gv[layer] + r_.crv[...]

            @pl.loop(1, NCTX)
            def _(r):
                vector_copy(r).start()

    def vector_second(layer):
        @pl.when(s == layer)
        def _():
            total = r_.vec[...]
            for r in range(1, NCTX):
                vector_copy(r).wait_recv()
                total = total + r_.vec_in[r]
            r_.vec_tp[...] = total
            for r in range(1, NTP):
                vector_tp_copy(r).start()

    def vector_last(layer):
        @pl.when(s == layer)
        def _():
            total = r_.vec_tp[...]
            shared = total
            for r in range(1, NTP):
                vector_tp_copy(r).wait_recv()
                shared = shared + r_.vec_tp_in[r - 1]
            r_.out_gain[0] = shared[0:2, :]
            r_.out_norm_bias[0] = shared[2:4, :]
            r_.out_branch[...] = shared[4:5, :]
            r_.out_up_bias[...] = total[5:6, :]
            for k in range(3):
                bias = total[6:7, k * LANES : (k + 1) * LANES]
                r_.out_att_bias[k] = bias


    def nothing():
        pass

    def wait_first_weights():
        for load in loads:
            load.wait()
        for item in weight_copies[:4]:
            item.wait_recv()

    wo_copies, g_copies = [], []

    def start_later_gathers():
        for r in range(1, NTP):
            item = copy("wo", r_.own_wo.at[0], r_.wo.at[s, t], at_tp(ring(r)), r - 1)
            wo_copies.append(start(item))
        g_copies.extend(gather_rows("g1", r_.gown.at[1], r_.gg.at[1]))
        for item in weight_copies[4:]:
            item.wait_recv()

    def pass_output_weight():
        for item in wo_copies:
            item.wait_recv()
        start(wo_pass)

    wo_pass = copy("wo_pass", r_.wo.at[s], r_.wo.at[s], core)
    forward(
        0,
        x_copies,
        wait_first_weights,
        start_later_gathers,
        pass_output_weight,
        wo_pass.wait_recv,
    )
    r_.xown[1] = r_.fo[0]
    x_copies = gather_rows("x1", r_.xown.at[1], r_.xg.at[1])
    grad_copies = send_attention_grads(1)

    def feed_ahead():
        feed_backward(1, g_copies)
        cross_start(0, 1)

    forward(1, x_copies, nothing, nothing, feed_ahead, nothing)

    rows_copy = start(copy("rows", r_.fo.at[1 - s], r_.out_rows.at[0, s], core))
    r_.out_rows[0, s] = r_.fo[s]

    def late_sums(layer):
        cross_start(1, layer)
        cross_start(2, layer)

    backward(
        1,
        grad_copies,
        lambda: scatter_terms(0, 1),
        nothing,
        lambda: gather_sums(0, 1),
        nothing,
        lambda: late_sums(1),
    )
    r_.gown[0] = r_.go[1]
    grad_copies = send_attention_grads(0)
    g_copies = gather_rows("g0", r_.gown.at[0], r_.gg.at[0])

    def finish_second():
        scatter_terms(1, 1)
        vector_first(1)

    def feed_last():
        feed_backward(0, g_copies)
        cross_start(0, 0)

    def sums_beside():
        scatter_terms(0, 0)
        gather_sums(1, 1)
        vector_second(1)

    def before_last():
        late_sums(0)
        scatter_terms(1, 0)
        vector_first(0)

    backward(
        0,
        grad_copies,
        finish_second,
        feed_last,
        sums_beside,
        lambda: gather_sums(0, 0),
        before_last,
    )
    grads_copy = start(copy("grads", r_.go.at[1 - s], r_.out_grads.at[0, s], core))
    r_.out_grads[0, s] = r_.go[s]
    gather_sums(1, 0)
    vector_second(0)
    for layer in (1, 0):
        await_sums(0, layer)
        vector_last(layer)
        await_sums(1, layer)
    rows_copy.wait_recv()
    grads_copy.wait_recv()


    for item in sent:
        item.wait_send()
    for layer in range(2):

        @pl.loop(1, NCTX)
        def _(r):
            wanted, item = key_send(layer, r - 1)

            @pl.when(wanted)
            def _():
                item.wait_send()

            key_block = wrap(c + r, NCTX)

            @pl.when(key_block <= top_block(c))
            def _():
                key_grad_send(layer, key_block).wait_send()

        @pl.when(s != layer)
        def _():
            for which in range(3):
                cross_copy(which, layer).wait_send()

    @pl.loop(1, NCTX)
    def _(r):
        for which in range(2):
            scatter_copy(which, r).wait_send()
            gather_copy(which, r).wait_send()
        vector_copy(r).wait_send()

    for r in range(1, NTP):
        vector_tp_copy(r).wait_send()


def run_step(operands):
    vmem = pl.BlockSpec(memory_space=pltpu.VMEM)
    dma = pltpu.SemaphoreType.DMA
    return pl.pallas_call(
        step_kernel,
        out_shape=[jax.ShapeDtypeStruct(shape, kind) for _, shape, kind in OUTPUTS],
        in_specs=[pl.BlockSpec(memory_space=space) for _, space in INPUTS],
        out_specs=[vmem] * len(OUTPUTS),
        scratch_shapes=[pltpu.VMEM(shape, kind) for _, shape, kind in SCRATCH]
        + [dma((COPIES,)), dma((COPIES,)), dma((6,))],
        compiler_params=pltpu.CompilerParams(
            collective_id=0, has_side_effects=True, vmem_limit_bytes=VMEM_LIMIT
        ),
        name="train_step",
    )(*operands)


RESULTS = (
    ((1, 2, OWN, D), BF16),
    ((1, 2, OWN, D), BF16),
    ((1, 2, D), F32),
    ((1, 2, D), F32),
    ((1, 3, D, OWN), F32),
    ((3, 1, OWN), F32),
    ((1, OWN, D), F32),
    ((1, D, D), F32),
    ((1, D), F32),
    ((1, D, D), F32),
    ((1, D), F32),
)


def hand_over_kernel(
    rows_in, grads_in, gain_in, norm_bias_in, p_in, q_in, att_bias_in, up_bias_in, branch_in, *results
):
    rows, grads, gain, norm_bias, att, att_bias, wo, up, up_bias, dn, branch = results
    rows[...] = rows_in[...]
    grads[...] = grads_in[...]
    gain[...] = gain_in[...]
    norm_bias[...] = norm_bias_in[...]
    att_bias[...] = att_bias_in[...]
    up_bias[...] = up_bias_in[...]
    branch[...] = branch_in[...]
    up[0] = p_in[0:8].astype(F32).reshape(D, D)
    dn[0] = p_in[8:16].astype(F32).reshape(D, D)
    wo[0] = q_in[0:4].astype(F32).reshape(OWN, D)
    turned = q_in[4:16].astype(F32).reshape(384, D).T
    for k in range(3):
        att[0, k] = turned[:, k * LANES : (k + 1) * LANES]


def hand_over(arrays):
    vmem = pl.BlockSpec(memory_space=pltpu.VMEM)
    return pl.pallas_call(
        hand_over_kernel,
        out_shape=[jax.ShapeDtypeStruct(shape, kind) for shape, kind in RESULTS],
        in_specs=[vmem] * len(arrays),
        out_specs=[vmem] * len(RESULTS),
        compiler_params=pltpu.CompilerParams(vmem_limit_bytes=VMEM_LIMIT),
        name="hand_over",
    )(*arrays)


def local(
    block_input,
    output_grad,
    sequence_lengths,
    norm_gain,
    norm_bias,
    attention_weight,
    attention_bias,
    output_weight,
    up_weight,
    up_bias,
    down_weight,
    branch_bias,
):
    results = run_step(
        (
            block_input,
            output_grad,
            sequence_lengths,
            norm_gain,
            norm_bias,
            attention_weight,
            jnp.swapaxes(attention_bias, 0, 1),
            output_weight,
            up_weight,
            up_bias,
            down_weight,
            branch_bias,
        )
    )
    results = hand_over(results)
    return tuple(results[:5]) + (jnp.swapaxes(results[5], 0, 1),) + tuple(results[6:])


def solution(mesh):
    placed = (
        P(None, ("ctx", "tp"), None),
        P(None, ("ctx", "tp"), None),
        P(),
        P("section", None, None),
        P("section", None, None),
        P("section", None, None, "tp"),
        P("section", None, "tp"),
        P("section", "tp", None),
        P("section", None, "tp"),
        P("section", "tp"),
        P("section", "tp", None),
        P("section", None),
    )
    return jax.shard_map(
        local,
        mesh=mesh,
        in_specs=placed,
        out_specs=(
            P("section", None, ("ctx", "tp"), None),
            P("section", None, ("ctx", "tp"), None),
            P("section", None, None),
            P("section", None, None),
            P("section", None, None, "tp"),
            P("section", None, "tp"),
            P("section", "tp", None),
            P("section", None, "tp"),
            P("section", "tp"),
            P("section", "tp", None),
            P("section", None),
        ),
        check_vma=False,
    )
```
